32 devices in a mesh: seq: 16 (over z, y, core), blk: 2 (over x).
Axes of the slice: x: 2, y: 2, z: 4, core: 2. Of those that a mesh axis runs over, the one named last changes fastest.
Arguments:
- tokens: bfloat16 [32, 1024, 768], P('seq', 'blk'), may hold values from -6 to 6
- sent_lengths: int32 [32, 4], P('seq'), may hold values from 0 to 1024, as said below
- w_query: bfloat16 [768, 768], P('seq'), may hold values from -0.21875 to 0.21875
- w_key: bfloat16 [768, 768], P('seq'), may hold values from -0.21875 to 0.21875
- w_value: bfloat16 [768, 768], P('seq'), may hold values from -0.21875 to 0.21875
- w_out: bfloat16 [768, 768], P('seq'), may hold values from -1.75 to 1.75
- shared_a: bfloat16 [768, 1024], P('seq'), may hold values from -0.21875 to 0.21875
- shared_b: bfloat16 [1024, 768], P('seq'), may hold values from -0.1875 to 0.1875
- w_in: bfloat16 [768, 3072], P('seq'), may hold values from -0.21875 to 0.21875
- w_back: bfloat16 [3072, 768], P('seq'), may hold values from -0.109375 to 0.109375
- gain_one: float32 [768], replicated, may hold values from 0.5 to 1.5
- gain_two: float32 [768], replicated, may hold values from 0.5 to 1.5
- scale_dq: float32 [1024], replicated, may hold values from 0.5 to 2
- shift_bq: float32 [768], replicated, may hold values from -4 to 4
- scale_dv: float32 [1024], replicated, may hold values from 0.5 to 2
- shift_bv: float32 [768], replicated, may hold values from -4 to 4
- cotangent: bfloat16 [32, 1024, 768], P('seq', 'blk'), may hold values from -6 to 6
Outputs:
- layer_out: bfloat16 [32, 1024, 768], P('seq', 'blk')
- grad_tokens: bfloat16 [32, 1024, 768], P('seq', 'blk')
- grad_dq: float32 [1024], replicated
- grad_bq: float32 [768], replicated
- grad_dv: float32 [1024], replicated
- grad_bv: float32 [768], replicated
The draws below stay inside these ranges and needn't reach their ends.
Inputs may be any that keep to these rules, and one draw needn't show every extreme that they name: `sent_lengths`: rows come in groups of 2 (the rows of one index of seq). In each group one row holds a single document of 1024 tokens and empty other slots. Every other row holds two to four sentences in order and then padding: the first two have 8 to 512 tokens each, the third and fourth 0 to 1024 // 2 (the fourth empty when the third is), and all together at most 1024 tokens.
All inputs are finite; a program needn't handle non-finite values.
Results may differ from the reference program's by a relative error of at most 0.024.
Values may be sent and summed in bfloat16 or wider, within the bound.
No kernel may reach another device: no remote copies, remote signals or barrier semaphores. Data moves between devices by JAX's collectives and lax.ppermute only.
A program may use at most 192 MiB of HBM per device.

```python
import math
import jax
import jax.numpy as jnp
from jax import lax

D = 768
HEADS = 12
HEAD_DIM = 64
FF = 3072
R = 1024
ROW = 1024
ROWS = 2
ROWS_ALL = 32


def draw_sent_lengths(key, part):
    key = jax.random.fold_in(key, 11)
    key_one, key_two, key_three, key_four, key_pick = jax.random.split(key, 5)
    half = ROW // 2
    first = jax.random.randint(key_one, (ROWS_ALL, 1), 8, half + 1)
    second = jax.random.randint(key_two, (ROWS_ALL, 1), 8, half + 1)
    room = ROW - first - second
    third = jax.random.randint(key_three, (ROWS_ALL, 1), 0, jnp.minimum(half, room) + 1)
    room_four = jnp.where(third > 0, jnp.minimum(half, room - third), 0)
    fourth = jax.random.randint(key_four, (ROWS_ALL, 1), 0, room_four + 1)
    groups = ROWS_ALL // ROWS
    picks = jax.random.randint(key_pick, (groups,), 0, ROWS)
    row_ids = jnp.arange(ROWS_ALL, dtype=jnp.int32)
    marked = (row_ids % ROWS == picks[row_ids // ROWS])[:, None]
    lengths = jnp.concatenate([first, second, third, fourth], axis=1)
    whole = jnp.concatenate([jnp.full((ROWS_ALL, 1), ROW, jnp.int32), jnp.zeros((ROWS_ALL, 3), jnp.int32)], axis=1)
    return jnp.where(marked, whole, lengths).astype(jnp.int32)


def shard_levels(rng, extent, cuts, least, top_value):
    factor_of, own = 1.0, jax.random.fold_in(rng, 6)
    for axis_at, shards_of in cuts:
        steps = jnp.exp(jax.random.uniform(jax.random.fold_in(own, axis_at), (shards_of,), jnp.float32, least / len(cuts), top_value / len(cuts)))
        factor_of = factor_of * jnp.repeat(steps, extent[axis_at] // shards_of).reshape([-1 if axis == axis_at else 1 for axis in range(len(extent))])
    return factor_of


def gaussian(stream_key, shape, scale, most, shards=(), kind=jnp.bfloat16):
    array = jax.random.normal(stream_key, shape, jnp.float32) * scale
    if len(shards) > 0:
        array = shard_levels(stream_key, shape, shards, -0.22, 0.18) * array
    return jnp.clip(array, min=-most, max=most).astype(kind)


def setup_inputs(seed: int = 0) -> dict:
    streams_of = jax.random.split(jax.random.key(seed), 18)
    return {
        "tokens": gaussian(streams_of[0], (ROWS_ALL, ROW, D), 1.0, 6.0, ((0, 16), (1, 2))),
        "sent_lengths": draw_sent_lengths(jax.random.fold_in(streams_of[17], 71), 0),
        "w_query": gaussian(streams_of[2], (D, D), D ** -0.5, 0.21875, ((0, 16),)),
        "w_key": gaussian(streams_of[3], (D, D), D ** -0.5, 0.21875, ((0, 16),)),
        "w_value": gaussian(streams_of[4], (D, D), D ** -0.5, 0.21875, ((0, 16),)),
        "w_out": gaussian(streams_of[5], (D, D), (D // 64) ** -0.5, 1.75, ((0, 16),)),
        "shared_a": gaussian(streams_of[6], (D, R), D ** -0.5, 0.21875, ((0, 16),)),
        "shared_b": gaussian(streams_of[7], (R, D), R ** -0.5, 0.1875, ((0, 16),)),
        "w_in": gaussian(streams_of[8], (D, FF), D ** -0.5, 0.21875, ((0, 16),)),
        "w_back": gaussian(streams_of[9], (FF, D), FF ** -0.5, 0.109375, ((0, 16),)),
        "gain_one": jnp.clip(1.0 + 0.1 * jax.random.normal(streams_of[10], (D,), jnp.float32), 0.5, 1.5),
        "gain_two": jnp.clip(1.0 + 0.1 * jax.random.normal(streams_of[11], (D,), jnp.float32), 0.5, 1.5),
        "scale_dq": jnp.clip(jnp.exp(jax.random.uniform(streams_of[12], (R,), jnp.float32, math.log(0.5), math.log(2.0))), 0.5, 2.0),
        "shift_bq": gaussian(streams_of[13], (D,), 1.0, 4.0, (), jnp.float32),
        "scale_dv": jnp.clip(jnp.exp(jax.random.uniform(streams_of[14], (R,), jnp.float32, math.log(0.5), math.log(2.0))), 0.5, 2.0),
        "shift_bv": gaussian(streams_of[15], (D,), 1.0, 4.0, (), jnp.float32),
        "cotangent": gaussian(streams_of[16], (ROWS_ALL, ROW, D), 1.0, 6.0, ((0, 16), (1, 2))),
    }


@jax.custom_vjp
def low(v):
    return lax.optimization_barrier(v.astype(jnp.bfloat16)).astype(jnp.float32)

@jax.custom_vjp
def low_back(v):
    return v

def low_keep(v):
    return (low(v), None)

def low_pass(kept, grad):
    return (grad,)

def back_keep(v):
    return (v, None)

def back_low(kept, grad):
    return (low(grad),)
low.defvjp(low_keep, low_pass)
low_back.defvjp(back_keep, back_low)
highest = lax.Precision.HIGHEST

def matmul(left, right):
    return jnp.dot(left, right, precision=highest)

def layer_norm(hidden, gain):
    centre = hidden - lax.optimization_barrier(jnp.mean(hidden, axis=-1, keepdims=True))
    spread = lax.optimization_barrier(jnp.mean(centre * centre, axis=-1, keepdims=True))
    return centre * lax.rsqrt(spread + 1e-05) * gain

def segment_ids(lengths, total):
    place = jnp.arange(total, dtype=jnp.int32)[None, :]
    bounds = jnp.cumsum(lengths, axis=1).astype(jnp.int32)
    counted = jnp.zeros((lengths.shape[0], total), jnp.int32)
    for column in range(lengths.shape[1]):
        counted = counted + (place >= bounds[:, column:column + 1]).astype(jnp.int32)
    return counted

def attend_row(pieces):
    queries, key_rows, value_rows, seg_row = pieces
    scores = jnp.einsum('qhd,khd->hqk', queries, key_rows, precision=highest) * 0.125
    allowed = seg_row[:, None] == seg_row[None, :]
    scores = low_back(jnp.where(allowed[None], scores, -1e+30))
    probs = jax.nn.softmax(scores, axis=-1)
    mixed = jnp.einsum('hqk,khd->qhd', low(probs), value_rows, precision=highest)
    return mixed.reshape(ROW, D)

def forward(tokens_f, scale_dq, shift_bq, scale_dv, shift_bv, weights, seg_full):
    w_query, w_key, w_value, w_out, shared_a, shared_b, w_in, w_back, gain_one, gain_two = weights
    token_rows = tokens_f.reshape(ROWS_ALL * ROW, D)
    projected = low(low_back(matmul(token_rows, shared_a)))
    lift_q = low(projected * scale_dq)
    lift_v = low(projected * scale_dv)
    extra_q = low_back(matmul(lift_q, shared_b))
    extra_v = low_back(matmul(lift_v, shared_b))
    queries = low(low_back(matmul(token_rows, w_query) + shift_bq * extra_q))
    key_rows = low(low_back(matmul(token_rows, w_key)))
    value_rows = low(low_back(matmul(token_rows, w_value) + shift_bv * extra_v))
    shape4 = (ROWS_ALL, ROW, HEADS, HEAD_DIM)
    context = lax.map(jax.checkpoint(attend_row), (queries.reshape(shape4), key_rows.reshape(shape4), value_rows.reshape(shape4), seg_full))
    context = low(low_back(context.reshape(ROWS_ALL * ROW, D)))
    resid_one = token_rows + low_back(matmul(context, w_out))
    normed_one = layer_norm(resid_one, gain_one)
    pre_act = low_back(matmul(low(normed_one), w_in))
    act_rows = low(jax.nn.gelu(pre_act, approximate=False))
    resid_two = normed_one + low_back(matmul(act_rows, w_back))
    return layer_norm(resid_two, gain_two).reshape(ROWS_ALL, ROW, D)

def reference(tokens, sent_lengths, w_query, w_key, w_value, w_out, shared_a, shared_b, w_in, w_back, gain_one, gain_two, scale_dq, shift_bq, scale_dv, shift_bv, cotangent):
    matrices = (w_query, w_key, w_value, w_out, shared_a, shared_b, w_in, w_back)
    weights = tuple((matrix.astype(jnp.float32) for matrix in matrices)) + (gain_one, gain_two)
    seg_full = segment_ids(sent_lengths, ROW)

    def layer_fn(tokens_f, vec_dq, vec_bq, vec_dv, vec_bv):
        return forward(tokens_f, vec_dq, vec_bq, vec_dv, vec_bv, weights, seg_full)
    result, pullback = jax.vjp(layer_fn, tokens.astype(jnp.float32), scale_dq, shift_bq, scale_dv, shift_bv)
    grads = pullback(cotangent.astype(jnp.float32))
    return (result.astype(jnp.bfloat16), grads[0].astype(jnp.bfloat16), grads[1], grads[2], grads[3], grads[4])
```

```python
import functools
import math

import jax
import jax.numpy as jnp
from jax import lax
from jax.experimental import pallas as pl
from jax.experimental.pallas import tpu as pltpu
from jax.sharding import PartitionSpec as P

HEADS = 12
HEAD_DIM = 64
bf16 = jnp.bfloat16
f32 = jnp.float32


LN2 = 0.6931471805599453
LOG2E = 1.4426950408889634
SEGS = 5
PARTS = 3
TILE = 256
STEP = 128

def dot_nt(a,b): return lax.dot_general(a,b,(((1,),(1,)),((),())),preferred_element_type=f32)
def dot_nn(a,b): return jnp.dot(a,b,preferred_element_type=f32)

def lane_row(test, wide, kind=f32):
    lane = lax.broadcasted_iota(jnp.int32, (1, wide), 1)
    return jnp.where(test(lane), 1.0, 0.0).astype(kind)

def part_rows(wide, start):
    return [lane_row(lambda l: l == start + n, wide) for n in range(PARTS)]

def spread(column, rows):
    top = column.astype(bf16).astype(f32)
    return (top*rows[0] + (column-top)*rows[1]).astype(bf16)

def cross_ones(wide, hd):
    a = lax.broadcasted_iota(jnp.int32, (wide, wide), 0) < hd
    b = lax.broadcasted_iota(jnp.int32, (wide, wide), 1) < hd
    return jnp.where(a != b, 1.0, 0.0).astype(bf16)

def side_rows(wide, hd):
    return [lane_row(lambda l: l < hd, wide, bf16), lane_row(lambda l: l >= hd, wide, bf16)]

def marks(plan, span, wide, hd, side):
    place = lax.broadcasted_iota(jnp.int32, (span, wide), 0)
    lane = lax.broadcasted_iota(jnp.int32, (span, wide), 1) - (hd if side == 0 else 0)
    lane = jnp.where((lane >= 0) & (lane < hd), lane, hd)
    seg = jnp.zeros((span, wide), jnp.int32)
    for n in range(SEGS-1):
        seg = seg + jnp.where(place >= plan[1+n], 1, 0)
    hit = lane == seg
    asked = jnp.where((lane < SEGS) & (lane != seg), 1.0, 0.0).astype(bf16)
    held = jnp.where(hit, -1e30, jnp.where((lane >= SEGS) & (lane < SEGS+PARTS), 1.0, 0.0)).astype(bf16)
    return asked, held

def by_half(mine, work):
    for n in range(2):
        @pl.when(mine == n)
        def _():
            work(n)

def query_tiles(plan, span, work, broad=512):
    tiles = span//TILE
    fewest = plan[5+tiles]
    for n in range(1, tiles):
        fewest = jnp.minimum(fewest, plan[5+tiles+n])
    @pl.when(fewest == tiles)
    def _():
        def one(i, carry):
            work(pl.ds(pl.multiple_of(i*broad, broad), broad), slice(0, span))
            return carry
        lax.fori_loop(0, span//broad, one, 0)
    @pl.when(fewest < tiles)
    def _():
        def one(i, carry):
            rows = pl.ds(pl.multiple_of(i*TILE, TILE), TILE)
            start = pl.multiple_of(plan[5+i]*STEP, STEP)
            for n in range(1, tiles+1):
                @pl.when(plan[5+tiles+i] == n)
                def _():
                    work(rows, pl.ds(start, n*TILE) if n < tiles else slice(0, span))
            return carry
        lax.fori_loop(0, tiles, one, 0)

def attend_kernel(plan, xo_ref, xp_ref, own_ref, par_ref, qa_ref, qf, kf, ka, va, og, outs, *, hd):
    half = xo_ref.shape[0]
    span = 2*half
    wide = 2*hd
    sides = side_rows(wide, hd)
    swap = cross_ones(wide, hd)
    first = lax.broadcasted_iota(jnp.int32, (span, wide), 1) < hd
    start = [hd+SEGS, SEGS]
    parts = [part_rows(wide, start[s]) for s in range(2)]
    @pl.when(pl.program_id(0) == 0)
    def _():
        for s in range(2):
            qf[s], kf[s] = marks(plan, span, wide, hd, s)
    longest = None
    for x_ref in (xo_ref, xp_ref):
        kp = x_ref[:, wide:2*wide]
        norms = jnp.max(dot_nn(kp*kp, swap), axis=0, keepdims=True)
        longest = norms if longest is None else jnp.maximum(longest, norms)
    def place(n):
        for x_ref, at in ((xo_ref, n), (xp_ref, 1-n)):
            rows = slice(at*half, (at+1)*half)
            qp = x_ref[:, 0:wide]
            kp = x_ref[:, wide:2*wide]
            vp = x_ref[:, 2*wide:3*wide]
            top = jnp.sqrt(dot_nn(qp*qp, swap) * longest) * 1.02
            for s in range(2):
                qa_ref[s, rows, :] = qp*sides[s] + (qf[s, rows, :] - (top*parts[s][0]).astype(bf16))
                ka[s, rows, :] = kp*sides[s] + kf[s, rows, :]
                va[s, rows, :] = vp*sides[s] + sides[1-s]
    by_half(plan[0], place)
    def weigh(rows, keys):
        for s in range(2):
            w = jnp.exp2(dot_nt(qa_ref[s, rows, :], ka[s, keys, :])).astype(bf16)
            og[s, rows, :] = dot_nn(w, va[s, keys, :])
    query_tiles(plan, span, weigh)
    @pl.when(jnp.logical_not(jnp.min(jnp.where(first, og[1], og[0])) > 2.0**-80))
    def _():
        def exact_tile(i, carry):
            rows = pl.ds(pl.multiple_of(i*TILE, TILE), TILE)
            for s in range(2):
                plain = qa_ref[s, rows, :] * (1.0 - parts[s][0]).astype(bf16)
                m = jnp.max(dot_nt(plain, ka[s]), axis=1, keepdims=True)
                qa_ref[s, rows, :] = plain - (jnp.broadcast_to(m, (TILE, wide))*parts[s][0]).astype(bf16)
            weigh(rows, slice(0, span))
            return carry
        lax.fori_loop(0, span//TILE, exact_tile, 0)
    total = jnp.where(first, og[1], og[0])
    outs[...] = (jnp.where(first, og[0], og[1]) / pltpu.roll(total, hd, 1)).astype(bf16)
    lse = -jnp.log2(total)
    for s in range(2):
        qa_ref[s] = qa_ref[s] + spread(lse, parts[s][1:])
    def leave(n):
        own_ref[...] = outs[n*half:(n+1)*half, :]
        par_ref[...] = outs[(1-n)*half:(2-n)*half, :]
    by_half(plan[0], leave)

def attend(plan, qkv_own, qkv_par, heads, hd):
    half = qkv_own.shape[0]; span = 2*half; mine = heads*hd; wide = 2*hd
    col = lambda p, s: (0, p)
    return pl.pallas_call(
        functools.partial(attend_kernel, hd=hd),
        grid_spec=pltpu.PrefetchScalarGridSpec(
            num_scalar_prefetch=1, grid=(heads//2,),
            in_specs=[pl.BlockSpec((half, 3*wide), col)]*2,
            out_specs=[
                pl.BlockSpec((half, wide), col),
                pl.BlockSpec((half, wide), col),
                pl.BlockSpec((2, span, wide), lambda p, s: (p, 0, 0)),
            ],
            scratch_shapes=[
                pltpu.VMEM((2, span, wide), bf16),
                pltpu.VMEM((2, span, wide), bf16),
                pltpu.VMEM((2, span, wide), bf16),
                pltpu.VMEM((2, span, wide), bf16),
                pltpu.VMEM((2, span, wide), f32),
                pltpu.VMEM((span, wide), bf16),
            ]),
        out_shape=[
            jax.ShapeDtypeStruct((half, mine), bf16),
            jax.ShapeDtypeStruct((half, mine), bf16),
            jax.ShapeDtypeStruct((heads, span, wide), bf16),
        ],
        compiler_params=pltpu.CompilerParams(vmem_limit_bytes=32<<20),
        cost_estimate=pl.CostEstimate(flops=4*span*span*mine, bytes_accessed=span*mine*12, transcendentals=span*span*heads),
    )(plan, qkv_own, qkv_par)

def attend_back_kernel(plan, xo_ref, xp_ref, co_ref, cp_ref, go_ref, gp_ref, qa_ref, own_ref, par_ref, kf, ka, va, ga, kt, kacc, vacc, qacc, *, hd):
    half = xo_ref.shape[0]
    span = 2*half
    wide = 2*hd
    sides = side_rows(wide, hd)
    low = [lane_row(lambda l: (l >= hd) & (l < hd+PARTS), wide, bf16), lane_row(lambda l: l < PARTS, wide, bf16)]
    parts = [part_rows(wide, hd), part_rows(wide, 0)]
    swap = cross_ones(wide, hd)
    first = lax.broadcasted_iota(jnp.int32, (half, wide), 1) < hd
    @pl.when(pl.program_id(0) == 0)
    def _():
        for s in range(2):
            kf[s] = marks(plan, span, wide, hd, s)[1]
    def place(n):
        for x_ref, c_ref, g_ref, at in ((xo_ref, co_ref, go_ref, n), (xp_ref, cp_ref, gp_ref, 1-n)):
            rows = slice(at*half, (at+1)*half)
            kp = x_ref[:, wide:2*wide]
            vp = x_ref[:, 2*wide:3*wide]
            gp = g_ref[...]
            kt[:, rows] = kp.T
            prod = gp.astype(f32) * c_ref[...].astype(f32)
            top = prod.astype(bf16)
            delta = dot_nn(top, swap) + dot_nn((prod - top.astype(f32)).astype(bf16), swap)
            for s in range(2):
                ka[s, rows, :] = kp*sides[s] + kf[s, rows, :]
                va[s, rows, :] = vp*sides[s] + low[s]
                ga[s, rows, :] = gp*sides[s] + spread(-delta, parts[s])
    by_half(plan[0], place)
    kacc[...] = jnp.zeros_like(kacc)
    vacc[...] = jnp.zeros_like(vacc)
    def work(rows, keys):
        for s in range(2):
            qq = qa_ref[s, rows, :]
            gg = ga[s, rows, :]
            probs = jnp.exp2(dot_nt(ka[s, keys, :], qq))
            slope = (probs * dot_nt(va[s, keys, :], gg)).astype(bf16)
            vacc[s, keys, :] += dot_nn(probs.astype(bf16), gg)
            kacc[s, keys, :] += dot_nn(slope, qq)
            qacc[s*hd:(s+1)*hd, rows] = dot_nn(kt[s*hd:(s+1)*hd, keys], slope)
    query_tiles(plan, span, work, TILE)
    def leave(n):
        for o_ref, at in ((own_ref, n), (par_ref, 1-n)):
            rows = slice(at*half, (at+1)*half)
            o_ref[:, 0:wide] = (qacc[:, rows].T * LN2).astype(bf16)
            o_ref[:, wide:2*wide] = (jnp.where(first, kacc[0, rows, :], kacc[1, rows, :]) * LN2).astype(bf16)
            o_ref[:, 2*wide:3*wide] = jnp.where(first, vacc[0, rows, :], vacc[1, rows, :]).astype(bf16)
    by_half(plan[0], leave)

def attend_back(plan, qkv_own, qkv_par, ctx_own, ctx_par, g_own, g_par, qa, heads, hd):
    half = qkv_own.shape[0]; span = 2*half; mine = heads*hd; wide = 2*hd
    col = lambda p, s: (0, p)
    return pl.pallas_call(
        functools.partial(attend_back_kernel, hd=hd),
        grid_spec=pltpu.PrefetchScalarGridSpec(
            num_scalar_prefetch=1, grid=(heads//2,),
            in_specs=[pl.BlockSpec((half, 3*wide), col)]*2 + [pl.BlockSpec((half, wide), col)]*4 + [pl.BlockSpec((2, span, wide), lambda p, s: (p, 0, 0))],
            out_specs=[pl.BlockSpec((half, 3*wide), col)]*2,
            scratch_shapes=[
                pltpu.VMEM((2, span, wide), bf16),
                pltpu.VMEM((2, span, wide), bf16),
                pltpu.VMEM((2, span, wide), bf16),
                pltpu.VMEM((2, span, wide), bf16),
                pltpu.VMEM((wide, span), bf16),
                pltpu.VMEM((2, span, wide), f32),
                pltpu.VMEM((2, span, wide), f32),
                pltpu.VMEM((wide, span), f32),
            ]),
        out_shape=[jax.ShapeDtypeStruct((half, 3*mine), bf16)]*2,
        compiler_params=pltpu.CompilerParams(vmem_limit_bytes=40<<20),
        cost_estimate=pl.CostEstimate(flops=10*span*span*mine, bytes_accessed=span*mine*20, transcendentals=span*span*heads),
    )(plan, qkv_own, qkv_par, ctx_own, ctx_par, g_own, g_par, qa)

def plan_row(lengths, my_block, span):
    bounds = jnp.cumsum(lengths)
    place = jnp.arange(span, dtype=jnp.int32)
    edges = jnp.concatenate([jnp.zeros((1,), jnp.int32), bounds, jnp.full((1,), span, jnp.int32)]).astype(jnp.int32)
    seg = jnp.sum((place[:, None] >= bounds[None, :]).astype(jnp.int32), axis=1)
    lo = edges[seg[0::TILE]]
    hi = edges[seg[TILE-1::TILE]+1]
    begin = lo // STEP
    count = (hi - begin*STEP + TILE-1)//TILE
    begin = jnp.minimum(begin, (span - count*TILE)//STEP)
    return jnp.concatenate([jnp.reshape(my_block, (1,)).astype(jnp.int32), bounds.astype(jnp.int32), begin.astype(jnp.int32), count.astype(jnp.int32)])


def centred(hidden):
    off = hidden - jnp.mean(hidden, axis=-1, keepdims=True)
    scale = lax.rsqrt(jnp.mean(off*off, axis=-1, keepdims=True) + 1e-05)
    return off*scale, scale

def norm_back(grad, unit, scale):
    inner = jnp.mean(grad*unit, axis=-1, keepdims=True)
    return scale*(grad - jnp.mean(grad, axis=-1, keepdims=True) - unit*inner)

def gelu_pair(x):
    size = jnp.abs(x)
    base = 1.0 + size*(0.3275911*0.7071067811865476)
    t = pl.reciprocal(base, approx=True)
    t = t*(2.0 - base*t)
    bell = jnp.exp2(x*x*(-0.7213475204444817))
    tail = t*(0.127414796 + t*(-0.142248368 + t*(0.7107068705 + t*(-0.7265760135 + t*0.5307027145))))*bell
    below = jnp.where(x < 0, tail, 1.0 - tail)
    return x*below, below + x*(bell*0.3989422804014327)

def ffn_kernel(place, co_ref, cr_ref, x_ref, cot_ref, g1_ref, g2_ref, pack_ref, out_ref, grad_ref, own_ref, send_ref, wo, wi, wb, slopes, gsum, sems, *, shards, cuts):
    width = x_ref.shape[1]
    lead = wo.shape[1]
    back = wb.shape[1]
    copies = [pltpu.make_async_copy(pack_ref.at[:, 0:lead, :], wo, sems.at[0])]
    for j in range(cuts):
        copies.append(pltpu.make_async_copy(pack_ref.at[:, lead*(1+j):lead*(2+j), :], wi.at[j], sems.at[1+j]))
    per = shards//cuts
    for j in range(cuts):
        copies.append(pltpu.make_async_copy(pack_ref.at[j*per:(j+1)*per, lead*(1+cuts):lead*(1+cuts)+back, :], wb.at[j*per:(j+1)*per], sems.at[1+cuts+j]))
    for c in copies:
        c.start()
    part = shards//2
    half = width//2
    mine = place[0]
    def out_rows(who):
        return wo[pl.ds(pl.multiple_of(who*part, part), part)].reshape(half, width)
    def w_in(j): return wi[j].reshape(width, width)
    def w_back(j): return wb[j*per:(j+1)*per].reshape(per*back, width)
    copies[0].wait()
    resid = x_ref[...].astype(f32) + dot_nn(co_ref[...], out_rows(mine)) + dot_nn(cr_ref[...], out_rows(1-mine))
    unit_one, scale_one = centred(resid)
    normed = unit_one*g1_ref[...]
    low = normed.astype(bf16)
    total = normed
    for j in range(cuts):
        copies[1+j].wait()
        pre = dot_nn(low, w_in(j))
        act, slope = gelu_pair(pre)
        slopes[j] = slope.astype(bf16)
        copies[1+cuts+j].wait()
        total = total + dot_nn(act.astype(bf16), w_back(j))
    unit_two, scale_two = centred(total)
    out_ref[...] = (unit_two*g2_ref[...]).astype(bf16)
    grad_two = norm_back(cot_ref[...].astype(f32)*g2_ref[...], unit_two, scale_two)
    low_two = grad_two.astype(bf16)
    grad = grad_two
    for j in range(cuts):
        pre_grad = (dot_nt(low_two, w_back(j))*slopes[j].astype(f32)).astype(bf16)
        grad = grad + dot_nt(pre_grad, w_in(j))
    grad_one = norm_back(grad*g1_ref[...], unit_one, scale_one)
    grad_ref[...] = grad_one
    low_one = grad_one.astype(bf16)
    own_ref[...] = dot_nt(low_one, out_rows(mine)).astype(bf16)
    send_ref[...] = dot_nt(low_one, out_rows(1-mine)).astype(bf16)

def ffn(place, ctx_own, ctx_recv, x, cot, gain_one, gain_two, pack, cuts):
    span, width = x.shape
    shards, total, _ = pack.shape
    lead = width//shards
    back = cuts*width//shards
    whole = lambda shape: pl.BlockSpec(shape, lambda i, s: (0,)*len(shape))
    return pl.pallas_call(
        functools.partial(ffn_kernel, shards=shards, cuts=cuts),
        grid_spec=pltpu.PrefetchScalarGridSpec(
            num_scalar_prefetch=1, grid=(1,),
            in_specs=[whole((span, width//2)), whole((span, width//2)), whole((span, width)), whole((span, width)), whole((1, width)), whole((1, width)), pl.BlockSpec(memory_space=pl.ANY)],
            out_specs=[whole((span, width)), whole((span, width)), whole((span, width//2)), whole((span, width//2))],
            scratch_shapes=[
                pltpu.VMEM((shards, lead, width), bf16),
                pltpu.VMEM((cuts, shards, lead, width), bf16),
                pltpu.VMEM((shards, back, width), bf16),
                pltpu.VMEM((cuts, span, width), bf16),
                pltpu.VMEM((8, 128), f32),
                pltpu.SemaphoreType.DMA((1+2*cuts,)),
            ]),
        out_shape=[
            jax.ShapeDtypeStruct((span, width), bf16),
            jax.ShapeDtypeStruct((span, width), f32),
            jax.ShapeDtypeStruct((span, width//2), bf16),
            jax.ShapeDtypeStruct((span, width//2), bf16),
        ],
        compiler_params=pltpu.CompilerParams(vmem_limit_bytes=56<<20),
        cost_estimate=pl.CostEstimate(flops=2*span*width*width*(2+4*cuts), bytes_accessed=2*(2+2*cuts)*width*width, transcendentals=2*span*width*cuts),
    )(place, ctx_own, ctx_recv, x, cot, gain_one, gain_two, pack)


def shifted(shard, axis, by):
    count = lax.axis_size(axis)
    return lax.ppermute(shard, axis, [(i, (i + by) % count) for i in range(count)])


def layer_norm(hidden, gain):
    centre = hidden - jnp.mean(hidden, axis=-1, keepdims=True)
    spread = jnp.mean(centre * centre, axis=-1, keepdims=True)
    return centre * lax.rsqrt(spread + 1e-05) * gain


def exact_gelu(values):
    return jax.nn.gelu(values, approximate=False)


def segment_ids(lengths, total):
    place = jnp.arange(total, dtype=jnp.int32)[None, :]
    bounds = jnp.cumsum(lengths, axis=1)
    counted = jnp.zeros((lengths.shape[0], total), jnp.int32)
    for column in range(lengths.shape[1]):
        counted = counted + (place >= bounds[:, column : column + 1]).astype(jnp.int32)
    return counted


def dot_plain(left, right):
    return jnp.dot(left, right, preferred_element_type=jnp.float32)


def dot_trans(left, right):
    return lax.dot_general(
        left, right, (((1,), (1,)), ((), ())), preferred_element_type=jnp.float32
    )


def block_grads(query_h, out_grad, lse_rows, delta_rows, key_h, value_h, allowed):
    scores = (
        jnp.einsum("rqhd,rkhd->rqhk", query_h, key_h, preferred_element_type=jnp.float32) * 0.125
    )
    probs = jnp.where(allowed, jnp.exp(scores - lse_rows[..., None]), 0.0)
    value_grad = jnp.einsum(
        "rqhk,rqhd->rkhd", probs.astype(jnp.bfloat16), out_grad, preferred_element_type=jnp.float32
    )
    prob_grad = jnp.einsum("rqhd,rkhd->rqhk", out_grad, value_h, preferred_element_type=jnp.float32)
    score_grad = (probs * (prob_grad - delta_rows[..., None])).astype(jnp.bfloat16)
    query_grad = (
        jnp.einsum("rqhk,rkhd->rqhd", score_grad, key_h, preferred_element_type=jnp.float32) * 0.125
    )
    key_grad = (
        jnp.einsum("rqhk,rqhd->rkhd", score_grad, query_h, preferred_element_type=jnp.float32)
        * 0.125
    )
    return (query_grad, key_grad, value_grad)


def body_any(
    tokens,
    sent_lengths,
    w_query,
    w_key,
    w_value,
    w_out,
    shared_a,
    shared_b,
    w_in,
    w_back,
    gain_one,
    gain_two,
    scale_dq,
    shift_bq,
    scale_dv,
    shift_bv,
    cotangent,
):
    row_count, span, width = tokens.shape
    head_count = HEADS
    head_size = HEAD_DIM
    blocks = lax.axis_size("blk")
    my_block = lax.axis_index("blk")
    token_count = row_count * span
    token_rows = tokens.reshape(token_count, width)
    seg_full = segment_ids(sent_lengths, span * blocks)
    seg_mine = lax.dynamic_slice_in_dim(seg_full, my_block * span, span, 1)
    w_queries, w_keys, w_values, proj_a, proj_b = (
        lax.all_gather(w_query, "seq", axis=0, tiled=True),
        lax.all_gather(w_key, "seq", axis=0, tiled=True),
        lax.all_gather(w_value, "seq", axis=0, tiled=True),
        lax.all_gather(shared_a, "seq", axis=0, tiled=True),
        lax.all_gather(shared_b, "seq", axis=0, tiled=True),
    )
    projected = dot_plain(token_rows, proj_a).astype(jnp.bfloat16)
    proj_float = projected.astype(jnp.float32)
    lift_q = (proj_float * scale_dq).astype(jnp.bfloat16)
    lift_v = (proj_float * scale_dv).astype(jnp.bfloat16)
    extra_q = dot_plain(lift_q, proj_b)
    extra_v = dot_plain(lift_v, proj_b)
    queries = (dot_plain(token_rows, w_queries) + shift_bq * extra_q).astype(jnp.bfloat16)
    key_rows = dot_plain(token_rows, w_keys).astype(jnp.bfloat16)
    value_rows = (dot_plain(token_rows, w_values) + shift_bv * extra_v).astype(jnp.bfloat16)
    shape4 = (row_count, span, head_count, head_size)
    query_h = queries.reshape(shape4)
    key_h = key_rows.reshape(shape4)
    value_h = value_rows.reshape(shape4)
    start_best = jnp.full((row_count, span, head_count), -1e30, jnp.float32)
    best = start_best
    key_piece = lax.all_gather(key_rows.reshape(row_count, span, width), "blk", axis=1, tiled=True)
    value_piece = lax.all_gather(
        value_rows.reshape(row_count, span, width), "blk", axis=1, tiled=True
    )
    length = key_piece.shape[1]
    key_part = key_piece.reshape(row_count, length, head_count, head_size)
    value_part = value_piece.reshape(row_count, length, head_count, head_size)
    seg_keys = seg_full
    allowed = (seg_mine[:, :, None] == seg_keys[:, None, :])[:, :, None, :]
    scores = (
        jnp.einsum("rqhd,rkhd->rqhk", query_h, key_part, preferred_element_type=jnp.float32) * 0.125
    )
    scores = jnp.where(allowed, scores, -1e30)
    new_best = jnp.maximum(best, jnp.max(scores, axis=-1))
    weight = jnp.where(allowed, jnp.exp(scores - new_best[..., None]), 0.0)
    total = jnp.sum(weight, axis=-1)
    accum = jnp.einsum(
        "rqhk,rkhd->rqhd",
        weight.astype(jnp.bfloat16),
        value_part,
        preferred_element_type=jnp.float32,
    )
    best, total, accum = (new_best, total, accum)
    log_total = best + jnp.log(total)
    context = accum / total[..., None]
    context_b = context.reshape(token_count, width).astype(jnp.bfloat16)
    w_outs, w_ins, w_backs = (
        lax.all_gather(w_out, "seq", axis=0, tiled=True),
        lax.all_gather(w_in, "seq", axis=0, tiled=True),
        lax.all_gather(w_back, "seq", axis=0, tiled=True),
    )

    def norm_first(hidden):
        return layer_norm(hidden, gain_one)

    def norm_second(hidden):
        return layer_norm(hidden, gain_two)

    resid_one = token_rows.astype(jnp.float32) + dot_plain(context_b, w_outs)
    normed_one, norm_one_pull = jax.vjp(norm_first, resid_one)
    pre_act = dot_plain(normed_one.astype(jnp.bfloat16), w_ins)
    act_float, gelu_pull = jax.vjp(exact_gelu, pre_act)
    ffn_part = dot_plain(act_float.astype(jnp.bfloat16), w_backs)
    normed_two, norm_two_pull = jax.vjp(norm_second, normed_one + ffn_part)
    layer_out = normed_two.astype(jnp.bfloat16).reshape(row_count, span, width)
    w_outs, w_ins, w_backs = (
        lax.all_gather(w_out, "seq", axis=0, tiled=True),
        lax.all_gather(w_in, "seq", axis=0, tiled=True),
        lax.all_gather(w_back, "seq", axis=0, tiled=True),
    )
    (grad_two,) = norm_two_pull(cotangent.reshape(token_count, width).astype(jnp.float32))
    act_grad = dot_trans(grad_two.astype(jnp.bfloat16), w_backs)
    (pre_grad,) = gelu_pull(act_grad)
    normed_grad = grad_two + dot_trans(pre_grad.astype(jnp.bfloat16), w_ins)
    (grad_one,) = norm_one_pull(normed_grad)
    context_grad = dot_trans(grad_one.astype(jnp.bfloat16), w_outs).astype(jnp.bfloat16)
    out_grad = context_grad.reshape(shape4)
    delta_rows = jnp.sum(out_grad.astype(jnp.float32) * context, axis=-1)
    zero_grads = jnp.zeros(shape4, jnp.float32)

    def key_step(step, carry):
        key_cur, value_cur, query_acc, key_acc, value_acc = carry
        source = (my_block - step) % blocks
        seg_keys = lax.dynamic_slice_in_dim(seg_full, source * span, span, 1)
        allowed = (seg_mine[:, :, None] == seg_keys[:, None, :])[:, :, None, :]
        q_part, k_part, v_part = block_grads(
            query_h, out_grad, log_total, delta_rows, key_cur, value_cur, allowed
        )
        key_acc, value_acc = (
            shifted((key_acc + k_part).astype(jnp.bfloat16), "blk", 1).astype(jnp.float32),
            shifted((value_acc + v_part).astype(jnp.bfloat16), "blk", 1).astype(jnp.float32),
        )
        key_cur, value_cur = shifted((key_cur, value_cur), "blk", 1)
        return (key_cur, value_cur, query_acc + q_part, key_acc, value_acc)

    looped = lax.fori_loop(
        0, blocks, key_step, (key_h, value_h, zero_grads, zero_grads, zero_grads)
    )
    query_acc, key_acc, value_acc = (looped[2], looped[3], looped[4])
    query_grad = query_acc.reshape(token_count, width).astype(jnp.bfloat16)
    key_grad = key_acc.reshape(token_count, width).astype(jnp.bfloat16)
    value_grad = value_acc.reshape(token_count, width).astype(jnp.bfloat16)
    w_queries, w_keys, w_values, proj_a, proj_b = (
        lax.all_gather(w_query, "seq", axis=0, tiled=True),
        lax.all_gather(w_key, "seq", axis=0, tiled=True),
        lax.all_gather(w_value, "seq", axis=0, tiled=True),
        lax.all_gather(shared_a, "seq", axis=0, tiled=True),
        lax.all_gather(shared_b, "seq", axis=0, tiled=True),
    )
    query_float = query_grad.astype(jnp.float32)
    value_float = value_grad.astype(jnp.float32)
    part_bq = jnp.sum(query_float * extra_q, axis=0)
    part_bv = jnp.sum(value_float * extra_v, axis=0)
    lift_q_grad = dot_trans((query_float * shift_bq).astype(jnp.bfloat16), proj_b)
    lift_v_grad = dot_trans((value_float * shift_bv).astype(jnp.bfloat16), proj_b)
    part_dq = jnp.sum(lift_q_grad * proj_float, axis=0)
    part_dv = jnp.sum(lift_v_grad * proj_float, axis=0)
    proj_grad = (lift_q_grad * scale_dq + lift_v_grad * scale_dv).astype(jnp.bfloat16)
    token_grad = (
        grad_one
        + dot_trans(query_grad, w_queries)
        + dot_trans(key_grad, w_keys)
        + dot_trans(value_grad, w_values)
        + dot_trans(proj_grad, proj_a)
    )
    grad_dq, grad_bq, grad_dv, grad_bv = lax.psum(
        (part_dq, part_bq, part_dv, part_bv), ("seq", "blk")
    )
    return (
        layer_out,
        token_grad.astype(jnp.bfloat16).reshape(row_count, span, width),
        grad_dq,
        grad_bq,
        grad_dv,
        grad_bv,
    )


def swapped(block):
    return lax.ppermute(block, "blk", [(0, 1), (1, 0)])


def summed(vector, groups):
    vector = vector + swapped(vector)
    hop = 1
    while hop < groups:
        vector = vector + lax.ppermute(vector, "seq", [(i, i ^ hop) for i in range(groups)])
        hop *= 2
    return vector


def body_two(
    tokens,
    sent_lengths,
    w_query,
    w_key,
    w_value,
    w_out,
    shared_a,
    shared_b,
    w_in,
    w_back,
    gain_one,
    gain_two,
    scale_dq,
    shift_bq,
    scale_dv,
    shift_bv,
    cotangent,
):
    row_count, span, width = tokens.shape
    shards = lax.axis_size("seq")
    mine = lax.axis_index("blk")
    heads = HEADS // 2
    part = heads * HEAD_DIM
    wide = 2 * HEAD_DIM
    pairs = heads // 2
    rank = shared_a.shape[1]
    cuts = w_in.shape[1] // width
    coef = 0.125 * LOG2E

    def columns(matrix):
        return lax.dynamic_slice_in_dim(matrix, mine * part, part, matrix.ndim - 1)

    def paired(triple):
        return [piece[..., n * wide : (n + 1) * wide] for n in range(pairs) for piece in triple]

    up = columns(shared_b)
    lead = shared_a.shape[0]
    first_pack = jnp.concatenate(
        [shared_a]
        + paired([columns(w_query), columns(w_key), columns(w_value)])
        + [up.reshape(lead, up.size // lead)],
        axis=1,
    )
    other = [swapped(tokens[row]) for row in range(row_count)]
    gathered = lax.all_gather(first_pack, "seq", axis=0)
    second_pack = jnp.concatenate(
        [w_out] + [w_in[:, n * width : (n + 1) * width] for n in range(cuts)] + [w_back], axis=0
    )
    pack = lax.all_gather(second_pack, "seq", axis=0)
    down = gathered[:, :, :rank].reshape(width, rank)
    mixed = gathered[:, :, rank : rank + 3 * part].reshape(width, 3 * part)
    lift = gathered[:, :, rank + 3 * part :].reshape(rank, part)
    lift_f = lift.astype(f32)
    inner = jnp.concatenate([lift_f * scale_dq[:, None], lift_f * scale_dv[:, None]], axis=1)
    merged = dot_nn(down, inner.astype(bf16))
    bend_q = columns(shift_bq)
    bend_v = columns(shift_bv)
    mixed_f = mixed.astype(f32)
    blocks = []
    for n in range(pairs):
        at = slice(n * wide, (n + 1) * wide)
        base = 3 * n * wide
        delta_q = merged[:, at] * bend_q[at]
        delta_v = merged[:, part + n * wide : part + (n + 1) * wide] * bend_v[at]
        blocks.append((mixed_f[:, base : base + wide] + delta_q) * coef)
        blocks.append(mixed_f[:, base + wide : base + 2 * wide])
        blocks.append(mixed_f[:, base + 2 * wide : base + 3 * wide] + delta_v)
    weights = jnp.concatenate(blocks, axis=1).astype(bf16)
    place = jnp.reshape(mine, (1,)).astype(jnp.int32)
    g_one = gain_one.reshape(1, width)
    g_two = gain_two.reshape(1, width)

    rows = range(row_count)
    plans = [plan_row(sent_lengths[row], mine, 2 * span) for row in rows]
    qkv_own = [dot_nn(tokens[row], weights).astype(bf16) for row in rows]
    qkv_par = [dot_nn(other[row], weights).astype(bf16) for row in rows]
    seen = [attend(plans[row], qkv_own[row], qkv_par[row], heads, HEAD_DIM) for row in rows]
    ctx_recv = [swapped(seen[row][1]) for row in rows]
    fed = [
        ffn(place, seen[row][0], ctx_recv[row], tokens[row], cotangent[row], g_one, g_two, pack, cuts)
        for row in rows
    ]
    grad_recv = [swapped(fed[row][3]) for row in rows]
    turned = [
        attend_back(
            plans[row], qkv_own[row], qkv_par[row], seen[row][0], seen[row][1],
            fed[row][2], grad_recv[row], seen[row][2], heads, HEAD_DIM,
        )
        for row in rows
    ]
    sent = [swapped(dot_nt(turned[row][1], weights).astype(bf16)) for row in rows]
    token_grad = [
        (fed[row][1] + dot_nt(turned[row][0], weights) + sent[row].astype(f32)).astype(bf16)
        for row in rows
    ]

    def outer(left, right):
        return lax.dot_general(left, right, (((0,), (0,)), ((), ())), preferred_element_type=f32)

    moment = sum(outer(tokens[row], turned[row][0]) + outer(other[row], turned[row][1]) for row in rows)
    moment_q = jnp.concatenate([moment[:, 3 * n * wide : (3 * n + 1) * wide] for n in range(pairs)], axis=1)
    moment_v = jnp.concatenate(
        [moment[:, (3 * n + 2) * wide : (3 * n + 3) * wide] for n in range(pairs)], axis=1
    )
    moment_q = moment_q * coef
    down_f = down.astype(f32)

    def whole(piece):
        return lax.dynamic_update_slice(jnp.zeros((width,), f32), piece, (mine * part,))

    part_bq = whole(jnp.sum(merged[:, :part] * moment_q, axis=0))
    part_bv = whole(jnp.sum(merged[:, part:] * moment_v, axis=0))
    part_dq = jnp.sum(down_f * dot_nt((moment_q * bend_q).astype(bf16), lift), axis=0)
    part_dv = jnp.sum(down_f * dot_nt((moment_v * bend_v).astype(bf16), lift), axis=0)
    flat = jnp.concatenate([part_dq, part_bq, part_dv, part_bv]).reshape(-1, 128)
    flat = summed(flat, shards).reshape(-1)
    return (
        jnp.stack([fed[row][0] for row in rows]),
        jnp.stack(token_grad),
        flat[:rank],
        flat[rank : rank + width],
        flat[rank + width : 2 * rank + width],
        flat[2 * rank + width :],
    )


def solution(mesh):
    return jax.shard_map(
        body_two if mesh.shape["blk"] == 2 else body_any,
        mesh=mesh,
        in_specs=(
            P("seq", "blk", None),
            P("seq", None),
            P("seq", None),
            P("seq", None),
            P("seq", None),
            P("seq", None),
            P("seq", None),
            P("seq", None),
            P("seq", None),
            P("seq", None),
            P(),
            P(),
            P(),
            P(),
            P(),
            P(),
            P("seq", "blk", None),
        ),
        out_specs=(P("seq", "blk", None), P("seq", "blk", None), P(), P(), P(), P()),
        check_vma=False,
    )
```

```python
import functools

import jax
import jax.numpy as jnp
from jax import lax
from jax.experimental import pallas as pl
from jax.experimental.pallas import tpu as pltpu
from jax.sharding import PartitionSpec as P

HEADS = 12
HEAD_DIM = 64
bf16 = jnp.bfloat16
f32 = jnp.float32


LN2 = 0.6931471805599453
LOG2E = 1.4426950408889634
SEGS = 5
PARTS = 3
TILE = 256
STEP = 128

def dot_nt(a,b): return lax.dot_general(a,b,(((1,),(1,)),((),())),preferred_element_type=f32)
def dot_nn(a,b): return jnp.dot(a,b,preferred_element_type=f32)

def lane_row(test, wide, kind=f32):
    lane = lax.broadcasted_iota(jnp.int32, (1, wide), 1)
    return jnp.where(test(lane), 1.0, 0.0).astype(kind)

def part_rows(wide, start):
    return [lane_row(lambda l: l == start + n, wide) for n in range(PARTS)]

def spread(column, rows):
    top = column.astype(bf16).astype(f32)
    return (top*rows[0] + (column-top)*rows[1]).astype(bf16)

def cross_ones(wide, hd):
    a = lax.broadcasted_iota(jnp.int32, (wide, wide), 0) < hd
    b = lax.broadcasted_iota(jnp.int32, (wide, wide), 1) < hd
    return jnp.where(a != b, 1.0, 0.0).astype(bf16)

def side_rows(wide, hd):
    return [lane_row(lambda l: l < hd, wide, bf16), lane_row(lambda l: l >= hd, wide, bf16)]

def marks(plan, span, wide, hd, side):
    place = lax.broadcasted_iota(jnp.int32, (span, wide), 0)
    lane = lax.broadcasted_iota(jnp.int32, (span, wide), 1) - (hd if side == 0 else 0)
    lane = jnp.where((lane >= 0) & (lane < hd), lane, hd)
    seg = jnp.zeros((span, wide), jnp.int32)
    for n in range(SEGS-1):
        seg = seg + jnp.where(place >= plan[1+n], 1, 0)
    hit = lane == seg
    asked = jnp.where((lane < SEGS) & (lane != seg), 1.0, 0.0).astype(bf16)
    held = jnp.where(hit, -1e30, jnp.where((lane >= SEGS) & (lane < SEGS+PARTS), 1.0, 0.0)).astype(bf16)
    return asked, held

def by_half(mine, work):
    for n in range(2):
        @pl.when(mine == n)
        def _():
            work(n)

def query_tiles(plan, span, work, broad=512):
    tiles = span//TILE
    fewest = plan[5+tiles]
    for n in range(1, tiles):
        fewest = jnp.minimum(fewest, plan[5+tiles+n])
    @pl.when(fewest == tiles)
    def _():
        def one(i, carry):
            work(pl.ds(pl.multiple_of(i*broad, broad), broad), slice(0, span))
            return carry
        lax.fori_loop(0, span//broad, one, 0)
    @pl.when(fewest < tiles)
    def _():
        def one(i, carry):
            rows = pl.ds(pl.multiple_of(i*TILE, TILE), TILE)
            start = pl.multiple_of(plan[5+i]*STEP, STEP)
            for n in range(1, tiles+1):
                @pl.when(plan[5+tiles+i] == n)
                def _():
                    work(rows, pl.ds(start, n*TILE) if n < tiles else slice(0, span))
            return carry
        lax.fori_loop(0, tiles, one, 0)

def attend_kernel(plan, xo_ref, xp_ref, own_ref, par_ref, qa_ref, qf, kf, ka, va, og, outs, *, hd):
    half = xo_ref.shape[0]
    span = 2*half
    wide = 2*hd
    sides = side_rows(wide, hd)
    swap = cross_ones(wide, hd)
    first = lax.broadcasted_iota(jnp.int32, (span, wide), 1) < hd
    start = [hd+SEGS, SEGS]
    parts = [part_rows(wide, start[s]) for s in range(2)]
    @pl.when(pl.program_id(0) == 0)
    def _():
        for s in range(2):
            qf[s], kf[s] = marks(plan, span, wide, hd, s)
    longest = None
    for x_ref in (xo_ref, xp_ref):
        kp = x_ref[:, wide:2*wide]
        norms = jnp.max(dot_nn(kp*kp, swap), axis=0, keepdims=True)
        longest = norms if longest is None else jnp.maximum(longest, norms)
    def place(n):
        for x_ref, at in ((xo_ref, n), (xp_ref, 1-n)):
            rows = slice(at*half, (at+1)*half)
            qp = x_ref[:, 0:wide]
            kp = x_ref[:, wide:2*wide]
            vp = x_ref[:, 2*wide:3*wide]
            top = jnp.sqrt(dot_nn(qp*qp, swap) * longest) * 1.02
            for s in range(2):
                qa_ref[s, rows, :] = qp*sides[s] + (qf[s, rows, :] - (top*parts[s][0]).astype(bf16))
                ka[s, rows, :] = kp*sides[s] + kf[s, rows, :]
                va[s, rows, :] = vp*sides[s] + sides[1-s]
    by_half(plan[0], place)
    def weigh(rows, keys):
        for s in range(2):
            w = jnp.exp2(dot_nt(qa_ref[s, rows, :], ka[s, keys, :])).astype(bf16)
            og[s, rows, :] = dot_nn(w, va[s, keys, :])
    query_tiles(plan, span, weigh)
    @pl.when(jnp.logical_not(jnp.min(jnp.where(first, og[1], og[0])) > 2.0**-80))
    def _():
        def exact_tile(i, carry):
            rows = pl.ds(pl.multiple_of(i*TILE, TILE), TILE)
            for s in range(2):
                plain = qa_ref[s, rows, :] * (1.0 - parts[s][0]).astype(bf16)
                m = jnp.max(dot_nt(plain, ka[s]), axis=1, keepdims=True)
                qa_ref[s, rows, :] = plain - (jnp.broadcast_to(m, (TILE, wide))*parts[s][0]).astype(bf16)
            weigh(rows, slice(0, span))
            return carry
        lax.fori_loop(0, span//TILE, exact_tile, 0)
    total = jnp.where(first, og[1], og[0])
    outs[...] = (jnp.where(first, og[0], og[1]) / pltpu.roll(total, hd, 1)).astype(bf16)
    lse = -jnp.log2(total)
    for s in range(2):
        qa_ref[s] = qa_ref[s] + spread(lse, parts[s][1:])
    def leave(n):
        own_ref[...] = outs[n*half:(n+1)*half, :]
        par_ref[...] = outs[(1-n)*half:(2-n)*half, :]
    by_half(plan[0], leave)

def attend(plan, qkv_own, qkv_par, heads, hd):
    half = qkv_own.shape[0]; span = 2*half; mine = heads*hd; wide = 2*hd
    col = lambda p, s: (0, p)
    return pl.pallas_call(
        functools.partial(attend_kernel, hd=hd),
        grid_spec=pltpu.PrefetchScalarGridSpec(
            num_scalar_prefetch=1, grid=(heads//2,),
            in_specs=[pl.BlockSpec((half, 3*wide), col)]*2,
            out_specs=[
                pl.BlockSpec((half, wide), col),
                pl.BlockSpec((half, wide), col),
                pl.BlockSpec((2, span, wide), lambda p, s: (p, 0, 0)),
            ],
            scratch_shapes=[
                pltpu.VMEM((2, span, wide), bf16),
                pltpu.VMEM((2, span, wide), bf16),
                pltpu.VMEM((2, span, wide), bf16),
                pltpu.VMEM((2, span, wide), bf16),
                pltpu.VMEM((2, span, wide), f32),
                pltpu.VMEM((span, wide), bf16),
            ]),
        out_shape=[
            jax.ShapeDtypeStruct((half, mine), bf16),
            jax.ShapeDtypeStruct((half, mine), bf16),
            jax.ShapeDtypeStruct((heads, span, wide), bf16),
        ],
        compiler_params=pltpu.CompilerParams(vmem_limit_bytes=32<<20),
        cost_estimate=pl.CostEstimate(flops=4*span*span*mine, bytes_accessed=span*mine*12, transcendentals=span*span*heads),
    )(plan, qkv_own, qkv_par)

def attend_back_kernel(plan, xo_ref, xp_ref, co_ref, cp_ref, go_ref, gp_ref, qa_ref, own_ref, par_ref, kf, ka, va, ga, kt, kacc, vacc, qacc, *, hd):
    half = xo_ref.shape[0]
    span = 2*half
    wide = 2*hd
    sides = side_rows(wide, hd)
    low = [lane_row(lambda l: (l >= hd) & (l < hd+PARTS), wide, bf16), lane_row(lambda l: l < PARTS, wide, bf16)]
    parts = [part_rows(wide, hd), part_rows(wide, 0)]
    swap = cross_ones(wide, hd)
    first = lax.broadcasted_iota(jnp.int32, (half, wide), 1) < hd
    @pl.when(pl.program_id(0) == 0)
    def _():
        for s in range(2):
            kf[s] = marks(plan, span, wide, hd, s)[1]
    def place(n):
        for x_ref, c_ref, g_ref, at in ((xo_ref, co_ref, go_ref, n), (xp_ref, cp_ref, gp_ref, 1-n)):
            rows = slice(at*half, (at+1)*half)
            kp = x_ref[:, wide:2*wide]
            vp = x_ref[:, 2*wide:3*wide]
            gp = g_ref[...]
            kt[:, rows] = kp.T
            prod = gp.astype(f32) * c_ref[...].astype(f32)
            top = prod.astype(bf16)
            delta = dot_nn(top, swap) + dot_nn((prod - top.astype(f32)).astype(bf16), swap)
            for s in range(2):
                ka[s, rows, :] = kp*sides[s] + kf[s, rows, :]
                va[s, rows, :] = vp*sides[s] + low[s]
                ga[s, rows, :] = gp*sides[s] + spread(-delta, parts[s])
    by_half(plan[0], place)
    kacc[...] = jnp.zeros_like(kacc)
    vacc[...] = jnp.zeros_like(vacc)
    def work(rows, keys):
        for s in range(2):
            qq = qa_ref[s, rows, :]
            gg = ga[s, rows, :]
            probs = jnp.exp2(dot_nt(ka[s, keys, :], qq))
            slope = (probs * dot_nt(va[s, keys, :], gg)).astype(bf16)
            vacc[s, keys, :] += dot_nn(probs.astype(bf16), gg)
            kacc[s, keys, :] += dot_nn(slope, qq)
            qacc[s*hd:(s+1)*hd, rows] = dot_nn(kt[s*hd:(s+1)*hd, keys], slope)
    query_tiles(plan, span, work, TILE)
    def leave(n):
        for o_ref, at in ((own_ref, n), (par_ref, 1-n)):
            rows = slice(at*half, (at+1)*half)
            o_ref[:, 0:wide] = (qacc[:, rows].T * LN2).astype(bf16)
            o_ref[:, wide:2*wide] = (jnp.where(first, kacc[0, rows, :], kacc[1, rows, :]) * LN2).astype(bf16)
            o_ref[:, 2*wide:3*wide] = jnp.where(first, vacc[0, rows, :], vacc[1, rows, :]).astype(bf16)
    by_half(plan[0], leave)

def attend_back(plan, qkv_own, qkv_par, ctx_own, ctx_par, g_own, g_par, qa, heads, hd):
    half = qkv_own.shape[0]; span = 2*half; mine = heads*hd; wide = 2*hd
    col = lambda p, s: (0, p)
    return pl.pallas_call(
        functools.partial(attend_back_kernel, hd=hd),
        grid_spec=pltpu.PrefetchScalarGridSpec(
            num_scalar_prefetch=1, grid=(heads//2,),
            in_specs=[pl.BlockSpec((half, 3*wide), col)]*2 + [pl.BlockSpec((half, wide), col)]*4 + [pl.BlockSpec((2, span, wide), lambda p, s: (p, 0, 0))],
            out_specs=[pl.BlockSpec((half, 3*wide), col)]*2,
            scratch_shapes=[
                pltpu.VMEM((2, span, wide), bf16),
                pltpu.VMEM((2, span, wide), bf16),
                pltpu.VMEM((2, span, wide), bf16),
                pltpu.VMEM((2, span, wide), bf16),
                pltpu.VMEM((wide, span), bf16),
                pltpu.VMEM((2, span, wide), f32),
                pltpu.VMEM((2, span, wide), f32),
                pltpu.VMEM((wide, span), f32),
            ]),
        out_shape=[jax.ShapeDtypeStruct((half, 3*mine), bf16)]*2,
        compiler_params=pltpu.CompilerParams(vmem_limit_bytes=40<<20),
        cost_estimate=pl.CostEstimate(flops=10*span*span*mine, bytes_accessed=span*mine*20, transcendentals=span*span*heads),
    )(plan, qkv_own, qkv_par, ctx_own, ctx_par, g_own, g_par, qa)

def plan_row(lengths, my_block, span):
    bounds = jnp.cumsum(lengths)
    place = jnp.arange(span, dtype=jnp.int32)
    edges = jnp.concatenate([jnp.zeros((1,), jnp.int32), bounds, jnp.full((1,), span, jnp.int32)]).astype(jnp.int32)
    seg = jnp.sum((place[:, None] >= bounds[None, :]).astype(jnp.int32), axis=1)
    lo = edges[seg[0::TILE]]
    hi = edges[seg[TILE-1::TILE]+1]
    begin = lo // STEP
    count = (hi - begin*STEP + TILE-1)//TILE
    begin = jnp.minimum(begin, (span - count*TILE)//STEP)
    return jnp.concatenate([jnp.reshape(my_block, (1,)).astype(jnp.int32), bounds.astype(jnp.int32), begin.astype(jnp.int32), count.astype(jnp.int32)])


def pack_kernel(place, a_ref, q_ref, k_ref, v_ref, b_ref, out_ref, in_ref, back_ref, first_ref, second_ref, *, wide):
    lead = a_ref.shape[0]
    width = out_ref.shape[1]
    row = 0
    pieces = [a_ref[:, at : at + wide] for at in range(0, a_ref.shape[1], wide)]
    for at in range(0, q_ref.shape[1], wide):
        pieces += [ref[:, at : at + wide] for ref in (q_ref, k_ref, v_ref)]
    pieces += [b_ref[:, at : at + wide] for at in range(0, b_ref.shape[1], wide)]
    for piece in pieces:
        first_ref[row : row + piece.shape[0], :] = piece
        row += piece.shape[0]
    row = 0
    pieces = [out_ref[...]]
    pieces += [in_ref[:, at : at + width] for at in range(0, in_ref.shape[1], width)]
    pieces += [back_ref[...]]
    for piece in pieces:
        second_ref[row : row + piece.shape[0], :] = piece
        row += piece.shape[0]


def packed(place, shared_a, w_query, w_key, w_value, shared_b, w_out, w_in, w_back, part, wide):
    lead, rank = shared_a.shape
    width = w_out.shape[1]
    rows = lead * (rank + 3 * part) // wide + shared_b.shape[0] * part // wide
    whole = lambda array: pl.BlockSpec(array.shape, lambda i, s: (0, 0))
    half = lambda array: pl.BlockSpec((array.shape[0], part), lambda i, s: (0, s[0]))
    total = lead + lead * w_in.shape[1] // width + w_back.shape[0]
    return pl.pallas_call(
        functools.partial(pack_kernel, wide=wide),
        grid_spec=pltpu.PrefetchScalarGridSpec(
            num_scalar_prefetch=1,
            grid=(1,),
            in_specs=[whole(shared_a), half(w_query), half(w_key), half(w_value), half(shared_b), whole(w_out), whole(w_in), whole(w_back)],
            out_specs=[pl.BlockSpec((rows, wide), lambda i, s: (0, 0)), pl.BlockSpec((total, width), lambda i, s: (0, 0))],
        ),
        out_shape=[jax.ShapeDtypeStruct((rows, wide), bf16), jax.ShapeDtypeStruct((total, width), bf16)],
        compiler_params=pltpu.CompilerParams(vmem_limit_bytes=16 << 20),
    )(place, shared_a, w_query, w_key, w_value, shared_b, w_out, w_in, w_back)


def merge_kernel(order, *refs, shards, rank, part, wide):
    pieces = refs[:shards]
    sq_ref, sv_ref, bq_ref, bv_ref, down, lift, weights, merged, mixed = refs[shards:]
    lead = down.shape[1]
    deep = lift.shape[1]
    pairs = part // wide
    for j in range(shards):
        at = order[j]
        row = 0
        for n in range(rank // wide):
            down[at, :, n * wide : (n + 1) * wide] = pieces[j][row : row + lead, :]
            row += lead
        for n in range(3 * pairs):
            mixed[at, :, n * wide : (n + 1) * wide] = pieces[j][row : row + lead, :]
            row += lead
        for n in range(pairs):
            lift[at, :, n * wide : (n + 1) * wide] = pieces[j][row : row + deep, :]
            row += deep
    low = down[...].reshape(shards * lead, rank)
    high = lift[...].reshape(shards * deep, part)
    delta_q = dot_nn(low * sq_ref[...].astype(bf16), high)
    merged[:, :part] = delta_q.astype(bf16)
    delta_q = delta_q * bq_ref[...]
    delta_v = dot_nn(low * sv_ref[...].astype(bf16), high)
    merged[:, part:] = delta_v.astype(bf16)
    delta_v = delta_v * bv_ref[...]
    for n in range(pairs):
        cols = slice(n * wide, (n + 1) * wide)
        base = 3 * n * wide
        get = lambda s: mixed[:, :, base + s * wide : base + (s + 1) * wide].reshape(shards * lead, wide)
        weights[:, base : base + wide] = ((get(0).astype(f32) + delta_q[:, cols]) * (0.125 * LOG2E)).astype(bf16)
        weights[:, base + wide : base + 2 * wide] = get(1)
        weights[:, base + 2 * wide : base + 3 * wide] = (get(2).astype(f32) + delta_v[:, cols]).astype(bf16)


def merge(order, pieces, scale_dq, scale_dv, bend_q, bend_v, lead, deep, rank, part, wide):
    shards = len(pieces)
    width = shards * lead
    whole = lambda shape: pl.BlockSpec(shape, lambda i, s: (0,) * len(shape))
    return pl.pallas_call(
        functools.partial(merge_kernel, shards=shards, rank=rank, part=part, wide=wide),
        grid_spec=pltpu.PrefetchScalarGridSpec(
            num_scalar_prefetch=1,
            grid=(1,),
            in_specs=[whole(pieces[0].shape)] * shards + [whole((1, rank))] * 2 + [whole((1, part))] * 2,
            out_specs=[whole((shards, lead, rank)), whole((shards, deep, part)), whole((width, 3 * part)), whole((width, 2 * part))],
            scratch_shapes=[pltpu.VMEM((shards, lead, 3 * part), bf16)],
        ),
        out_shape=[
            jax.ShapeDtypeStruct((shards, lead, rank), bf16),
            jax.ShapeDtypeStruct((shards, deep, part), bf16),
            jax.ShapeDtypeStruct((width, 3 * part), bf16),
            jax.ShapeDtypeStruct((width, 2 * part), bf16),
        ],
        compiler_params=pltpu.CompilerParams(vmem_limit_bytes=40 << 20),
    )(order, *pieces, scale_dq, scale_dv, bend_q, bend_v)


def flipped(block, mask):
    count = lax.axis_size("seq")
    return lax.ppermute(block, "seq", [(i, i ^ mask) for i in range(count)])


def collected(piece, shards):
    held = {0: piece}
    for mask in range(shards - 4, 0, -4):
        held[mask] = flipped(piece, mask)
    for mask in range(0, shards, 4):
        held[mask + 1] = flipped(held[mask], 1)
        held[mask + 2] = flipped(held[mask], 2)
    for mask in range(0, shards, 4):
        held[mask + 3] = flipped(held[mask + 2], 1)
    return [held[mask] for mask in range(shards)]


def centred(hidden):
    off = hidden - jnp.mean(hidden, axis=-1, keepdims=True)
    scale = lax.rsqrt(jnp.mean(off*off, axis=-1, keepdims=True) + 1e-05)
    return off*scale, scale

def norm_back(grad, unit, scale):
    inner = jnp.mean(grad*unit, axis=-1, keepdims=True)
    return scale*(grad - jnp.mean(grad, axis=-1, keepdims=True) - unit*inner)

def gelu_pair(x):
    size = jnp.abs(x)
    base = 1.0 + size*(0.3275911*0.7071067811865476)
    t = pl.reciprocal(base, approx=True)
    t = t*(2.0 - base*t)
    bell = jnp.exp2(x*x*(-0.7213475204444817))
    tail = t*(0.127414796 + t*(-0.142248368 + t*(0.7107068705 + t*(-0.7265760135 + t*0.5307027145))))*bell
    below = jnp.where(x < 0, tail, 1.0 - tail)
    return x*below, below + x*(bell*0.3989422804014327)

def ffn_kernel(place, co_ref, cr_ref, x_ref, cot_ref, g1_ref, g2_ref, pack_ref, out_ref, grad_ref, own_ref, send_ref, wo, wi, wb, slopes, gsum, sems, *, shards, cuts):
    width = x_ref.shape[1]
    lead = wo.shape[1]
    back = wb.shape[1]
    copies = [pltpu.make_async_copy(pack_ref.at[:, 0:lead, :], wo, sems.at[0])]
    for j in range(cuts):
        copies.append(pltpu.make_async_copy(pack_ref.at[:, lead*(1+j):lead*(2+j), :], wi.at[j], sems.at[1+j]))
    per = shards//cuts
    for j in range(cuts):
        copies.append(pltpu.make_async_copy(pack_ref.at[j*per:(j+1)*per, lead*(1+cuts):lead*(1+cuts)+back, :], wb.at[j*per:(j+1)*per], sems.at[1+cuts+j]))
    for c in copies:
        c.start()
    part = shards//2
    half = width//2
    mine = place[0]
    def out_rows(who):
        return wo[pl.ds(pl.multiple_of(who*part, part), part)].reshape(half, width)
    def w_in(j): return wi[j].reshape(width, width)
    def w_back(j): return wb[j*per:(j+1)*per].reshape(per*back, width)
    copies[0].wait()
    resid = x_ref[...].astype(f32) + dot_nn(co_ref[...], out_rows(mine)) + dot_nn(cr_ref[...], out_rows(1-mine))
    unit_one, scale_one = centred(resid)
    normed = unit_one*g1_ref[...]
    low = normed.astype(bf16)
    total = normed
    for j in range(cuts):
        copies[1+j].wait()
        pre = dot_nn(low, w_in(j))
        act, slope = gelu_pair(pre)
        slopes[j] = slope.astype(bf16)
        copies[1+cuts+j].wait()
        total = total + dot_nn(act.astype(bf16), w_back(j))
    unit_two, scale_two = centred(total)
    out_ref[...] = (unit_two*g2_ref[...]).astype(bf16)
    grad_two = norm_back(cot_ref[...].astype(f32)*g2_ref[...], unit_two, scale_two)
    low_two = grad_two.astype(bf16)
    grad = grad_two
    for j in range(cuts):
        pre_grad = (dot_nt(low_two, w_back(j))*slopes[j].astype(f32)).astype(bf16)
        grad = grad + dot_nt(pre_grad, w_in(j))
    grad_one = norm_back(grad*g1_ref[...], unit_one, scale_one)
    grad_ref[...] = grad_one
    low_one = grad_one.astype(bf16)
    own_ref[...] = dot_nt(low_one, out_rows(mine)).astype(bf16)
    send_ref[...] = dot_nt(low_one, out_rows(1-mine)).astype(bf16)

def ffn(place, ctx_own, ctx_recv, x, cot, gain_one, gain_two, pack, cuts):
    span, width = x.shape
    shards, total, _ = pack.shape
    lead = width//shards
    back = cuts*width//shards
    whole = lambda shape: pl.BlockSpec(shape, lambda i, s: (0,)*len(shape))
    return pl.pallas_call(
        functools.partial(ffn_kernel, shards=shards, cuts=cuts),
        grid_spec=pltpu.PrefetchScalarGridSpec(
            num_scalar_prefetch=1, grid=(1,),
            in_specs=[whole((span, width//2)), whole((span, width//2)), whole((span, width)), whole((span, width)), whole((1, width)), whole((1, width)), pl.BlockSpec(memory_space=pl.ANY)],
            out_specs=[whole((span, width)), whole((span, width)), whole((span, width//2)), whole((span, width//2))],
            scratch_shapes=[
                pltpu.VMEM((shards, lead, width), bf16),
                pltpu.VMEM((cuts, shards, lead, width), bf16),
                pltpu.VMEM((shards, back, width), bf16),
                pltpu.VMEM((cuts, span, width), bf16),
                pltpu.VMEM((8, 128), f32),
                pltpu.SemaphoreType.DMA((1+2*cuts,)),
            ]),
        out_shape=[
            jax.ShapeDtypeStruct((span, width), bf16),
            jax.ShapeDtypeStruct((span, width), f32),
            jax.ShapeDtypeStruct((span, width//2), bf16),
            jax.ShapeDtypeStruct((span, width//2), bf16),
        ],
        compiler_params=pltpu.CompilerParams(vmem_limit_bytes=56<<20),
        cost_estimate=pl.CostEstimate(flops=2*span*width*width*(2+4*cuts), bytes_accessed=2*(2+2*cuts)*width*width, transcendentals=2*span*width*cuts),
    )(place, ctx_own, ctx_recv, x, cot, gain_one, gain_two, pack)


def shifted(shard, axis, by):
    count = lax.axis_size(axis)
    return lax.ppermute(shard, axis, [(i, (i + by) % count) for i in range(count)])


def layer_norm(hidden, gain):
    centre = hidden - jnp.mean(hidden, axis=-1, keepdims=True)
    spread = jnp.mean(centre * centre, axis=-1, keepdims=True)
    return centre * lax.rsqrt(spread + 1e-05) * gain


def exact_gelu(values):
    return jax.nn.gelu(values, approximate=False)


def segment_ids(lengths, total):
    place = jnp.arange(total, dtype=jnp.int32)[None, :]
    bounds = jnp.cumsum(lengths, axis=1)
    counted = jnp.zeros((lengths.shape[0], total), jnp.int32)
    for column in range(lengths.shape[1]):
        counted = counted + (place >= bounds[:, column : column + 1]).astype(jnp.int32)
    return counted


def dot_plain(left, right):
    return jnp.dot(left, right, preferred_element_type=jnp.float32)


def dot_trans(left, right):
    return lax.dot_general(
        left, right, (((1,), (1,)), ((), ())), preferred_element_type=jnp.float32
    )


def block_grads(query_h, out_grad, lse_rows, delta_rows, key_h, value_h, allowed):
    scores = (
        jnp.einsum("rqhd,rkhd->rqhk", query_h, key_h, preferred_element_type=jnp.float32) * 0.125
    )
    probs = jnp.where(allowed, jnp.exp(scores - lse_rows[..., None]), 0.0)
    value_grad = jnp.einsum(
        "rqhk,rqhd->rkhd", probs.astype(jnp.bfloat16), out_grad, preferred_element_type=jnp.float32
    )
    prob_grad = jnp.einsum("rqhd,rkhd->rqhk", out_grad, value_h, preferred_element_type=jnp.float32)
    score_grad = (probs * (prob_grad - delta_rows[..., None])).astype(jnp.bfloat16)
    query_grad = (
        jnp.einsum("rqhk,rkhd->rqhd", score_grad, key_h, preferred_element_type=jnp.float32) * 0.125
    )
    key_grad = (
        jnp.einsum("rqhk,rqhd->rkhd", score_grad, query_h, preferred_element_type=jnp.float32)
        * 0.125
    )
    return (query_grad, key_grad, value_grad)


def body_any(
    tokens,
    sent_lengths,
    w_query,
    w_key,
    w_value,
    w_out,
    shared_a,
    shared_b,
    w_in,
    w_back,
    gain_one,
    gain_two,
    scale_dq,
    shift_bq,
    scale_dv,
    shift_bv,
    cotangent,
):
    row_count, span, width = tokens.shape
    head_count = HEADS
    head_size = HEAD_DIM
    blocks = lax.axis_size("blk")
    my_block = lax.axis_index("blk")
    token_count = row_count * span
    token_rows = tokens.reshape(token_count, width)
    seg_full = segment_ids(sent_lengths, span * blocks)
    seg_mine = lax.dynamic_slice_in_dim(seg_full, my_block * span, span, 1)
    w_queries, w_keys, w_values, proj_a, proj_b = (
        lax.all_gather(w_query, "seq", axis=0, tiled=True),
        lax.all_gather(w_key, "seq", axis=0, tiled=True),
        lax.all_gather(w_value, "seq", axis=0, tiled=True),
        lax.all_gather(shared_a, "seq", axis=0, tiled=True),
        lax.all_gather(shared_b, "seq", axis=0, tiled=True),
    )
    projected = dot_plain(token_rows, proj_a).astype(jnp.bfloat16)
    proj_float = projected.astype(jnp.float32)
    lift_q = (proj_float * scale_dq).astype(jnp.bfloat16)
    lift_v = (proj_float * scale_dv).astype(jnp.bfloat16)
    extra_q = dot_plain(lift_q, proj_b)
    extra_v = dot_plain(lift_v, proj_b)
    queries = (dot_plain(token_rows, w_queries) + shift_bq * extra_q).astype(jnp.bfloat16)
    key_rows = dot_plain(token_rows, w_keys).astype(jnp.bfloat16)
    value_rows = (dot_plain(token_rows, w_values) + shift_bv * extra_v).astype(jnp.bfloat16)
    shape4 = (row_count, span, head_count, head_size)
    query_h = queries.reshape(shape4)
    key_h = key_rows.reshape(shape4)
    value_h = value_rows.reshape(shape4)
    start_best = jnp.full((row_count, span, head_count), -1e30, jnp.float32)
    best = start_best
    key_piece = lax.all_gather(key_rows.reshape(row_count, span, width), "blk", axis=1, tiled=True)
    value_piece = lax.all_gather(
        value_rows.reshape(row_count, span, width), "blk", axis=1, tiled=True
    )
    length = key_piece.shape[1]
    key_part = key_piece.reshape(row_count, length, head_count, head_size)
    value_part = value_piece.reshape(row_count, length, head_count, head_size)
    seg_keys = seg_full
    allowed = (seg_mine[:, :, None] == seg_keys[:, None, :])[:, :, None, :]
    scores = (
        jnp.einsum("rqhd,rkhd->rqhk", query_h, key_part, preferred_element_type=jnp.float32) * 0.125
    )
    scores = jnp.where(allowed, scores, -1e30)
    new_best = jnp.maximum(best, jnp.max(scores, axis=-1))
    weight = jnp.where(allowed, jnp.exp(scores - new_best[..., None]), 0.0)
    total = jnp.sum(weight, axis=-1)
    accum = jnp.einsum(
        "rqhk,rkhd->rqhd",
        weight.astype(jnp.bfloat16),
        value_part,
        preferred_element_type=jnp.float32,
    )
    best, total, accum = (new_best, total, accum)
    log_total = best + jnp.log(total)
    context = accum / total[..., None]
    context_b = context.reshape(token_count, width).astype(jnp.bfloat16)
    w_outs, w_ins, w_backs = (
        lax.all_gather(w_out, "seq", axis=0, tiled=True),
        lax.all_gather(w_in, "seq", axis=0, tiled=True),
        lax.all_gather(w_back, "seq", axis=0, tiled=True),
    )

    def norm_first(hidden):
        return layer_norm(hidden, gain_one)

    def norm_second(hidden):
        return layer_norm(hidden, gain_two)

    resid_one = token_rows.astype(jnp.float32) + dot_plain(context_b, w_outs)
    normed_one, norm_one_pull = jax.vjp(norm_first, resid_one)
    pre_act = dot_plain(normed_one.astype(jnp.bfloat16), w_ins)
    act_float, gelu_pull = jax.vjp(exact_gelu, pre_act)
    ffn_part = dot_plain(act_float.astype(jnp.bfloat16), w_backs)
    normed_two, norm_two_pull = jax.vjp(norm_second, normed_one + ffn_part)
    layer_out = normed_two.astype(jnp.bfloat16).reshape(row_count, span, width)
    w_outs, w_ins, w_backs = (
        lax.all_gather(w_out, "seq", axis=0, tiled=True),
        lax.all_gather(w_in, "seq", axis=0, tiled=True),
        lax.all_gather(w_back, "seq", axis=0, tiled=True),
    )
    (grad_two,) = norm_two_pull(cotangent.reshape(token_count, width).astype(jnp.float32))
    act_grad = dot_trans(grad_two.astype(jnp.bfloat16), w_backs)
    (pre_grad,) = gelu_pull(act_grad)
    normed_grad = grad_two + dot_trans(pre_grad.astype(jnp.bfloat16), w_ins)
    (grad_one,) = norm_one_pull(normed_grad)
    context_grad = dot_trans(grad_one.astype(jnp.bfloat16), w_outs).astype(jnp.bfloat16)
    out_grad = context_grad.reshape(shape4)
    delta_rows = jnp.sum(out_grad.astype(jnp.float32) * context, axis=-1)
    zero_grads = jnp.zeros(shape4, jnp.float32)

    def key_step(step, carry):
        key_cur, value_cur, query_acc, key_acc, value_acc = carry
        source = (my_block - step) % blocks
        seg_keys = lax.dynamic_slice_in_dim(seg_full, source * span, span, 1)
        allowed = (seg_mine[:, :, None] == seg_keys[:, None, :])[:, :, None, :]
        q_part, k_part, v_part = block_grads(
            query_h, out_grad, log_total, delta_rows, key_cur, value_cur, allowed
        )
        key_acc, value_acc = (
            shifted((key_acc + k_part).astype(jnp.bfloat16), "blk", 1).astype(jnp.float32),
            shifted((value_acc + v_part).astype(jnp.bfloat16), "blk", 1).astype(jnp.float32),
        )
        key_cur, value_cur = shifted((key_cur, value_cur), "blk", 1)
        return (key_cur, value_cur, query_acc + q_part, key_acc, value_acc)

    looped = lax.fori_loop(
        0, blocks, key_step, (key_h, value_h, zero_grads, zero_grads, zero_grads)
    )
    query_acc, key_acc, value_acc = (looped[2], looped[3], looped[4])
    query_grad = query_acc.reshape(token_count, width).astype(jnp.bfloat16)
    key_grad = key_acc.reshape(token_count, width).astype(jnp.bfloat16)
    value_grad = value_acc.reshape(token_count, width).astype(jnp.bfloat16)
    w_queries, w_keys, w_values, proj_a, proj_b = (
        lax.all_gather(w_query, "seq", axis=0, tiled=True),
        lax.all_gather(w_key, "seq", axis=0, tiled=True),
        lax.all_gather(w_value, "seq", axis=0, tiled=True),
        lax.all_gather(shared_a, "seq", axis=0, tiled=True),
        lax.all_gather(shared_b, "seq", axis=0, tiled=True),
    )
    query_float = query_grad.astype(jnp.float32)
    value_float = value_grad.astype(jnp.float32)
    part_bq = jnp.sum(query_float * extra_q, axis=0)
    part_bv = jnp.sum(value_float * extra_v, axis=0)
    lift_q_grad = dot_trans((query_float * shift_bq).astype(jnp.bfloat16), proj_b)
    lift_v_grad = dot_trans((value_float * shift_bv).astype(jnp.bfloat16), proj_b)
    part_dq = jnp.sum(lift_q_grad * proj_float, axis=0)
    part_dv = jnp.sum(lift_v_grad * proj_float, axis=0)
    proj_grad = (lift_q_grad * scale_dq + lift_v_grad * scale_dv).astype(jnp.bfloat16)
    token_grad = (
        grad_one
        + dot_trans(query_grad, w_queries)
        + dot_trans(key_grad, w_keys)
        + dot_trans(value_grad, w_values)
        + dot_trans(proj_grad, proj_a)
    )
    grad_dq, grad_bq, grad_dv, grad_bv = lax.psum(
        (part_dq, part_bq, part_dv, part_bv), ("seq", "blk")
    )
    return (
        layer_out,
        token_grad.astype(jnp.bfloat16).reshape(row_count, span, width),
        grad_dq,
        grad_bq,
        grad_dv,
        grad_bv,
    )


def swapped(block):
    return lax.ppermute(block, "blk", [(0, 1), (1, 0)])


def summed(vector, groups):
    vector = vector + swapped(vector)
    hop = 1
    while hop < groups:
        vector = vector + flipped(vector, hop)
        hop *= 2
    return vector


def body_two(
    tokens,
    sent_lengths,
    w_query,
    w_key,
    w_value,
    w_out,
    shared_a,
    shared_b,
    w_in,
    w_back,
    gain_one,
    gain_two,
    scale_dq,
    shift_bq,
    scale_dv,
    shift_bv,
    cotangent,
):
    row_count, span, width = tokens.shape
    shards = lax.axis_size("seq")
    mine = lax.axis_index("blk")
    heads = HEADS // 2
    part = heads * HEAD_DIM
    wide = 2 * HEAD_DIM
    pairs = heads // 2
    lead, rank = shared_a.shape
    cuts = w_in.shape[1] // width
    coef = 0.125 * LOG2E
    rows = range(row_count)
    place = jnp.reshape(mine, (1,)).astype(jnp.int32)

    def columns(vector):
        return lax.dynamic_slice_in_dim(vector, mine * part, part, 0)

    first_pack, second_pack = packed(
        place, shared_a, w_query, w_key, w_value, shared_b, w_out, w_in, w_back, part, wide
    )
    pack = lax.all_gather(second_pack, "seq", axis=0)
    pieces = collected(first_pack, shards)
    other = [swapped(tokens[row]) for row in rows]
    order = jnp.arange(shards, dtype=jnp.int32) ^ lax.axis_index("seq").astype(jnp.int32)
    bend_q = columns(shift_bq)
    bend_v = columns(shift_bv)
    down, lift, weights, merged = merge(
        order, pieces, scale_dq.reshape(1, rank), scale_dv.reshape(1, rank),
        bend_q.reshape(1, part), bend_v.reshape(1, part), lead, shared_b.shape[0], rank, part, wide,
    )
    down = down.reshape(width, rank)
    lift = lift.reshape(rank, part)
    g_one = gain_one.reshape(1, width)
    g_two = gain_two.reshape(1, width)

    plans = [plan_row(sent_lengths[row], mine, 2 * span) for row in rows]
    qkv_own = [dot_nn(tokens[row], weights).astype(bf16) for row in rows]
    qkv_par = [dot_nn(other[row], weights).astype(bf16) for row in rows]
    seen = [attend(plans[row], qkv_own[row], qkv_par[row], heads, HEAD_DIM) for row in rows]
    ctx_recv = [swapped(seen[row][1]) for row in rows]
    fed = [
        ffn(place, seen[row][0], ctx_recv[row], tokens[row], cotangent[row], g_one, g_two, pack, cuts)
        for row in rows
    ]
    grad_recv = [swapped(fed[row][3]) for row in rows]
    sent = []
    turned = []
    for row in rows:
        grads = attend_back(
            plans[row], qkv_own[row], qkv_par[row], seen[row][0], seen[row][1],
            fed[row][2], grad_recv[row], seen[row][2], heads, HEAD_DIM,
        )
        partial = dot_nt(grads[1], weights).astype(bf16)
        if sent:
            grads, partial, sent[-1] = lax.optimization_barrier((grads, partial, sent[-1]))
        turned.append(grads)
        sent.append(swapped(partial))

    token_grad = [
        (fed[row][1] + dot_nt(turned[row][0], weights) + sent[row].astype(f32)).astype(bf16)
        for row in rows
    ]

    def outer(left, right):
        return lax.dot_general(left, right, (((0,), (0,)), ((), ())), preferred_element_type=f32)

    moment = sum(outer(tokens[row], turned[row][0]) + outer(other[row], turned[row][1]) for row in rows)
    moment_q = jnp.concatenate([moment[:, 3 * n * wide : (3 * n + 1) * wide] for n in range(pairs)], axis=1)
    moment_v = jnp.concatenate(
        [moment[:, (3 * n + 2) * wide : (3 * n + 3) * wide] for n in range(pairs)], axis=1
    )
    moment_q = moment_q * coef
    down_f = down.astype(f32)
    merged_f = merged.astype(f32)

    def whole(piece):
        return lax.dynamic_update_slice(jnp.zeros((width,), f32), piece, (mine * part,))

    part_bq = whole(jnp.sum(merged_f[:, :part] * moment_q, axis=0))
    part_bv = whole(jnp.sum(merged_f[:, part:] * moment_v, axis=0))
    part_dq = jnp.sum(down_f * dot_nt((moment_q * bend_q).astype(bf16), lift), axis=0)
    part_dv = jnp.sum(down_f * dot_nt((moment_v * bend_v).astype(bf16), lift), axis=0)
    flat = jnp.concatenate([part_dq, part_bq, part_dv, part_bv]).reshape(-1, 128)
    flat = summed(flat, shards).reshape(-1)
    return (
        jnp.stack([fed[row][0] for row in rows]),
        jnp.stack(token_grad),
        flat[:rank],
        flat[rank : rank + width],
        flat[rank + width : 2 * rank + width],
        flat[2 * rank + width :],
    )


def solution(mesh):
    return jax.shard_map(
        body_two if mesh.shape["blk"] == 2 and mesh.shape["seq"] == 16 else body_any,
        mesh=mesh,
        in_specs=(
            P("seq", "blk", None),
            P("seq", None),
            P("seq", None),
            P("seq", None),
            P("seq", None),
            P("seq", None),
            P("seq", None),
            P("seq", None),
            P("seq", None),
            P("seq", None),
            P(),
            P(),
            P(),
            P(),
            P(),
            P(),
            P("seq", "blk", None),
        ),
        out_specs=(P("seq", "blk", None), P("seq", "blk", None), P(), P(), P(), P()),
        check_vma=False,
    )
```

```python
import functools

import jax
import jax.numpy as jnp
from jax import lax
from jax.experimental import pallas as pl
from jax.experimental.pallas import tpu as pltpu
from jax.sharding import PartitionSpec as P

HEADS = 12
HEAD_DIM = 64
bf16 = jnp.bfloat16
f32 = jnp.float32


LN2 = 0.6931471805599453
LOG2E = 1.4426950408889634
SEGS = 5
PARTS = 3
TILE = 256
STEP = 128

def dot_nt(a,b): return lax.dot_general(a,b,(((1,),(1,)),((),())),preferred_element_type=f32)
def dot_nn(a,b): return jnp.dot(a,b,preferred_element_type=f32)

def lane_row(test, wide, kind=f32):
    lane = lax.broadcasted_iota(jnp.int32, (1, wide), 1)
    return jnp.where(test(lane), 1.0, 0.0).astype(kind)

def part_rows(wide, start):
    return [lane_row(lambda l: l == start + n, wide) for n in range(PARTS)]

def spread(column, rows):
    top = column.astype(bf16).astype(f32)
    return (top*rows[0] + (column-top)*rows[1]).astype(bf16)

def cross_ones(wide, hd):
    a = lax.broadcasted_iota(jnp.int32, (wide, wide), 0) < hd
    b = lax.broadcasted_iota(jnp.int32, (wide, wide), 1) < hd
    return jnp.where(a != b, 1.0, 0.0).astype(bf16)

def side_rows(wide, hd):
    return [lane_row(lambda l: l < hd, wide, bf16), lane_row(lambda l: l >= hd, wide, bf16)]

def bounds_of(lens, row):
    bounds = [lens[row, 0]]
    for n in range(1, SEGS-1):
        bounds.append(bounds[-1] + lens[row, n])
    return bounds

def key_span(bounds, i, span):
    low = 0
    for bound in bounds:
        low = jnp.where(bound <= i*TILE, bound, low)
    high = span
    for bound in reversed(bounds):
        high = jnp.where(bound > i*TILE + TILE-1, bound, high)
    begin = lax.div(low, STEP)
    count = lax.div(high - begin*STEP + TILE-1, TILE)
    return jnp.minimum(begin, lax.div(span - count*TILE, STEP)), count

def marks(bounds, span, wide, hd, side):
    place = lax.broadcasted_iota(jnp.int32, (span, wide), 0)
    lane = lax.broadcasted_iota(jnp.int32, (span, wide), 1) - (hd if side == 0 else 0)
    lane = jnp.where((lane >= 0) & (lane < hd), lane, hd)
    seg = jnp.zeros((span, wide), jnp.int32)
    for bound in bounds:
        seg = seg + jnp.where(place >= bound, 1, 0)
    asked = jnp.where((lane < SEGS) & (lane != seg), 1.0, 0.0).astype(bf16)
    held = jnp.where(lane == seg, -1e30, jnp.where((lane >= SEGS) & (lane < SEGS+PARTS), 1.0, 0.0)).astype(bf16)
    return asked, held

def by_half(mine, work):
    for n in range(2):
        @pl.when(mine == n)
        def _():
            work(n)

def query_tiles(bounds, span, work, broad):
    tiles = span//TILE
    fewest = tiles
    for i in range(tiles):
        fewest = jnp.minimum(fewest, key_span(bounds, i, span)[1])
    @pl.when(fewest == tiles)
    def _():
        def one(i, carry):
            work(pl.ds(pl.multiple_of(i*broad, broad), broad), slice(0, span))
            return carry
        lax.fori_loop(0, span//broad, one, 0)
    @pl.when(fewest < tiles)
    def _():
        def one(i, carry):
            rows = pl.ds(pl.multiple_of(i*TILE, TILE), TILE)
            begin, count = key_span(bounds, i, span)
            start = pl.multiple_of(begin*STEP, STEP)
            for n in range(1, tiles+1):
                @pl.when(count == n)
                def _():
                    work(rows, pl.ds(start, n*TILE) if n < tiles else slice(0, span))
            return carry
        lax.fori_loop(0, tiles, one, 0)

def attend_kernel(spot, lens, xo_ref, xp_ref, own_ref, par_ref, qa_ref, qf, kf, ka, va, og, outs, *, hd, row):
    half = xo_ref.shape[0]
    bounds = bounds_of(lens, row)
    span = 2*half
    wide = 2*hd
    sides = side_rows(wide, hd)
    swap = cross_ones(wide, hd)
    first = lax.broadcasted_iota(jnp.int32, (span, wide), 1) < hd
    start = [hd+SEGS, SEGS]
    parts = [part_rows(wide, start[s]) for s in range(2)]
    @pl.when(pl.program_id(0) == 0)
    def _():
        for s in range(2):
            qf[s], kf[s] = marks(bounds, span, wide, hd, s)
    longest = None
    for x_ref in (xo_ref, xp_ref):
        kp = x_ref[:, wide:2*wide]
        norms = jnp.max(dot_nn(kp*kp, swap), axis=0, keepdims=True)
        longest = norms if longest is None else jnp.maximum(longest, norms)
    def place(n):
        for x_ref, at in ((xo_ref, n), (xp_ref, 1-n)):
            rows = slice(at*half, (at+1)*half)
            qp = x_ref[:, 0:wide]
            kp = x_ref[:, wide:2*wide]
            vp = x_ref[:, 2*wide:3*wide]
            top = jnp.sqrt(dot_nn(qp*qp, swap) * longest) * 1.02
            for s in range(2):
                qa_ref[s, rows, :] = qp*sides[s] + (qf[s, rows, :] - (top*parts[s][0]).astype(bf16))
                ka[s, rows, :] = kp*sides[s] + kf[s, rows, :]
                va[s, rows, :] = vp*sides[s] + sides[1-s]
    by_half(spot[0], place)
    def weigh(rows, keys):
        for s in range(2):
            w = jnp.exp2(dot_nt(qa_ref[s, rows, :], ka[s, keys, :])).astype(bf16)
            og[s, rows, :] = dot_nn(w, va[s, keys, :])
    query_tiles(bounds, span, weigh, 512)
    @pl.when(jnp.logical_not(jnp.min(jnp.where(first, og[1], og[0])) > 2.0**-80))
    def _():
        def exact_tile(i, carry):
            rows = pl.ds(pl.multiple_of(i*TILE, TILE), TILE)
            for s in range(2):
                plain = qa_ref[s, rows, :] * (1.0 - parts[s][0]).astype(bf16)
                m = jnp.max(dot_nt(plain, ka[s]), axis=1, keepdims=True)
                qa_ref[s, rows, :] = plain - (jnp.broadcast_to(m, (TILE, wide))*parts[s][0]).astype(bf16)
            weigh(rows, slice(0, span))
            return carry
        lax.fori_loop(0, span//TILE, exact_tile, 0)
    total = jnp.where(first, og[1], og[0])
    outs[...] = (jnp.where(first, og[0], og[1]) / pltpu.roll(total, hd, 1)).astype(bf16)
    lse = -jnp.log2(total)
    for s in range(2):
        qa_ref[s] = qa_ref[s] + spread(lse, parts[s][1:])
    def leave(n):
        own_ref[...] = outs[n*half:(n+1)*half, :]
        par_ref[...] = outs[(1-n)*half:(2-n)*half, :]
    by_half(spot[0], leave)

def attend(row, spot, lens, qkv_own, qkv_par, heads, hd):
    half = qkv_own.shape[0]//lens.shape[0]; span = 2*half; mine = heads*hd; wide = 2*hd
    col = lambda p, s, l: (0, p)
    return pl.pallas_call(
        functools.partial(attend_kernel, hd=hd, row=row),
        grid_spec=pltpu.PrefetchScalarGridSpec(
            num_scalar_prefetch=2, grid=(heads//2,),
            in_specs=[pl.BlockSpec((half, 3*wide), lambda p, s, l: (row, p))]*2,
            out_specs=[
                pl.BlockSpec((half, wide), col),
                pl.BlockSpec((half, wide), col),
                pl.BlockSpec((2, span, wide), lambda p, s, l: (p, 0, 0)),
            ],
            scratch_shapes=[
                pltpu.VMEM((2, span, wide), bf16),
                pltpu.VMEM((2, span, wide), bf16),
                pltpu.VMEM((2, span, wide), bf16),
                pltpu.VMEM((2, span, wide), bf16),
                pltpu.VMEM((2, span, wide), f32),
                pltpu.VMEM((span, wide), bf16),
            ]),
        out_shape=[
            jax.ShapeDtypeStruct((half, mine), bf16),
            jax.ShapeDtypeStruct((half, mine), bf16),
            jax.ShapeDtypeStruct((heads, span, wide), bf16),
        ],
        compiler_params=pltpu.CompilerParams(vmem_limit_bytes=32<<20),
        cost_estimate=pl.CostEstimate(flops=16*span*span*mine, bytes_accessed=span*mine*12, transcendentals=span*span*heads),
    )(spot, lens, qkv_own, qkv_par)

def attend_back_kernel(spot, lens, xo_ref, xp_ref, co_ref, cp_ref, go_ref, gp_ref, qa_ref, *refs, hd, row):
    own_ref, par_ref, kf, ka, va, ga, kt, kacc, vacc, qacc = refs[-10:]
    half = xo_ref.shape[0]
    bounds = bounds_of(lens, row)
    span = 2*half
    wide = 2*hd
    sides = side_rows(wide, hd)
    low = [lane_row(lambda l: (l >= hd) & (l < hd+PARTS), wide, bf16), lane_row(lambda l: l < PARTS, wide, bf16)]
    parts = [part_rows(wide, hd), part_rows(wide, 0)]
    swap = cross_ones(wide, hd)
    first = lax.broadcasted_iota(jnp.int32, (half, wide), 1) < hd
    @pl.when(pl.program_id(0) == 0)
    def _():
        for s in range(2):
            kf[s] = marks(bounds, span, wide, hd, s)[1]
    def place(n):
        for x_ref, c_ref, g_ref, at in ((xo_ref, co_ref, go_ref, n), (xp_ref, cp_ref, gp_ref, 1-n)):
            rows = slice(at*half, (at+1)*half)
            kp = x_ref[:, wide:2*wide]
            vp = x_ref[:, 2*wide:3*wide]
            gp = g_ref[...]
            kt[:, rows] = kp.T
            prod = gp.astype(f32) * c_ref[...].astype(f32)
            top = prod.astype(bf16)
            delta = dot_nn(top, swap) + dot_nn((prod - top.astype(f32)).astype(bf16), swap)
            for s in range(2):
                ka[s, rows, :] = kp*sides[s] + kf[s, rows, :]
                va[s, rows, :] = vp*sides[s] + low[s]
                ga[s, rows, :] = gp*sides[s] + spread(-delta, parts[s])
    by_half(spot[0], place)
    kacc[...] = jnp.zeros_like(kacc)
    vacc[...] = jnp.zeros_like(vacc)
    def work(rows, keys):
        for s in range(2):
            qq = qa_ref[s, rows, :]
            gg = ga[s, rows, :]
            probs = jnp.exp2(dot_nt(ka[s, keys, :], qq))
            slope = (probs * dot_nt(va[s, keys, :], gg)).astype(bf16)
            vacc[s, keys, :] += dot_nn(probs.astype(bf16), gg)
            kacc[s, keys, :] += dot_nn(slope, qq)
            qacc[s*hd:(s+1)*hd, rows] = dot_nn(kt[s*hd:(s+1)*hd, keys], slope)
    query_tiles(bounds, span, work, TILE)
    def leave(n):
        for o_ref, at in ((own_ref, n), (par_ref, 1-n)):
            rows = slice(at*half, (at+1)*half)
            o_ref[:, 0:wide] = (qacc[:, rows].T * LN2).astype(bf16)
            o_ref[:, wide:2*wide] = (jnp.where(first, kacc[0, rows, :], kacc[1, rows, :]) * LN2).astype(bf16)
            o_ref[:, 2*wide:3*wide] = jnp.where(first, vacc[0, rows, :], vacc[1, rows, :]).astype(bf16)
    by_half(spot[0], leave)

def attend_back(row, spot, lens, qkv_own, qkv_par, ctx_own, ctx_par, g_own, g_par, qa, before, heads, hd):
    count = lens.shape[0]
    half = qkv_own.shape[0]//count; span = 2*half; mine = heads*hd; wide = 2*hd
    col = lambda p, s, l: (0, p)
    at_row = lambda p, s, l: (row, p)
    return pl.pallas_call(
        functools.partial(attend_back_kernel, hd=hd, row=row),
        grid_spec=pltpu.PrefetchScalarGridSpec(
            num_scalar_prefetch=2, grid=(heads//2,),
            in_specs=[pl.BlockSpec((half, 3*wide), at_row)]*2 + [pl.BlockSpec((half, wide), col)]*4
            + [pl.BlockSpec((2, span, wide), lambda p, s, l: (p, 0, 0))] + [pl.BlockSpec(memory_space=pl.ANY)]*len(before),
            out_specs=[pl.BlockSpec((half, 3*wide), at_row)]*2,
            scratch_shapes=[
                pltpu.VMEM((2, span, wide), bf16),
                pltpu.VMEM((2, span, wide), bf16),
                pltpu.VMEM((2, span, wide), bf16),
                pltpu.VMEM((2, span, wide), bf16),
                pltpu.VMEM((wide, span), bf16),
                pltpu.VMEM((2, span, wide), f32),
                pltpu.VMEM((2, span, wide), f32),
                pltpu.VMEM((wide, span), f32),
            ]),
        out_shape=[jax.ShapeDtypeStruct((count*half, 3*mine), bf16)]*2,
        input_output_aliases={9+n: n for n in range(len(before))},
        compiler_params=pltpu.CompilerParams(vmem_limit_bytes=40<<20),
        cost_estimate=pl.CostEstimate(flops=40*span*span*mine, bytes_accessed=span*mine*20, transcendentals=span*span*heads),
    )(spot, lens, qkv_own, qkv_par, ctx_own, ctx_par, g_own, g_par, qa, *before)


def pack_kernel(place, a_ref, q_ref, k_ref, v_ref, b_ref, out_ref, in_ref, back_ref, *refs, wide):
    vectors, (first_ref, second_ref, vecs) = refs[:-3], refs[-3:]
    vecs[...] = jnp.zeros_like(vecs)
    for n, ref in enumerate(vectors):
        vecs[n : n + 1, : ref.shape[0]] = ref[...].reshape(1, ref.shape[0])
    lead = a_ref.shape[0]
    width = out_ref.shape[1]
    row = 0
    pieces = [a_ref[:, at : at + wide] for at in range(0, a_ref.shape[1], wide)]
    for at in range(0, q_ref.shape[1], wide):
        pieces += [ref[:, at : at + wide] for ref in (q_ref, k_ref, v_ref)]
    pieces += [b_ref[:, at : at + wide] for at in range(0, b_ref.shape[1], wide)]
    for piece in pieces:
        first_ref[row : row + piece.shape[0], :] = piece
        row += piece.shape[0]
    row = 0
    pieces = [out_ref[...]]
    pieces += [in_ref[:, at : at + width] for at in range(0, in_ref.shape[1], width)]
    pieces += [back_ref[...]]
    for piece in pieces:
        second_ref[row : row + piece.shape[0], :] = piece
        row += piece.shape[0]


def packed(place, shared_a, w_query, w_key, w_value, shared_b, w_out, w_in, w_back, vectors, part, wide):
    lead, rank = shared_a.shape
    width = w_out.shape[1]
    rows = lead * (rank + 3 * part) // wide + shared_b.shape[0] * part // wide
    whole = lambda array: pl.BlockSpec(array.shape, lambda i, s: (0, 0))
    half = lambda array: pl.BlockSpec((array.shape[0], part), lambda i, s: (0, s[0]))
    total = lead + lead * w_in.shape[1] // width + w_back.shape[0]
    return pl.pallas_call(
        functools.partial(pack_kernel, wide=wide),
        grid_spec=pltpu.PrefetchScalarGridSpec(
            num_scalar_prefetch=1,
            grid=(1,),
            in_specs=[whole(shared_a), half(w_query), half(w_key), half(w_value), half(shared_b), whole(w_out), whole(w_in), whole(w_back)]
            + [pl.BlockSpec(vector.shape, lambda i, s: (0,)) for vector in vectors],
            out_specs=[pl.BlockSpec((rows, wide), lambda i, s: (0, 0)), pl.BlockSpec((total, width), lambda i, s: (0, 0)), pl.BlockSpec((8, rank), lambda i, s: (0, 0))],
        ),
        out_shape=[jax.ShapeDtypeStruct((rows, wide), bf16), jax.ShapeDtypeStruct((total, width), bf16), jax.ShapeDtypeStruct((8, rank), f32)],
        compiler_params=pltpu.CompilerParams(vmem_limit_bytes=60 << 20),
    )(place, shared_a, w_query, w_key, w_value, shared_b, w_out, w_in, w_back, *vectors)


def bent(vecs, at, side, part):
    row = vecs[at : at + 1, : 2 * part]
    return jnp.where(side == 0, row[:, :part], row[:, part:])


def merge_kernel(spot, *refs, shards, rank, part, wide):
    quads = refs[:4]
    vecs, down, lift, weights, merged, mixed = refs[4:]
    each = quads[0].shape[0] // 4
    lead = down.shape[1]
    deep = lift.shape[1]
    pairs = part // wide
    for j in range(shards):
        at = spot[1] ^ j
        piece = quads[j % 4]
        row = each * (j // 4)
        for n in range(rank // wide):
            down[at, :, n * wide : (n + 1) * wide] = piece[row : row + lead, :]
            row += lead
        for n in range(3 * pairs):
            mixed[at, :, n * wide : (n + 1) * wide] = piece[row : row + lead, :]
            row += lead
        for n in range(pairs):
            lift[at, :, n * wide : (n + 1) * wide] = piece[row : row + deep, :]
            row += deep
    low = down[...].reshape(shards * lead, rank)
    high = lift[...].reshape(shards * deep, part)
    delta_q = dot_nn(low * vecs[0:1, :].astype(bf16), high)
    merged[:, :part] = delta_q.astype(bf16)
    delta_q = delta_q * bent(vecs, 2, spot[0], part)
    delta_v = dot_nn(low * vecs[1:2, :].astype(bf16), high)
    merged[:, part:] = delta_v.astype(bf16)
    delta_v = delta_v * bent(vecs, 3, spot[0], part)
    for n in range(pairs):
        cols = slice(n * wide, (n + 1) * wide)
        base = 3 * n * wide
        get = lambda s: mixed[:, :, base + s * wide : base + (s + 1) * wide].reshape(shards * lead, wide)
        weights[:, base : base + wide] = ((get(0).astype(f32) + delta_q[:, cols]) * (0.125 * LOG2E)).astype(bf16)
        weights[:, base + wide : base + 2 * wide] = get(1)
        weights[:, base + 2 * wide : base + 3 * wide] = (get(2).astype(f32) + delta_v[:, cols]).astype(bf16)


def merge(spot, quads, vecs, shards, lead, deep, rank, part, wide):
    width = shards * lead
    whole = lambda shape: pl.BlockSpec(shape, lambda i, s: (0,) * len(shape))
    return pl.pallas_call(
        functools.partial(merge_kernel, shards=shards, rank=rank, part=part, wide=wide),
        grid_spec=pltpu.PrefetchScalarGridSpec(
            num_scalar_prefetch=1,
            grid=(1,),
            in_specs=[whole(quads[0].shape)] * 4 + [whole(vecs.shape)],
            out_specs=[whole((shards, lead, rank)), whole((shards, deep, part)), whole((width, 3 * part)), whole((width, 2 * part))],
            scratch_shapes=[pltpu.VMEM((shards, lead, 3 * part), bf16)],
        ),
        out_shape=[
            jax.ShapeDtypeStruct((shards, lead, rank), bf16),
            jax.ShapeDtypeStruct((shards, deep, part), bf16),
            jax.ShapeDtypeStruct((width, 3 * part), bf16),
            jax.ShapeDtypeStruct((width, 2 * part), bf16),
        ],
        compiler_params=pltpu.CompilerParams(vmem_limit_bytes=40 << 20),
        cost_estimate=pl.CostEstimate(flops=40 * width * rank * part, bytes_accessed=1 << 20, transcendentals=0),
    )(spot, *quads, vecs)


def flipped(block, mask):
    count = lax.axis_size("seq")
    return lax.ppermute(block, "seq", [(i, i ^ mask) for i in range(count)])


def far_piece(piece):
    count = lax.axis_size("seq")
    pairs = [(2 * i + b, 2 * (i ^ (8 + 4 * b)) + b) for i in range(count) for b in range(2)]
    return lax.ppermute(piece, ("seq", "blk"), pairs)


def spread_square(block):
    across = flipped(block, 2)
    return [block, flipped(block, 1), across, flipped(across, 1)]


def trained_kernel(spot, moment_ref, merged_ref, down_ref, lift_ref, vecs, out_ref, *, wide):
    lead = down_ref.shape[1]
    width = down_ref.shape[0] * lead
    rank = down_ref.shape[2]
    part = lift_ref.shape[2]
    pairs = part // wide
    coef = 0.125 * LOG2E
    down = down_ref[...].reshape(width, rank).astype(f32)
    lift = lift_ref[...].reshape(rank, part)
    out_ref[...] = jnp.zeros_like(out_ref)
    base = 0
    for s in (0, 2):
        pieces = [moment_ref[:, (3 * n + s) * wide : (3 * n + s + 1) * wide] for n in range(pairs)]
        moment = jnp.concatenate(pieces, axis=1)
        if s == 0:
            moment = moment * coef
        held = merged_ref[:, s // 2 * part : (s // 2 + 1) * part].astype(f32)
        shift = jnp.sum(held * moment, axis=0, keepdims=True)
        bent_moment = (moment * bent(vecs, 2 + s // 2, spot[0], part)).astype(bf16)
        scale = jnp.sum(down * dot_nt(bent_moment, lift), axis=0, keepdims=True)
        for n in range(rank // wide):
            out_ref[base + n : base + n + 1, :] = scale[:, n * wide : (n + 1) * wide]
        base += rank // wide
        for n in range(pairs):
            out_ref[pl.ds(base + pairs * spot[0] + n, 1), :] = shift[:, n * wide : (n + 1) * wide]
        base += 2 * pairs


def trained(spot, moment, merged, down, lift, vecs, wide):
    rank, part = down.shape[2], lift.shape[2]
    whole = lambda array: pl.BlockSpec(array.shape, lambda i, s: (0,) * array.ndim)
    rows = 2 * (rank + 2 * part) // wide
    arrays = (moment, merged, down, lift, vecs)
    return pl.pallas_call(
        functools.partial(trained_kernel, wide=wide),
        grid_spec=pltpu.PrefetchScalarGridSpec(
            num_scalar_prefetch=1,
            grid=(1,),
            in_specs=[whole(array) for array in arrays],
            out_specs=pl.BlockSpec((rows, wide), lambda i, s: (0, 0)),
        ),
        out_shape=jax.ShapeDtypeStruct((rows, wide), f32),
        compiler_params=pltpu.CompilerParams(vmem_limit_bytes=60 << 20),
    )(spot, *arrays)


def finish_kernel(base_ref, sent_ref, *refs):
    refs[-1][...] = (base_ref[...] + sent_ref[...].astype(f32)).astype(bf16)


def finish(row, count, base, sent, before):
    span, width = sent.shape
    at_row = pl.BlockSpec((span, width), lambda i: (row, 0))
    return pl.pallas_call(
        finish_kernel,
        grid=(1,),
        in_specs=[at_row, pl.BlockSpec((span, width), lambda i: (0, 0))] + [pl.BlockSpec(memory_space=pl.ANY)] * len(before),
        out_specs=pl.BlockSpec((None, span, width), lambda i: (row, 0, 0)),
        out_shape=jax.ShapeDtypeStruct((count, span, width), bf16),
        input_output_aliases={2 + n: n for n in range(len(before))},
        compiler_params=pltpu.CompilerParams(vmem_limit_bytes=60 << 20),
    )(base, sent, *before)


def centred(hidden):
    off = hidden - jnp.mean(hidden, axis=-1, keepdims=True)
    scale = lax.rsqrt(jnp.mean(off*off, axis=-1, keepdims=True) + 1e-05)
    return off*scale, scale

def norm_back(grad, unit, scale):
    inner = jnp.mean(grad*unit, axis=-1, keepdims=True)
    return scale*(grad - jnp.mean(grad, axis=-1, keepdims=True) - unit*inner)

def gelu_pair(x):
    size = jnp.abs(x)
    base = 1.0 + size*(0.3275911*0.7071067811865476)
    t = pl.reciprocal(base, approx=True)
    t = t*(2.0 - base*t)
    bell = jnp.exp2(x*x*(-0.7213475204444817))
    tail = t*(0.127414796 + t*(-0.142248368 + t*(0.7107068705 + t*(-0.7265760135 + t*0.5307027145))))*bell
    below = jnp.where(x < 0, tail, 1.0 - tail)
    return x*below, below + x*(bell*0.3989422804014327)

def ffn_kernel(spot, co_ref, cr_ref, x_ref, cot_ref, g1_ref, g2_ref, *refs, shards, cuts):
    pieces = refs[:shards]
    out_ref, grad_ref, own_ref, send_ref, wo, wi, wb, acts, slopes, sems = refs[-10:]
    width = x_ref.shape[1]
    lead = wo.shape[1]
    back = wb.shape[1]
    mine = spot[0]
    groups = [0, 4, 8 + 4*mine, 12 - 4*mine]
    ats = [spot[1] ^ (groups[j//4] + j%4) for j in range(shards)]
    for j in range(shards):
        pltpu.make_async_copy(pieces[j].at[0:lead, :], wo.at[ats[j]], sems.at[0]).start()
    for n in range(cuts):
        for j in range(shards):
            rows = slice(lead*(1+n), lead*(2+n))
            pltpu.make_async_copy(pieces[j].at[rows, :], wi.at[n, ats[j]], sems.at[1+n]).start()
    for j in range(shards):
        rows = slice(lead*(1+cuts), lead*(1+cuts)+back)
        pltpu.make_async_copy(pieces[j].at[rows, :], wb.at[ats[j]], sems.at[1+cuts]).start()
    def arrived(held, n):
        pltpu.make_async_copy(held, held, sems.at[n]).wait()
    part = shards//2
    half = width//2
    def out_rows(who):
        return wo[pl.ds(pl.multiple_of(who*part, part), part)].reshape(half, width)
    def w_in(j): return wi[j].reshape(width, width)
    def w_back(): return wb[...].reshape(shards*back, width)
    arrived(wo, 0)
    resid = x_ref[...].astype(f32) + dot_nn(co_ref[...], out_rows(mine)) + dot_nn(cr_ref[...], out_rows(1-mine))
    unit_one, scale_one = centred(resid)
    gain_one = g1_ref[...].reshape(1, width)
    gain_two = g2_ref[...].reshape(1, width)
    normed = unit_one*gain_one
    low = normed.astype(bf16)
    for j in range(cuts):
        arrived(wi.at[j], 1+j)
        act, slope = gelu_pair(dot_nn(low, w_in(j)))
        acts[:, j*width:(j+1)*width] = act.astype(bf16)
        slopes[:, j*width:(j+1)*width] = slope.astype(bf16)
    arrived(wb, 1+cuts)
    unit_two, scale_two = centred(normed + dot_nn(acts[...], w_back()))
    out_ref[...] = (unit_two*gain_two).astype(bf16)
    grad_two = norm_back(cot_ref[...].astype(f32)*gain_two, unit_two, scale_two)
    low_two = grad_two.astype(bf16)
    grad = grad_two
    per = shards//cuts
    for j in range(cuts):
        cols = slice(j*width, (j+1)*width)
        pre_grad = dot_nt(low_two, wb[j*per:(j+1)*per].reshape(per*back, width))*slopes[:, cols].astype(f32)
        acts[:, cols] = pre_grad.astype(bf16)
    for j in range(cuts):
        grad = grad + dot_nt(acts[:, j*width:(j+1)*width], w_in(j))
    grad_one = norm_back(grad*gain_one, unit_one, scale_one)
    grad_ref[...] = grad_one
    low_one = grad_one.astype(bf16)
    send_ref[...] = dot_nt(low_one, out_rows(1-mine)).astype(bf16)
    own_ref[...] = dot_nt(low_one, out_rows(mine)).astype(bf16)

def ffn(row, spot, ctx_own, ctx_recv, x, cot, gain_one, gain_two, pieces, before, cuts):
    count, span, width = x.shape
    shards = len(pieces)
    lead = width//shards
    back = cuts*width//shards
    whole = lambda shape: pl.BlockSpec(shape, lambda i, s: (0,)*len(shape))
    at_row = pl.BlockSpec((None, span, width), lambda i, s: (row, 0, 0))
    anywhere = pl.BlockSpec(memory_space=pl.ANY)
    return pl.pallas_call(
        functools.partial(ffn_kernel, shards=shards, cuts=cuts),
        grid_spec=pltpu.PrefetchScalarGridSpec(
            num_scalar_prefetch=1, grid=(1,),
            in_specs=[whole((span, width//2))]*2 + [at_row]*2 + [whole((width,))]*2 + [anywhere]*(shards+len(before)),
            out_specs=[at_row, at_row, whole((span, width//2)), whole((span, width//2))],
            scratch_shapes=[
                pltpu.VMEM((shards, lead, width), bf16),
                pltpu.VMEM((cuts, shards, lead, width), bf16),
                pltpu.VMEM((shards, back, width), bf16),
                pltpu.VMEM((span, cuts*width), bf16),
                pltpu.VMEM((span, cuts*width), bf16),
                pltpu.SemaphoreType.DMA((2+cuts,)),
            ]),
        out_shape=[
            jax.ShapeDtypeStruct((count, span, width), bf16),
            jax.ShapeDtypeStruct((count, span, width), f32),
            jax.ShapeDtypeStruct((span, width//2), bf16),
            jax.ShapeDtypeStruct((span, width//2), bf16),
        ],
        input_output_aliases={7+shards+n: n for n in range(len(before))},
        compiler_params=pltpu.CompilerParams(vmem_limit_bytes=56<<20),
        cost_estimate=pl.CostEstimate(flops=8*span*width*width*(2+4*cuts), bytes_accessed=2*(2+2*cuts)*width*width, transcendentals=2*span*width*cuts),
    )(spot, ctx_own, ctx_recv, x, cot, gain_one, gain_two, *pieces, *before)


def shifted(shard, axis, by):
    count = lax.axis_size(axis)
    return lax.ppermute(shard, axis, [(i, (i + by) % count) for i in range(count)])


def layer_norm(hidden, gain):
    centre = hidden - jnp.mean(hidden, axis=-1, keepdims=True)
    spread = jnp.mean(centre * centre, axis=-1, keepdims=True)
    return centre * lax.rsqrt(spread + 1e-05) * gain


def exact_gelu(values):
    return jax.nn.gelu(values, approximate=False)


def segment_ids(lengths, total):
    place = jnp.arange(total, dtype=jnp.int32)[None, :]
    bounds = jnp.cumsum(lengths, axis=1)
    counted = jnp.zeros((lengths.shape[0], total), jnp.int32)
    for column in range(lengths.shape[1]):
        counted = counted + (place >= bounds[:, column : column + 1]).astype(jnp.int32)
    return counted


def dot_plain(left, right):
    return jnp.dot(left, right, preferred_element_type=jnp.float32)


def dot_trans(left, right):
    return lax.dot_general(
        left, right, (((1,), (1,)), ((), ())), preferred_element_type=jnp.float32
    )


def block_grads(query_h, out_grad, lse_rows, delta_rows, key_h, value_h, allowed):
    scores = (
        jnp.einsum("rqhd,rkhd->rqhk", query_h, key_h, preferred_element_type=jnp.float32) * 0.125
    )
    probs = jnp.where(allowed, jnp.exp(scores - lse_rows[..., None]), 0.0)
    value_grad = jnp.einsum(
        "rqhk,rqhd->rkhd", probs.astype(jnp.bfloat16), out_grad, preferred_element_type=jnp.float32
    )
    prob_grad = jnp.einsum("rqhd,rkhd->rqhk", out_grad, value_h, preferred_element_type=jnp.float32)
    score_grad = (probs * (prob_grad - delta_rows[..., None])).astype(jnp.bfloat16)
    query_grad = (
        jnp.einsum("rqhk,rkhd->rqhd", score_grad, key_h, preferred_element_type=jnp.float32) * 0.125
    )
    key_grad = (
        jnp.einsum("rqhk,rqhd->rkhd", score_grad, query_h, preferred_element_type=jnp.float32)
        * 0.125
    )
    return (query_grad, key_grad, value_grad)


def body_any(
    tokens,
    sent_lengths,
    w_query,
    w_key,
    w_value,
    w_out,
    shared_a,
    shared_b,
    w_in,
    w_back,
    gain_one,
    gain_two,
    scale_dq,
    shift_bq,
    scale_dv,
    shift_bv,
    cotangent,
):
    row_count, span, width = tokens.shape
    head_count = HEADS
    head_size = HEAD_DIM
    blocks = lax.axis_size("blk")
    my_block = lax.axis_index("blk")
    token_count = row_count * span
    token_rows = tokens.reshape(token_count, width)
    seg_full = segment_ids(sent_lengths, span * blocks)
    seg_mine = lax.dynamic_slice_in_dim(seg_full, my_block * span, span, 1)
    w_queries, w_keys, w_values, proj_a, proj_b = (
        lax.all_gather(w_query, "seq", axis=0, tiled=True),
        lax.all_gather(w_key, "seq", axis=0, tiled=True),
        lax.all_gather(w_value, "seq", axis=0, tiled=True),
        lax.all_gather(shared_a, "seq", axis=0, tiled=True),
        lax.all_gather(shared_b, "seq", axis=0, tiled=True),
    )
    projected = dot_plain(token_rows, proj_a).astype(jnp.bfloat16)
    proj_float = projected.astype(jnp.float32)
    lift_q = (proj_float * scale_dq).astype(jnp.bfloat16)
    lift_v = (proj_float * scale_dv).astype(jnp.bfloat16)
    extra_q = dot_plain(lift_q, proj_b)
    extra_v = dot_plain(lift_v, proj_b)
    queries = (dot_plain(token_rows, w_queries) + shift_bq * extra_q).astype(jnp.bfloat16)
    key_rows = dot_plain(token_rows, w_keys).astype(jnp.bfloat16)
    value_rows = (dot_plain(token_rows, w_values) + shift_bv * extra_v).astype(jnp.bfloat16)
    shape4 = (row_count, span, head_count, head_size)
    query_h = queries.reshape(shape4)
    key_h = key_rows.reshape(shape4)
    value_h = value_rows.reshape(shape4)
    start_best = jnp.full((row_count, span, head_count), -1e30, jnp.float32)
    best = start_best
    key_piece = lax.all_gather(key_rows.reshape(row_count, span, width), "blk", axis=1, tiled=True)
    value_piece = lax.all_gather(
        value_rows.reshape(row_count, span, width), "blk", axis=1, tiled=True
    )
    length = key_piece.shape[1]
    key_part = key_piece.reshape(row_count, length, head_count, head_size)
    value_part = value_piece.reshape(row_count, length, head_count, head_size)
    seg_keys = seg_full
    allowed = (seg_mine[:, :, None] == seg_keys[:, None, :])[:, :, None, :]
    scores = (
        jnp.einsum("rqhd,rkhd->rqhk", query_h, key_part, preferred_element_type=jnp.float32) * 0.125
    )
    scores = jnp.where(allowed, scores, -1e30)
    new_best = jnp.maximum(best, jnp.max(scores, axis=-1))
    weight = jnp.where(allowed, jnp.exp(scores - new_best[..., None]), 0.0)
    total = jnp.sum(weight, axis=-1)
    accum = jnp.einsum(
        "rqhk,rkhd->rqhd",
        weight.astype(jnp.bfloat16),
        value_part,
        preferred_element_type=jnp.float32,
    )
    best, total, accum = (new_best, total, accum)
    log_total = best + jnp.log(total)
    context = accum / total[..., None]
    context_b = context.reshape(token_count, width).astype(jnp.bfloat16)
    w_outs, w_ins, w_backs = (
        lax.all_gather(w_out, "seq", axis=0, tiled=True),
        lax.all_gather(w_in, "seq", axis=0, tiled=True),
        lax.all_gather(w_back, "seq", axis=0, tiled=True),
    )

    def norm_first(hidden):
        return layer_norm(hidden, gain_one)

    def norm_second(hidden):
        return layer_norm(hidden, gain_two)

    resid_one = token_rows.astype(jnp.float32) + dot_plain(context_b, w_outs)
    normed_one, norm_one_pull = jax.vjp(norm_first, resid_one)
    pre_act = dot_plain(normed_one.astype(jnp.bfloat16), w_ins)
    act_float, gelu_pull = jax.vjp(exact_gelu, pre_act)
    ffn_part = dot_plain(act_float.astype(jnp.bfloat16), w_backs)
    normed_two, norm_two_pull = jax.vjp(norm_second, normed_one + ffn_part)
    layer_out = normed_two.astype(jnp.bfloat16).reshape(row_count, span, width)
    w_outs, w_ins, w_backs = (
        lax.all_gather(w_out, "seq", axis=0, tiled=True),
        lax.all_gather(w_in, "seq", axis=0, tiled=True),
        lax.all_gather(w_back, "seq", axis=0, tiled=True),
    )
    (grad_two,) = norm_two_pull(cotangent.reshape(token_count, width).astype(jnp.float32))
    act_grad = dot_trans(grad_two.astype(jnp.bfloat16), w_backs)
    (pre_grad,) = gelu_pull(act_grad)
    normed_grad = grad_two + dot_trans(pre_grad.astype(jnp.bfloat16), w_ins)
    (grad_one,) = norm_one_pull(normed_grad)
    context_grad = dot_trans(grad_one.astype(jnp.bfloat16), w_outs).astype(jnp.bfloat16)
    out_grad = context_grad.reshape(shape4)
    delta_rows = jnp.sum(out_grad.astype(jnp.float32) * context, axis=-1)
    zero_grads = jnp.zeros(shape4, jnp.float32)

    def key_step(step, carry):
        key_cur, value_cur, query_acc, key_acc, value_acc = carry
        source = (my_block - step) % blocks
        seg_keys = lax.dynamic_slice_in_dim(seg_full, source * span, span, 1)
        allowed = (seg_mine[:, :, None] == seg_keys[:, None, :])[:, :, None, :]
        q_part, k_part, v_part = block_grads(
            query_h, out_grad, log_total, delta_rows, key_cur, value_cur, allowed
        )
        key_acc, value_acc = (
            shifted((key_acc + k_part).astype(jnp.bfloat16), "blk", 1).astype(jnp.float32),
            shifted((value_acc + v_part).astype(jnp.bfloat16), "blk", 1).astype(jnp.float32),
        )
        key_cur, value_cur = shifted((key_cur, value_cur), "blk", 1)
        return (key_cur, value_cur, query_acc + q_part, key_acc, value_acc)

    looped = lax.fori_loop(
        0, blocks, key_step, (key_h, value_h, zero_grads, zero_grads, zero_grads)
    )
    query_acc, key_acc, value_acc = (looped[2], looped[3], looped[4])
    query_grad = query_acc.reshape(token_count, width).astype(jnp.bfloat16)
    key_grad = key_acc.reshape(token_count, width).astype(jnp.bfloat16)
    value_grad = value_acc.reshape(token_count, width).astype(jnp.bfloat16)
    w_queries, w_keys, w_values, proj_a, proj_b = (
        lax.all_gather(w_query, "seq", axis=0, tiled=True),
        lax.all_gather(w_key, "seq", axis=0, tiled=True),
        lax.all_gather(w_value, "seq", axis=0, tiled=True),
        lax.all_gather(shared_a, "seq", axis=0, tiled=True),
        lax.all_gather(shared_b, "seq", axis=0, tiled=True),
    )
    query_float = query_grad.astype(jnp.float32)
    value_float = value_grad.astype(jnp.float32)
    part_bq = jnp.sum(query_float * extra_q, axis=0)
    part_bv = jnp.sum(value_float * extra_v, axis=0)
    lift_q_grad = dot_trans((query_float * shift_bq).astype(jnp.bfloat16), proj_b)
    lift_v_grad = dot_trans((value_float * shift_bv).astype(jnp.bfloat16), proj_b)
    part_dq = jnp.sum(lift_q_grad * proj_float, axis=0)
    part_dv = jnp.sum(lift_v_grad * proj_float, axis=0)
    proj_grad = (lift_q_grad * scale_dq + lift_v_grad * scale_dv).astype(jnp.bfloat16)
    token_grad = (
        grad_one
        + dot_trans(query_grad, w_queries)
        + dot_trans(key_grad, w_keys)
        + dot_trans(value_grad, w_values)
        + dot_trans(proj_grad, proj_a)
    )
    grad_dq, grad_bq, grad_dv, grad_bv = lax.psum(
        (part_dq, part_bq, part_dv, part_bv), ("seq", "blk")
    )
    return (
        layer_out,
        token_grad.astype(jnp.bfloat16).reshape(row_count, span, width),
        grad_dq,
        grad_bq,
        grad_dv,
        grad_bv,
    )


def swapped(block):
    return lax.ppermute(block, "blk", [(0, 1), (1, 0)])


def summed_groups(vector):
    vector = vector + flipped(vector, 1)
    vector = vector + flipped(vector, 2)
    return (vector + flipped(vector, 4)) + (flipped(vector, 8) + flipped(vector, 12))


def body_two(
    tokens,
    sent_lengths,
    w_query,
    w_key,
    w_value,
    w_out,
    shared_a,
    shared_b,
    w_in,
    w_back,
    gain_one,
    gain_two,
    scale_dq,
    shift_bq,
    scale_dv,
    shift_bv,
    cotangent,
):
    row_count, span, width = tokens.shape
    shards = lax.axis_size("seq")
    heads = HEADS // 2
    part = heads * HEAD_DIM
    wide = 2 * HEAD_DIM
    lead, rank = shared_a.shape
    deep = shared_b.shape[0]
    cuts = w_in.shape[1] // width
    rows = range(row_count)
    spot = jnp.stack([lax.axis_index("blk"), lax.axis_index("seq")]).astype(jnp.int32)

    first, second, vecs = packed(
        spot, shared_a, w_query, w_key, w_value, shared_b, w_out, w_in, w_back,
        (scale_dq, scale_dv, shift_bq, shift_bv), part, wide,
    )
    tie = lax.optimization_barrier

    def core(block):
        return flipped(block, 1)

    other = swapped(tokens)
    lines = [flipped(first, 4), flipped(first, 8), flipped(first, 12)]
    second_over = flipped(second, 2)
    lines, second_over, second = tie((lines, second_over, second))
    quad = jnp.concatenate([first] + lines, axis=0)
    quad_over = flipped(quad, 2)
    quad_core = core(quad)
    far = far_piece(second)
    near = flipped(second, 4)
    quad_over, quad_core, far, near, other = tie((quad_over, quad_core, far, near, other))
    down, lift, weights, merged = merge(
        spot, (quad, quad_core, quad_over, core(quad_over)), vecs, shards, lead, deep, rank, part, wide
    )
    tokens_flat = tokens.reshape(row_count * span, width)
    other_flat = other.reshape(row_count * span, width)
    qkv_own = dot_nn(tokens_flat, weights).astype(bf16)
    qkv_par = dot_nn(other_flat, weights).astype(bf16)
    qkv_own, qkv_par, second, second_over, far, near = tie((qkv_own, qkv_par, second, second_over, far, near))
    last = swapped(far)
    far_over = flipped(far, 2)
    near_over = flipped(second_over, 4)
    second_core, second_over_core = core(second), core(second_over)
    seen = [attend(0, spot, sent_lengths, qkv_own, qkv_par, heads, HEAD_DIM)]
    seen[0], last, far_over, near_over, second_core, second_over_core, qkv_own, qkv_par, near, far = tie(
        (seen[0], last, far_over, near_over, second_core, second_over_core, qkv_own, qkv_par, near, far)
    )
    ctx_recv = [swapped(seen[0][1])]
    last_over = flipped(last, 2)
    near_core, far_core, near_over_core = core(near), core(far), core(near_over)
    seen.append(attend(1, spot, sent_lengths, qkv_own, qkv_par, heads, HEAD_DIM))
    seen[1], ctx_recv[0], last_over, near_core, far_core, near_over_core, far_over, last = tie(
        (seen[1], ctx_recv[0], last_over, near_core, far_core, near_over_core, far_over, last)
    )
    ctx_recv.append(swapped(seen[1][1]))
    pack = [second, second_core, second_over, second_over_core, near, near_core, near_over, near_over_core]
    pack += [far, far_core, far_over, core(far_over), last, core(last), last_over, core(last_over)]
    fed = []
    for row in rows:
        before = fed[-1][:2] if fed else []
        fed.append(
            ffn(row, spot, seen[row][0], ctx_recv[row], tokens, cotangent, gain_one, gain_two, pack, before, cuts)
        )
    layer_out, grad_one = fed[-1][:2]
    grad_recv = [swapped(fed[row][3]) for row in rows]
    sent = []
    grads = []
    for row in rows:
        grads = attend_back(
            row, spot, sent_lengths, qkv_own, qkv_par, seen[row][0], seen[row][1],
            fed[row][2], grad_recv[row], seen[row][2], grads, heads, HEAD_DIM,
        )
        partial = dot_nt(grads[1][row * span : (row + 1) * span], weights).astype(bf16)
        if sent:
            grads, partial, sent[-1] = lax.optimization_barrier((grads, partial, sent[-1]))
        grads, partial = lax.optimization_barrier((grads, partial))
        sent.append(swapped(partial))

    def outer(left, right):
        return lax.dot_general(left, right, (((0,), (0,)), ((), ())), preferred_element_type=f32)

    moment = outer(tokens_flat, grads[0]) + outer(other_flat, grads[1])
    flat = summed_groups(trained(spot, moment, merged, down, lift, vecs, wide))
    base = grad_one.reshape(row_count * span, width) + dot_nt(grads[0], weights)
    token_grad = []
    for row in rows[:-1]:
        token_grad = [finish(row, row_count, base, sent[row], token_grad)]
    flat, sent[-1], token_grad = lax.optimization_barrier((flat, sent[-1], token_grad))
    flat = (flat + swapped(flat)).reshape(-1)
    token_grad = finish(row_count - 1, row_count, base, sent[-1], token_grad)
    return (
        layer_out,
        token_grad,
        flat[:rank],
        flat[rank : rank + width],
        flat[rank + width : 2 * rank + width],
        flat[2 * rank + width :],
    )


def solution(mesh):
    return jax.shard_map(
        body_two if mesh.shape["blk"] == 2 and mesh.shape["seq"] == 16 else body_any,
        mesh=mesh,
        in_specs=(
            P("seq", "blk", None),
            P("seq", None),
            P("seq", None),
            P("seq", None),
            P("seq", None),
            P("seq", None),
            P("seq", None),
            P("seq", None),
            P("seq", None),
            P("seq", None),
            P(),
            P(),
            P(),
            P(),
            P(),
            P(),
            P("seq", "blk", None),
        ),
        out_specs=(P("seq", "blk", None), P("seq", "blk", None), P(), P(), P(), P()),
        check_vma=False,
    )
```

```python
import functools

import jax
import jax.numpy as jnp
from jax import lax
from jax.experimental import pallas as pl
from jax.experimental.pallas import tpu as pltpu
from jax.sharding import PartitionSpec as P

HEADS = 12
HEAD_DIM = 64
bf16 = jnp.bfloat16
f32 = jnp.float32


LN2 = 0.6931471805599453
LOG2E = 1.4426950408889634
SEGS = 5
PARTS = 3
TILE = 256
STEP = 128

def dot_nt(a,b): return lax.dot_general(a,b,(((1,),(1,)),((),())),preferred_element_type=f32)
def dot_nn(a,b): return jnp.dot(a,b,preferred_element_type=f32)

def lane_row(test, wide, kind=f32):
    lane = lax.broadcasted_iota(jnp.int32, (1, wide), 1)
    return jnp.where(test(lane), 1.0, 0.0).astype(kind)

def part_rows(wide, start):
    return [lane_row(lambda l: l == start + n, wide) for n in range(PARTS)]

def spread(column, rows):
    top = column.astype(bf16).astype(f32)
    return (top*rows[0] + (column-top)*rows[1]).astype(bf16)

def cross_ones(wide, hd):
    a = lax.broadcasted_iota(jnp.int32, (wide, wide), 0) < hd
    b = lax.broadcasted_iota(jnp.int32, (wide, wide), 1) < hd
    return jnp.where(a != b, 1.0, 0.0).astype(bf16)

def side_rows(wide, hd):
    return [lane_row(lambda l: l < hd, wide, bf16), lane_row(lambda l: l >= hd, wide, bf16)]

def bounds_of(lens, row):
    bounds = [lens[row, 0]]
    for n in range(1, SEGS-1):
        bounds.append(bounds[-1] + lens[row, n])
    return bounds

def key_span(bounds, i, span):
    low = 0
    for bound in bounds:
        low = jnp.where(bound <= i*TILE, bound, low)
    high = span
    for bound in reversed(bounds):
        high = jnp.where(bound > i*TILE + TILE-1, bound, high)
    begin = lax.div(low, STEP)
    count = lax.div(high - begin*STEP + TILE-1, TILE)
    return jnp.minimum(begin, lax.div(span - count*TILE, STEP)), count

def marks(bounds, span, wide, hd, side):
    place = lax.broadcasted_iota(jnp.int32, (span, wide), 0)
    lane = lax.broadcasted_iota(jnp.int32, (span, wide), 1) - (hd if side == 0 else 0)
    lane = jnp.where((lane >= 0) & (lane < hd), lane, hd)
    seg = jnp.zeros((span, wide), jnp.int32)
    for bound in bounds:
        seg = seg + jnp.where(place >= bound, 1, 0)
    asked = jnp.where((lane < SEGS) & (lane != seg), 1.0, 0.0).astype(bf16)
    held = jnp.where(lane == seg, -1e30, jnp.where((lane >= SEGS) & (lane < SEGS+PARTS), 1.0, 0.0)).astype(bf16)
    return asked, held

def by_half(mine, work):
    for n in range(2):
        @pl.when(mine == n)
        def _():
            work(n)

def query_tiles(bounds, span, work, broad):
    tiles = span//TILE
    fewest = tiles
    for i in range(tiles):
        fewest = jnp.minimum(fewest, key_span(bounds, i, span)[1])
    @pl.when(fewest == tiles)
    def _():
        def one(i, carry):
            work(pl.ds(pl.multiple_of(i*broad, broad), broad), slice(0, span))
            return carry
        lax.fori_loop(0, span//broad, one, 0)
    @pl.when(fewest < tiles)
    def _():
        def one(i, carry):
            rows = pl.ds(pl.multiple_of(i*TILE, TILE), TILE)
            begin, count = key_span(bounds, i, span)
            start = pl.multiple_of(begin*STEP, STEP)
            for n in range(1, tiles+1):
                @pl.when(count == n)
                def _():
                    work(rows, pl.ds(start, n*TILE) if n < tiles else slice(0, span))
            return carry
        lax.fori_loop(0, tiles, one, 0)

def attend_kernel(spot, lens, xo_ref, xp_ref, own_ref, par_ref, qa_ref, qf, kf, ka, va, og, outs, *, hd, row):
    half = xo_ref.shape[0]
    bounds = bounds_of(lens, row)
    span = 2*half
    wide = 2*hd
    sides = side_rows(wide, hd)
    swap = cross_ones(wide, hd)
    first = lax.broadcasted_iota(jnp.int32, (span, wide), 1) < hd
    start = [hd+SEGS, SEGS]
    parts = [part_rows(wide, start[s]) for s in range(2)]
    @pl.when(pl.program_id(0) == 0)
    def _():
        for s in range(2):
            qf[s], kf[s] = marks(bounds, span, wide, hd, s)
    longest = None
    for x_ref in (xo_ref, xp_ref):
        kp = x_ref[:, wide:2*wide]
        norms = jnp.max(dot_nn(kp*kp, swap), axis=0, keepdims=True)
        longest = norms if longest is None else jnp.maximum(longest, norms)
    def place(n):
        for x_ref, at in ((xo_ref, n), (xp_ref, 1-n)):
            rows = slice(at*half, (at+1)*half)
            qp = x_ref[:, 0:wide]
            kp = x_ref[:, wide:2*wide]
            vp = x_ref[:, 2*wide:3*wide]
            top = jnp.sqrt(dot_nn(qp*qp, swap) * longest) * 1.02
            for s in range(2):
                qa_ref[s, rows, :] = qp*sides[s] + (qf[s, rows, :] - (top*parts[s][0]).astype(bf16))
                ka[s, rows, :] = kp*sides[s] + kf[s, rows, :]
                va[s, rows, :] = vp*sides[s] + sides[1-s]
    by_half(spot[0], place)
    def weigh(rows, keys):
        for s in range(2):
            w = jnp.exp2(dot_nt(qa_ref[s, rows, :], ka[s, keys, :])).astype(bf16)
            og[s, rows, :] = dot_nn(w, va[s, keys, :])
    query_tiles(bounds, span, weigh, 512)
    @pl.when(jnp.logical_not(jnp.min(jnp.where(first, og[1], og[0])) > 2.0**-80))
    def _():
        def exact_tile(i, carry):
            rows = pl.ds(pl.multiple_of(i*TILE, TILE), TILE)
            for s in range(2):
                plain = qa_ref[s, rows, :] * (1.0 - parts[s][0]).astype(bf16)
                m = jnp.max(dot_nt(plain, ka[s]), axis=1, keepdims=True)
                qa_ref[s, rows, :] = plain - (jnp.broadcast_to(m, (TILE, wide))*parts[s][0]).astype(bf16)
            weigh(rows, slice(0, span))
            return carry
        lax.fori_loop(0, span//TILE, exact_tile, 0)
    total = jnp.where(first, og[1], og[0])
    outs[...] = (jnp.where(first, og[0], og[1]) / pltpu.roll(total, hd, 1)).astype(bf16)
    lse = -jnp.log2(total)
    for s in range(2):
        qa_ref[s] = qa_ref[s] + spread(lse, parts[s][1:])
    def leave(n):
        own_ref[...] = outs[n*half:(n+1)*half, :]
        par_ref[...] = outs[(1-n)*half:(2-n)*half, :]
    by_half(spot[0], leave)

def attend(row, spot, lens, qkv, heads, hd):
    count = lens.shape[0]
    half = qkv.shape[0]//(2*count); span = 2*half; mine = heads*hd; wide = 2*hd
    col = lambda p, s, l: (0, p)
    return pl.pallas_call(
        functools.partial(attend_kernel, hd=hd, row=row),
        grid_spec=pltpu.PrefetchScalarGridSpec(
            num_scalar_prefetch=2, grid=(heads//2,),
            in_specs=[pl.BlockSpec((half, 3*wide), lambda p, s, l: (row, p)), pl.BlockSpec((half, 3*wide), lambda p, s, l: (count+row, p))],
            out_specs=[
                pl.BlockSpec((half, wide), col),
                pl.BlockSpec((half, wide), col),
                pl.BlockSpec((2, span, wide), lambda p, s, l: (p, 0, 0)),
            ],
            scratch_shapes=[
                pltpu.VMEM((2, span, wide), bf16),
                pltpu.VMEM((2, span, wide), bf16),
                pltpu.VMEM((2, span, wide), bf16),
                pltpu.VMEM((2, span, wide), bf16),
                pltpu.VMEM((2, span, wide), f32),
                pltpu.VMEM((span, wide), bf16),
            ]),
        out_shape=[
            jax.ShapeDtypeStruct((half, mine), bf16),
            jax.ShapeDtypeStruct((half, mine), bf16),
            jax.ShapeDtypeStruct((heads, span, wide), bf16),
        ],
        compiler_params=pltpu.CompilerParams(vmem_limit_bytes=32<<20),
        cost_estimate=pl.CostEstimate(flops=16*span*span*mine, bytes_accessed=span*mine*12, transcendentals=span*span*heads),
    )(spot, lens, qkv, qkv)

def attend_back_kernel(spot, lens, xo_ref, xp_ref, co_ref, cp_ref, go_ref, gp_ref, qa_ref, *refs, hd, row):
    out_ref, kf, ka, va, ga, kt, kacc, vacc, qacc = refs[-9:]
    half = xo_ref.shape[0]
    bounds = bounds_of(lens, row)
    span = 2*half
    wide = 2*hd
    sides = side_rows(wide, hd)
    low = [lane_row(lambda l: (l >= hd) & (l < hd+PARTS), wide, bf16), lane_row(lambda l: l < PARTS, wide, bf16)]
    parts = [part_rows(wide, hd), part_rows(wide, 0)]
    swap = cross_ones(wide, hd)
    first = lax.broadcasted_iota(jnp.int32, (half, wide), 1) < hd
    @pl.when(pl.program_id(0) == 0)
    def _():
        for s in range(2):
            kf[s] = marks(bounds, span, wide, hd, s)[1]
    def place(n):
        for x_ref, c_ref, g_ref, at in ((xo_ref, co_ref, go_ref, n), (xp_ref, cp_ref, gp_ref, 1-n)):
            rows = slice(at*half, (at+1)*half)
            kp = x_ref[:, wide:2*wide]
            vp = x_ref[:, 2*wide:3*wide]
            gp = g_ref[...]
            kt[:, rows] = kp.T
            prod = gp.astype(f32) * c_ref[...].astype(f32)
            top = prod.astype(bf16)
            delta = dot_nn(top, swap) + dot_nn((prod - top.astype(f32)).astype(bf16), swap)
            for s in range(2):
                ka[s, rows, :] = kp*sides[s] + kf[s, rows, :]
                va[s, rows, :] = vp*sides[s] + low[s]
                ga[s, rows, :] = gp*sides[s] + spread(-delta, parts[s])
    by_half(spot[0], place)
    kacc[...] = jnp.zeros_like(kacc)
    vacc[...] = jnp.zeros_like(vacc)
    def work(rows, keys):
        for s in range(2):
            qq = qa_ref[s, rows, :]
            gg = ga[s, rows, :]
            probs = jnp.exp2(dot_nt(ka[s, keys, :], qq))
            slope = (probs * dot_nt(va[s, keys, :], gg)).astype(bf16)
            vacc[s, keys, :] += dot_nn(probs.astype(bf16), gg)
            kacc[s, keys, :] += dot_nn(slope, qq)
            qacc[s*hd:(s+1)*hd, rows] = dot_nn(kt[s*hd:(s+1)*hd, keys], slope)
    query_tiles(bounds, span, work, TILE)
    def leave(n):
        for part, at in ((0, n), (1, 1-n)):
            rows = slice(at*half, (at+1)*half)
            out_ref[part, :, 0:wide] = (qacc[:, rows].T * LN2).astype(bf16)
            out_ref[part, :, wide:2*wide] = (jnp.where(first, kacc[0, rows, :], kacc[1, rows, :]) * LN2).astype(bf16)
            out_ref[part, :, 2*wide:3*wide] = jnp.where(first, vacc[0, rows, :], vacc[1, rows, :]).astype(bf16)
    by_half(spot[0], leave)

def attend_back(row, spot, lens, qkv, ctx_own, ctx_par, g_own, g_par, qa, before, heads, hd):
    count = lens.shape[0]
    half = qkv.shape[0]//(2*count); span = 2*half; mine = heads*hd; wide = 2*hd
    col = lambda p, s, l: (0, p)
    at_row = lambda p, s, l: (row, p)
    return pl.pallas_call(
        functools.partial(attend_back_kernel, hd=hd, row=row),
        grid_spec=pltpu.PrefetchScalarGridSpec(
            num_scalar_prefetch=2, grid=(heads//2,),
            in_specs=[pl.BlockSpec((half, 3*wide), at_row), pl.BlockSpec((half, 3*wide), lambda p, s, l: (count+row, p))] + [pl.BlockSpec((half, wide), col)]*4
            + [pl.BlockSpec((2, span, wide), lambda p, s, l: (p, 0, 0))] + [pl.BlockSpec(memory_space=pl.ANY)]*len(before),
            out_specs=pl.BlockSpec((2, half, 3*wide), lambda p, s, l: (0, row, p)),
            scratch_shapes=[
                pltpu.VMEM((2, span, wide), bf16),
                pltpu.VMEM((2, span, wide), bf16),
                pltpu.VMEM((2, span, wide), bf16),
                pltpu.VMEM((2, span, wide), bf16),
                pltpu.VMEM((wide, span), bf16),
                pltpu.VMEM((2, span, wide), f32),
                pltpu.VMEM((2, span, wide), f32),
                pltpu.VMEM((wide, span), f32),
            ]),
        out_shape=jax.ShapeDtypeStruct((2, count*half, 3*mine), bf16),
        input_output_aliases={9+n: n for n in range(len(before))},
        compiler_params=pltpu.CompilerParams(vmem_limit_bytes=40<<20),
        cost_estimate=pl.CostEstimate(flops=40*span*span*mine, bytes_accessed=span*mine*20, transcendentals=span*span*heads),
    )(spot, lens, qkv, qkv, ctx_own, ctx_par, g_own, g_par, qa, *before)


def pack_kernel(place, a_ref, q_ref, k_ref, v_ref, b_ref, out_ref, in_ref, back_ref, *refs, wide):
    vectors, (first_ref, second_ref, vecs) = refs[:-3], refs[-3:]
    vecs[...] = jnp.zeros_like(vecs)
    for n, ref in enumerate(vectors):
        vecs[n : n + 1, : ref.shape[0]] = ref[...].reshape(1, ref.shape[0])
    lead = a_ref.shape[0]
    width = out_ref.shape[1]
    row = 0
    pieces = [a_ref[:, at : at + wide] for at in range(0, a_ref.shape[1], wide)]
    for at in range(0, q_ref.shape[1], wide):
        pieces += [ref[:, at : at + wide] for ref in (q_ref, k_ref, v_ref)]
    pieces += [b_ref[:, at : at + wide] for at in range(0, b_ref.shape[1], wide)]
    for piece in pieces:
        first_ref[row : row + piece.shape[0], :] = piece
        row += piece.shape[0]
    row = 0
    pieces = [out_ref[...]]
    pieces += [in_ref[:, at : at + width] for at in range(0, in_ref.shape[1], width)]
    pieces += [back_ref[...]]
    for piece in pieces:
        second_ref[row : row + piece.shape[0], :] = piece
        row += piece.shape[0]


def packed(place, shared_a, w_query, w_key, w_value, shared_b, w_out, w_in, w_back, vectors, part, wide):
    lead, rank = shared_a.shape
    width = w_out.shape[1]
    rows = lead * (rank + 3 * part) // wide + shared_b.shape[0] * part // wide
    whole = lambda array: pl.BlockSpec(array.shape, lambda i, s: (0, 0))
    half = lambda array: pl.BlockSpec((array.shape[0], part), lambda i, s: (0, s[0]))
    total = lead + lead * w_in.shape[1] // width + w_back.shape[0]
    return pl.pallas_call(
        functools.partial(pack_kernel, wide=wide),
        grid_spec=pltpu.PrefetchScalarGridSpec(
            num_scalar_prefetch=1,
            grid=(1,),
            in_specs=[whole(shared_a), half(w_query), half(w_key), half(w_value), half(shared_b), whole(w_out), whole(w_in), whole(w_back)]
            + [pl.BlockSpec(vector.shape, lambda i, s: (0,)) for vector in vectors],
            out_specs=[pl.BlockSpec((rows, wide), lambda i, s: (0, 0)), pl.BlockSpec((total, width), lambda i, s: (0, 0)), pl.BlockSpec((8, rank), lambda i, s: (0, 0))],
        ),
        out_shape=[jax.ShapeDtypeStruct((rows, wide), bf16), jax.ShapeDtypeStruct((total, width), bf16), jax.ShapeDtypeStruct((8, rank), f32)],
        compiler_params=pltpu.CompilerParams(vmem_limit_bytes=60 << 20),
    )(place, shared_a, w_query, w_key, w_value, shared_b, w_out, w_in, w_back, *vectors)


def bent(vecs, at, side, part):
    row = vecs[at : at + 1, : 2 * part]
    return jnp.where(side == 0, row[:, :part], row[:, part:])


def merge_kernel(spot, *refs, shards, rank, part, wide):
    quads = refs[:4]
    vecs, down, lift, weights, merged, mixed = refs[4:]
    each = quads[0].shape[0] // 4
    lead = down.shape[1]
    deep = lift.shape[1]
    pairs = part // wide
    for j in range(shards):
        at = spot[1] ^ j
        piece = quads[j % 4]
        row = each * (j // 4)
        for n in range(rank // wide):
            down[at, :, n * wide : (n + 1) * wide] = piece[row : row + lead, :]
            row += lead
        for n in range(3 * pairs):
            mixed[at, :, n * wide : (n + 1) * wide] = piece[row : row + lead, :]
            row += lead
        for n in range(pairs):
            lift[at, :, n * wide : (n + 1) * wide] = piece[row : row + deep, :]
            row += deep
    low = down[...].reshape(shards * lead, rank)
    high = lift[...].reshape(shards * deep, part)
    delta_q = dot_nn(low * vecs[0:1, :].astype(bf16), high)
    merged[:, :part] = delta_q.astype(bf16)
    delta_q = delta_q * bent(vecs, 2, spot[0], part)
    delta_v = dot_nn(low * vecs[1:2, :].astype(bf16), high)
    merged[:, part:] = delta_v.astype(bf16)
    delta_v = delta_v * bent(vecs, 3, spot[0], part)
    for n in range(pairs):
        cols = slice(n * wide, (n + 1) * wide)
        base = 3 * n * wide
        get = lambda s: mixed[:, :, base + s * wide : base + (s + 1) * wide].reshape(shards * lead, wide)
        weights[:, base : base + wide] = ((get(0).astype(f32) + delta_q[:, cols]) * (0.125 * LOG2E)).astype(bf16)
        weights[:, base + wide : base + 2 * wide] = get(1)
        weights[:, base + 2 * wide : base + 3 * wide] = (get(2).astype(f32) + delta_v[:, cols]).astype(bf16)


def merge(spot, quads, vecs, shards, lead, deep, rank, part, wide):
    width = shards * lead
    whole = lambda shape: pl.BlockSpec(shape, lambda i, s: (0,) * len(shape))
    return pl.pallas_call(
        functools.partial(merge_kernel, shards=shards, rank=rank, part=part, wide=wide),
        grid_spec=pltpu.PrefetchScalarGridSpec(
            num_scalar_prefetch=1,
            grid=(1,),
            in_specs=[whole(quads[0].shape)] * 4 + [whole(vecs.shape)],
            out_specs=[whole((shards, lead, rank)), whole((shards, deep, part)), whole((width, 3 * part)), whole((width, 2 * part))],
            scratch_shapes=[pltpu.VMEM((shards, lead, 3 * part), bf16)],
        ),
        out_shape=[
            jax.ShapeDtypeStruct((shards, lead, rank), bf16),
            jax.ShapeDtypeStruct((shards, deep, part), bf16),
            jax.ShapeDtypeStruct((width, 3 * part), bf16),
            jax.ShapeDtypeStruct((width, 2 * part), bf16),
        ],
        compiler_params=pltpu.CompilerParams(vmem_limit_bytes=40 << 20),
        cost_estimate=pl.CostEstimate(flops=40 * width * rank * part, bytes_accessed=1 << 20, transcendentals=0),
    )(spot, *quads, vecs)


def flipped(block, mask):
    count = lax.axis_size("seq")
    return lax.ppermute(block, "seq", [(i, i ^ mask) for i in range(count)])


def far_piece(piece):
    count = lax.axis_size("seq")
    pairs = [(2 * i + b, 2 * (i ^ (8 + 4 * b)) + b) for i in range(count) for b in range(2)]
    return lax.ppermute(piece, ("seq", "blk"), pairs)


def spread_square(block):
    across = flipped(block, 2)
    return [block, flipped(block, 1), across, flipped(across, 1)]


def trained_kernel(
    spot, turned_ref, grad_ref, vecs, merged_hbm, down_hbm, lift_hbm, out_ref, moment, merged_ref, down_ref, lift_ref, sems,
    *, wide
):
    held = ((merged_hbm, merged_ref), (down_hbm, down_ref), (lift_hbm, lift_ref))
    lead = down_ref.shape[1]
    width = down_ref.shape[0] * lead
    rank = down_ref.shape[2]
    part = lift_ref.shape[2]
    pairs = part // wide
    picked = [grad_ref[:, (3 * n + s) * wide : (3 * n + s + 1) * wide] for s in (0, 2) for n in range(pairs)]
    added = dot_nn(turned_ref[...], jnp.concatenate(picked, axis=1))
    @pl.when(pl.program_id(0) == 0)
    def _():
        for n, (source, target) in enumerate(held):
            pltpu.make_async_copy(source, target, sems.at[n]).start()
        moment[...] = added
    @pl.when(pl.program_id(0) > 0)
    def _():
        moment[...] += added
    @pl.when(pl.program_id(0) == pl.num_programs(0) - 1)
    def _():
        for n, (source, target) in enumerate(held):
            pltpu.make_async_copy(source, target, sems.at[n]).wait()
        down = down_ref[...].reshape(width, rank).astype(f32)
        lift = lift_ref[...].reshape(rank, part)
        out_ref[...] = jnp.zeros_like(out_ref)
        base = 0
        for s, coef in ((0, 0.125 * LOG2E), (1, 1.0)):
            cols = slice(s * part, (s + 1) * part)
            shift = jnp.sum(merged_ref[:, cols].astype(f32) * moment[:, cols], axis=0, keepdims=True) * coef
            bend = bent(vecs, 2 + s, spot[0], part) * coef
            bent_moment = (moment[:, cols] * bend).astype(bf16)
            scale = jnp.sum(down * dot_nt(bent_moment, lift), axis=0, keepdims=True)
            for n in range(rank // wide):
                out_ref[base + n : base + n + 1, :] = scale[:, n * wide : (n + 1) * wide]
            base += rank // wide
            for n in range(pairs):
                out_ref[pl.ds(base + pairs * spot[0] + n, 1), :] = shift[:, n * wide : (n + 1) * wide]
            base += 2 * pairs


def trained(spot, turned, grads, merged, down, lift, vecs, wide):
    rank, part = down.shape[2], lift.shape[2]
    width, total = turned.shape
    step = total // 4
    whole = lambda array: pl.BlockSpec(array.shape, lambda i, s: (0,) * array.ndim)
    rows = 2 * (rank + 2 * part) // wide
    return pl.pallas_call(
        functools.partial(trained_kernel, wide=wide),
        grid_spec=pltpu.PrefetchScalarGridSpec(
            num_scalar_prefetch=1,
            grid=(4,),
            in_specs=[
                pl.BlockSpec((width, step), lambda i, s: (0, i)),
                pl.BlockSpec((step, grads.shape[1]), lambda i, s: (i, 0)),
            ]
            + [whole(vecs)] + [pl.BlockSpec(memory_space=pl.ANY)] * 3,
            out_specs=pl.BlockSpec((rows, wide), lambda i, s: (0, 0)),
            scratch_shapes=[pltpu.VMEM((width, 2 * part), f32)]
            + [pltpu.VMEM(array.shape, bf16) for array in (merged, down, lift)] + [pltpu.SemaphoreType.DMA((3,))],
        ),
        out_shape=jax.ShapeDtypeStruct((rows, wide), f32),
        compiler_params=pltpu.CompilerParams(vmem_limit_bytes=60 << 20),
        cost_estimate=pl.CostEstimate(flops=8 * width * total * part, bytes_accessed=12 << 20, transcendentals=0),
    )(spot, turned, grads, vecs, merged, down, lift)


def finish_kernel(base_ref, *refs, parts):
    out_ref = refs[-1]
    each = refs[0].shape[0]
    for n in range(parts):
        rows = slice(n * each, (n + 1) * each)
        out_ref[rows, :] = (base_ref[rows, :].astype(f32) + refs[n][...].astype(f32)).astype(bf16)


def finish(row, count, base, sent, before):
    each, width = sent[0].shape
    span = each * len(sent)
    return pl.pallas_call(
        functools.partial(finish_kernel, parts=len(sent)),
        grid=(1,),
        in_specs=[pl.BlockSpec((span, width), lambda i: (row, 0))]
        + [pl.BlockSpec((each, width), lambda i: (0, 0))] * len(sent)
        + [pl.BlockSpec(memory_space=pl.ANY)] * len(before),
        out_specs=pl.BlockSpec((None, span, width), lambda i: (row, 0, 0)),
        out_shape=jax.ShapeDtypeStruct((count, span, width), bf16),
        input_output_aliases={1 + len(sent) + n: n for n in range(len(before))},
        compiler_params=pltpu.CompilerParams(vmem_limit_bytes=60 << 20),
    )(base, *sent, *before)


def centred(hidden):
    off = hidden - jnp.mean(hidden, axis=-1, keepdims=True)
    scale = lax.rsqrt(jnp.mean(off*off, axis=-1, keepdims=True) + 1e-05)
    return off*scale, scale

def norm_back(grad, unit, scale):
    inner = jnp.mean(grad*unit, axis=-1, keepdims=True)
    return scale*(grad - jnp.mean(grad, axis=-1, keepdims=True) - unit*inner)

def gelu_pair(x):
    size = jnp.abs(x)
    base = 1.0 + size*(0.3275911*0.7071067811865476)
    t = pl.reciprocal(base, approx=True)
    t = t*(2.0 - base*t)
    bell = jnp.exp2(x*x*(-0.7213475204444817))
    tail = t*(0.127414796 + t*(-0.142248368 + t*(0.7107068705 + t*(-0.7265760135 + t*0.5307027145))))*bell
    below = jnp.where(x < 0, tail, 1.0 - tail)
    return x*below, below + x*(bell*0.3989422804014327)

def ffn_kernel(spot, co_ref, cr_ref, x_ref, cot_ref, g1_ref, g2_ref, *refs, shards, cuts):
    pieces = refs[:shards]
    out_ref, grad_ref, own_ref, send_ref, wo, wi, wb, slopes, sems = refs[-9:]
    width = x_ref.shape[1]
    lead = wo.shape[1]
    back = wb.shape[1]
    mine = spot[0]
    groups = [0, 4, 8 + 4*mine, 12 - 4*mine]
    ats = [spot[1] ^ (groups[j//4] + j%4) for j in range(shards)]
    for j in range(shards):
        pltpu.make_async_copy(pieces[j].at[0:lead, :], wo.at[ats[j]], sems.at[0]).start()
    for n in range(cuts):
        for j in range(shards):
            rows = slice(lead*(1+n), lead*(2+n))
            pltpu.make_async_copy(pieces[j].at[rows, :], wi.at[n, ats[j]], sems.at[1+n]).start()
    for j in range(shards):
        rows = slice(lead*(1+cuts), lead*(1+cuts)+back)
        pltpu.make_async_copy(pieces[j].at[rows, :], wb.at[ats[j]], sems.at[1+cuts]).start()
    def arrived(held, n):
        pltpu.make_async_copy(held, held, sems.at[n]).wait()
    part = shards//2
    half = width//2
    def out_rows(who):
        return wo[pl.ds(pl.multiple_of(who*part, part), part)].reshape(half, width)
    def w_in(j): return wi[j].reshape(width, width)
    per = shards//cuts
    def w_back(j): return wb[j*per:(j+1)*per].reshape(per*back, width)
    arrived(wo, 0)
    resid = x_ref[...].astype(f32) + dot_nn(co_ref[...], out_rows(mine)) + dot_nn(cr_ref[...], out_rows(1-mine))
    unit_one, scale_one = centred(resid)
    gain_one = g1_ref[...].reshape(1, width)
    gain_two = g2_ref[...].reshape(1, width)
    normed = unit_one*gain_one
    low = normed.astype(bf16)
    total = normed
    for j in range(cuts):
        arrived(wi.at[j], 1+j)
        act, slope = gelu_pair(dot_nn(low, w_in(j)))
        slopes[j] = slope.astype(bf16)
        if j == 0:
            arrived(wb, 1+cuts)
        total = total + dot_nn(act.astype(bf16), w_back(j))
    unit_two, scale_two = centred(total)
    out_ref[...] = (unit_two*gain_two).astype(bf16)
    grad_two = norm_back(cot_ref[...].astype(f32)*gain_two, unit_two, scale_two)
    low_two = grad_two.astype(bf16)
    grad = grad_two
    for j in range(cuts):
        pre_grad = (dot_nt(low_two, w_back(j))*slopes[j].astype(f32)).astype(bf16)
        grad = grad + dot_nt(pre_grad, w_in(j))
    grad_one = norm_back(grad*gain_one, unit_one, scale_one)
    low_one = grad_one.astype(bf16)
    grad_ref[...] = low_one
    send_ref[...] = dot_nt(low_one, out_rows(1-mine)).astype(bf16)
    own_ref[...] = dot_nt(low_one, out_rows(mine)).astype(bf16)

def ffn(row, spot, ctx_own, ctx_recv, x, cot, gain_one, gain_two, pieces, before, cuts):
    count, span, width = x.shape
    shards = len(pieces)
    lead = width//shards
    back = cuts*width//shards
    whole = lambda shape: pl.BlockSpec(shape, lambda i, s: (0,)*len(shape))
    at_row = pl.BlockSpec((None, span, width), lambda i, s: (row, 0, 0))
    anywhere = pl.BlockSpec(memory_space=pl.ANY)
    return pl.pallas_call(
        functools.partial(ffn_kernel, shards=shards, cuts=cuts),
        grid_spec=pltpu.PrefetchScalarGridSpec(
            num_scalar_prefetch=1, grid=(1,),
            in_specs=[whole((span, width//2))]*2 + [at_row]*2 + [whole((width,))]*2 + [anywhere]*(shards+len(before)),
            out_specs=[at_row, at_row, whole((span, width//2)), whole((span, width//2))],
            scratch_shapes=[
                pltpu.VMEM((shards, lead, width), bf16),
                pltpu.VMEM((cuts, shards, lead, width), bf16),
                pltpu.VMEM((shards, back, width), bf16),
                pltpu.VMEM((cuts, span, width), bf16),
                pltpu.SemaphoreType.DMA((2+cuts,)),
            ]),
        out_shape=[
            jax.ShapeDtypeStruct((count, span, width), bf16),
            jax.ShapeDtypeStruct((count, span, width), bf16),
            jax.ShapeDtypeStruct((span, width//2), bf16),
            jax.ShapeDtypeStruct((span, width//2), bf16),
        ],
        input_output_aliases={7+shards+n: n for n in range(len(before))},
        compiler_params=pltpu.CompilerParams(vmem_limit_bytes=56<<20),
        cost_estimate=pl.CostEstimate(flops=8*span*width*width*(2+4*cuts), bytes_accessed=2*(2+2*cuts)*width*width, transcendentals=2*span*width*cuts),
    )(spot, ctx_own, ctx_recv, x, cot, gain_one, gain_two, *pieces, *before)


def shifted(shard, axis, by):
    count = lax.axis_size(axis)
    return lax.ppermute(shard, axis, [(i, (i + by) % count) for i in range(count)])


def layer_norm(hidden, gain):
    centre = hidden - jnp.mean(hidden, axis=-1, keepdims=True)
    spread = jnp.mean(centre * centre, axis=-1, keepdims=True)
    return centre * lax.rsqrt(spread + 1e-05) * gain


def exact_gelu(values):
    return jax.nn.gelu(values, approximate=False)


def segment_ids(lengths, total):
    place = jnp.arange(total, dtype=jnp.int32)[None, :]
    bounds = jnp.cumsum(lengths, axis=1)
    counted = jnp.zeros((lengths.shape[0], total), jnp.int32)
    for column in range(lengths.shape[1]):
        counted = counted + (place >= bounds[:, column : column + 1]).astype(jnp.int32)
    return counted


def dot_plain(left, right):
    return jnp.dot(left, right, preferred_element_type=jnp.float32)


def dot_trans(left, right):
    return lax.dot_general(
        left, right, (((1,), (1,)), ((), ())), preferred_element_type=jnp.float32
    )


def block_grads(query_h, out_grad, lse_rows, delta_rows, key_h, value_h, allowed):
    scores = (
        jnp.einsum("rqhd,rkhd->rqhk", query_h, key_h, preferred_element_type=jnp.float32) * 0.125
    )
    probs = jnp.where(allowed, jnp.exp(scores - lse_rows[..., None]), 0.0)
    value_grad = jnp.einsum(
        "rqhk,rqhd->rkhd", probs.astype(jnp.bfloat16), out_grad, preferred_element_type=jnp.float32
    )
    prob_grad = jnp.einsum("rqhd,rkhd->rqhk", out_grad, value_h, preferred_element_type=jnp.float32)
    score_grad = (probs * (prob_grad - delta_rows[..., None])).astype(jnp.bfloat16)
    query_grad = (
        jnp.einsum("rqhk,rkhd->rqhd", score_grad, key_h, preferred_element_type=jnp.float32) * 0.125
    )
    key_grad = (
        jnp.einsum("rqhk,rqhd->rkhd", score_grad, query_h, preferred_element_type=jnp.float32)
        * 0.125
    )
    return (query_grad, key_grad, value_grad)


def body_any(
    tokens,
    sent_lengths,
    w_query,
    w_key,
    w_value,
    w_out,
    shared_a,
    shared_b,
    w_in,
    w_back,
    gain_one,
    gain_two,
    scale_dq,
    shift_bq,
    scale_dv,
    shift_bv,
    cotangent,
):
    row_count, span, width = tokens.shape
    head_count = HEADS
    head_size = HEAD_DIM
    blocks = lax.axis_size("blk")
    my_block = lax.axis_index("blk")
    token_count = row_count * span
    token_rows = tokens.reshape(token_count, width)
    seg_full = segment_ids(sent_lengths, span * blocks)
    seg_mine = lax.dynamic_slice_in_dim(seg_full, my_block * span, span, 1)
    w_queries, w_keys, w_values, proj_a, proj_b = (
        lax.all_gather(w_query, "seq", axis=0, tiled=True),
        lax.all_gather(w_key, "seq", axis=0, tiled=True),
        lax.all_gather(w_value, "seq", axis=0, tiled=True),
        lax.all_gather(shared_a, "seq", axis=0, tiled=True),
        lax.all_gather(shared_b, "seq", axis=0, tiled=True),
    )
    projected = dot_plain(token_rows, proj_a).astype(jnp.bfloat16)
    proj_float = projected.astype(jnp.float32)
    lift_q = (proj_float * scale_dq).astype(jnp.bfloat16)
    lift_v = (proj_float * scale_dv).astype(jnp.bfloat16)
    extra_q = dot_plain(lift_q, proj_b)
    extra_v = dot_plain(lift_v, proj_b)
    queries = (dot_plain(token_rows, w_queries) + shift_bq * extra_q).astype(jnp.bfloat16)
    key_rows = dot_plain(token_rows, w_keys).astype(jnp.bfloat16)
    value_rows = (dot_plain(token_rows, w_values) + shift_bv * extra_v).astype(jnp.bfloat16)
    shape4 = (row_count, span, head_count, head_size)
    query_h = queries.reshape(shape4)
    key_h = key_rows.reshape(shape4)
    value_h = value_rows.reshape(shape4)
    start_best = jnp.full((row_count, span, head_count), -1e30, jnp.float32)
    best = start_best
    key_piece = lax.all_gather(key_rows.reshape(row_count, span, width), "blk", axis=1, tiled=True)
    value_piece = lax.all_gather(
        value_rows.reshape(row_count, span, width), "blk", axis=1, tiled=True
    )
    length = key_piece.shape[1]
    key_part = key_piece.reshape(row_count, length, head_count, head_size)
    value_part = value_piece.reshape(row_count, length, head_count, head_size)
    seg_keys = seg_full
    allowed = (seg_mine[:, :, None] == seg_keys[:, None, :])[:, :, None, :]
    scores = (
        jnp.einsum("rqhd,rkhd->rqhk", query_h, key_part, preferred_element_type=jnp.float32) * 0.125
    )
    scores = jnp.where(allowed, scores, -1e30)
    new_best = jnp.maximum(best, jnp.max(scores, axis=-1))
    weight = jnp.where(allowed, jnp.exp(scores - new_best[..., None]), 0.0)
    total = jnp.sum(weight, axis=-1)
    accum = jnp.einsum(
        "rqhk,rkhd->rqhd",
        weight.astype(jnp.bfloat16),
        value_part,
        preferred_element_type=jnp.float32,
    )
    best, total, accum = (new_best, total, accum)
    log_total = best + jnp.log(total)
    context = accum / total[..., None]
    context_b = context.reshape(token_count, width).astype(jnp.bfloat16)
    w_outs, w_ins, w_backs = (
        lax.all_gather(w_out, "seq", axis=0, tiled=True),
        lax.all_gather(w_in, "seq", axis=0, tiled=True),
        lax.all_gather(w_back, "seq", axis=0, tiled=True),
    )

    def norm_first(hidden):
        return layer_norm(hidden, gain_one)

    def norm_second(hidden):
        return layer_norm(hidden, gain_two)

    resid_one = token_rows.astype(jnp.float32) + dot_plain(context_b, w_outs)
    normed_one, norm_one_pull = jax.vjp(norm_first, resid_one)
    pre_act = dot_plain(normed_one.astype(jnp.bfloat16), w_ins)
    act_float, gelu_pull = jax.vjp(exact_gelu, pre_act)
    ffn_part = dot_plain(act_float.astype(jnp.bfloat16), w_backs)
    normed_two, norm_two_pull = jax.vjp(norm_second, normed_one + ffn_part)
    layer_out = normed_two.astype(jnp.bfloat16).reshape(row_count, span, width)
    w_outs, w_ins, w_backs = (
        lax.all_gather(w_out, "seq", axis=0, tiled=True),
        lax.all_gather(w_in, "seq", axis=0, tiled=True),
        lax.all_gather(w_back, "seq", axis=0, tiled=True),
    )
    (grad_two,) = norm_two_pull(cotangent.reshape(token_count, width).astype(jnp.float32))
    act_grad = dot_trans(grad_two.astype(jnp.bfloat16), w_backs)
    (pre_grad,) = gelu_pull(act_grad)
    normed_grad = grad_two + dot_trans(pre_grad.astype(jnp.bfloat16), w_ins)
    (grad_one,) = norm_one_pull(normed_grad)
    context_grad = dot_trans(grad_one.astype(jnp.bfloat16), w_outs).astype(jnp.bfloat16)
    out_grad = context_grad.reshape(shape4)
    delta_rows = jnp.sum(out_grad.astype(jnp.float32) * context, axis=-1)
    zero_grads = jnp.zeros(shape4, jnp.float32)

    def key_step(step, carry):
        key_cur, value_cur, query_acc, key_acc, value_acc = carry
        source = (my_block - step) % blocks
        seg_keys = lax.dynamic_slice_in_dim(seg_full, source * span, span, 1)
        allowed = (seg_mine[:, :, None] == seg_keys[:, None, :])[:, :, None, :]
        q_part, k_part, v_part = block_grads(
            query_h, out_grad, log_total, delta_rows, key_cur, value_cur, allowed
        )
        key_acc, value_acc = (
            shifted((key_acc + k_part).astype(jnp.bfloat16), "blk", 1).astype(jnp.float32),
            shifted((value_acc + v_part).astype(jnp.bfloat16), "blk", 1).astype(jnp.float32),
        )
        key_cur, value_cur = shifted((key_cur, value_cur), "blk", 1)
        return (key_cur, value_cur, query_acc + q_part, key_acc, value_acc)

    looped = lax.fori_loop(
        0, blocks, key_step, (key_h, value_h, zero_grads, zero_grads, zero_grads)
    )
    query_acc, key_acc, value_acc = (looped[2], looped[3], looped[4])
    query_grad = query_acc.reshape(token_count, width).astype(jnp.bfloat16)
    key_grad = key_acc.reshape(token_count, width).astype(jnp.bfloat16)
    value_grad = value_acc.reshape(token_count, width).astype(jnp.bfloat16)
    w_queries, w_keys, w_values, proj_a, proj_b = (
        lax.all_gather(w_query, "seq", axis=0, tiled=True),
        lax.all_gather(w_key, "seq", axis=0, tiled=True),
        lax.all_gather(w_value, "seq", axis=0, tiled=True),
        lax.all_gather(shared_a, "seq", axis=0, tiled=True),
        lax.all_gather(shared_b, "seq", axis=0, tiled=True),
    )
    query_float = query_grad.astype(jnp.float32)
    value_float = value_grad.astype(jnp.float32)
    part_bq = jnp.sum(query_float * extra_q, axis=0)
    part_bv = jnp.sum(value_float * extra_v, axis=0)
    lift_q_grad = dot_trans((query_float * shift_bq).astype(jnp.bfloat16), proj_b)
    lift_v_grad = dot_trans((value_float * shift_bv).astype(jnp.bfloat16), proj_b)
    part_dq = jnp.sum(lift_q_grad * proj_float, axis=0)
    part_dv = jnp.sum(lift_v_grad * proj_float, axis=0)
    proj_grad = (lift_q_grad * scale_dq + lift_v_grad * scale_dv).astype(jnp.bfloat16)
    token_grad = (
        grad_one
        + dot_trans(query_grad, w_queries)
        + dot_trans(key_grad, w_keys)
        + dot_trans(value_grad, w_values)
        + dot_trans(proj_grad, proj_a)
    )
    grad_dq, grad_bq, grad_dv, grad_bv = lax.psum(
        (part_dq, part_bq, part_dv, part_bv), ("seq", "blk")
    )
    return (
        layer_out,
        token_grad.astype(jnp.bfloat16).reshape(row_count, span, width),
        grad_dq,
        grad_bq,
        grad_dv,
        grad_bv,
    )


def swapped(block):
    return lax.ppermute(block, "blk", [(0, 1), (1, 0)])


def summed_groups(vector):
    vector = vector + flipped(vector, 1)
    vector = vector + flipped(vector, 2)
    return (vector + flipped(vector, 4)) + (flipped(vector, 8) + flipped(vector, 12))


def body_two(
    tokens,
    sent_lengths,
    w_query,
    w_key,
    w_value,
    w_out,
    shared_a,
    shared_b,
    w_in,
    w_back,
    gain_one,
    gain_two,
    scale_dq,
    shift_bq,
    scale_dv,
    shift_bv,
    cotangent,
):
    row_count, span, width = tokens.shape
    shards = lax.axis_size("seq")
    heads = HEADS // 2
    part = heads * HEAD_DIM
    wide = 2 * HEAD_DIM
    lead, rank = shared_a.shape
    deep = shared_b.shape[0]
    cuts = w_in.shape[1] // width
    rows = range(row_count)
    spot = jnp.stack([lax.axis_index("blk"), lax.axis_index("seq")]).astype(jnp.int32)

    first, second, vecs = packed(
        spot, shared_a, w_query, w_key, w_value, shared_b, w_out, w_in, w_back,
        (scale_dq, scale_dv, shift_bq, shift_bv), part, wide,
    )
    tie = lax.optimization_barrier

    def core(block):
        return flipped(block, 1)

    other = swapped(tokens)
    lines = [flipped(first, 4), flipped(first, 8), flipped(first, 12)]
    second_over = flipped(second, 2)
    lines, second_over, second = tie((lines, second_over, second))
    quad = jnp.concatenate([first] + lines, axis=0)
    quad_over = flipped(quad, 2)
    quad_core = core(quad)
    far = far_piece(second)
    near = flipped(second, 4)
    both = jnp.concatenate([tokens, other], axis=0).reshape(2 * row_count * span, width)
    turned = both.T
    quad_over, quad_core, far, near, both, turned = tie((quad_over, quad_core, far, near, both, turned))
    down, lift, weights, merged = merge(
        spot, (quad, quad_core, quad_over, core(quad_over)), vecs, shards, lead, deep, rank, part, wide
    )
    qkv = dot_nn(both, weights).astype(bf16)
    qkv, second, second_over, far, near = tie((qkv, second, second_over, far, near))
    last = swapped(far)
    far_over = flipped(far, 2)
    near_over = flipped(second_over, 4)
    second_core, second_over_core = core(second), core(second_over)
    seen = [attend(0, spot, sent_lengths, qkv, heads, HEAD_DIM)]
    seen[0], last, far_over, near_over, second_core, second_over_core, qkv, near, far = tie(
        (seen[0], last, far_over, near_over, second_core, second_over_core, qkv, near, far)
    )
    ctx_recv = [swapped(seen[0][1])]
    last_over = flipped(last, 2)
    near_core, far_core, near_over_core = core(near), core(far), core(near_over)
    seen.append(attend(1, spot, sent_lengths, qkv, heads, HEAD_DIM))
    seen[1], ctx_recv[0], last_over, near_core, far_core, near_over_core, far_over, last = tie(
        (seen[1], ctx_recv[0], last_over, near_core, far_core, near_over_core, far_over, last)
    )
    ctx_recv.append(swapped(seen[1][1]))
    pack = [second, second_core, second_over, second_over_core, near, near_core, near_over, near_over_core]
    pack += [far, far_core, far_over, core(far_over), last, core(last), last_over, core(last_over)]
    fed = []
    for row in rows:
        before = fed[-1][:2] if fed else []
        fed.append(
            ffn(row, spot, seen[row][0], ctx_recv[row], tokens, cotangent, gain_one, gain_two, pack, before, cuts)
        )
    layer_out, grad_one = fed[-1][:2]
    grad_recv = [swapped(fed[row][3]) for row in rows]
    sent = []
    grads = []
    for row in rows:
        whole = attend_back(
            row, spot, sent_lengths, qkv, seen[row][0], seen[row][1],
            fed[row][2], grad_recv[row], seen[row][2], grads, heads, HEAD_DIM,
        )
        halves = 1 if row + 1 < row_count else 2
        each = span // halves
        partials = [
            dot_nt(whole[1, row * span + n * each : row * span + (n + 1) * each], weights).astype(bf16)
            for n in range(halves)
        ]
        if sent:
            whole, partials, sent[-1] = tie((whole, partials, sent[-1]))
        whole, partials = tie((whole, partials))
        grads = [whole]
        sent.append([swapped(partial) for partial in partials])
    whole = grads[0]
    flat = trained(spot, turned, whole.reshape(2 * row_count * span, 3 * part), merged, down, lift, vecs, wide)
    flat, sent[-1][0] = tie((flat, sent[-1][0]))
    flat = summed_groups(flat)
    base = grad_one.reshape(row_count * span, width).astype(f32) + dot_nt(whole[0], weights)
    base = base.astype(bf16)
    token_grad = []
    for row in rows[:-1]:
        token_grad = [finish(row, row_count, base, sent[row], token_grad)]
    flat, sent[-1], token_grad = tie((flat, sent[-1], token_grad))
    flat = (flat + swapped(flat)).reshape(-1)
    token_grad = finish(row_count - 1, row_count, base, sent[-1], token_grad)
    return (
        layer_out,
        token_grad,
        flat[:rank],
        flat[rank : rank + width],
        flat[rank + width : 2 * rank + width],
        flat[2 * rank + width :],
    )


def solution(mesh):
    return jax.shard_map(
        body_two if mesh.shape["blk"] == 2 and mesh.shape["seq"] == 16 else body_any,
        mesh=mesh,
        in_specs=(
            P("seq", "blk", None),
            P("seq", None),
            P("seq", None),
            P("seq", None),
            P("seq", None),
            P("seq", None),
            P("seq", None),
            P("seq", None),
            P("seq", None),
            P("seq", None),
            P(),
            P(),
            P(),
            P(),
            P(),
            P(),
            P("seq", "blk", None),
        ),
        out_specs=(P("seq", "blk", None), P("seq", "blk", None), P(), P(), P(), P()),
        check_vma=False,
    )
```

```python
import functools

import jax
import jax.numpy as jnp
from jax import lax
from jax.experimental import pallas as pl
from jax.experimental.pallas import tpu as pltpu
from jax.sharding import PartitionSpec as P

HEADS = 12
HEAD_DIM = 64
bf16 = jnp.bfloat16
f32 = jnp.float32


LN2 = 0.6931471805599453
LOG2E = 1.4426950408889634
SEGS = 5
PARTS = 3
TILE = 256
STEP = 128

def dot_nt(a,b): return lax.dot_general(a,b,(((1,),(1,)),((),())),preferred_element_type=f32)
def dot_nn(a,b): return jnp.dot(a,b,preferred_element_type=f32)

def lane_row(test, wide, kind=f32):
    lane = lax.broadcasted_iota(jnp.int32, (1, wide), 1)
    return jnp.where(test(lane), 1.0, 0.0).astype(kind)

def part_rows(wide, start):
    return [lane_row(lambda l: l == start + n, wide) for n in range(PARTS)]

def spread(column, rows):
    top = column.astype(bf16).astype(f32)
    return (top*rows[0] + (column-top)*rows[1]).astype(bf16)

def cross_ones(wide, hd):
    a = lax.broadcasted_iota(jnp.int32, (wide, wide), 0) < hd
    b = lax.broadcasted_iota(jnp.int32, (wide, wide), 1) < hd
    return jnp.where(a != b, 1.0, 0.0).astype(bf16)

def side_rows(wide, hd):
    return [lane_row(lambda l: l < hd, wide, bf16), lane_row(lambda l: l >= hd, wide, bf16)]

def bounds_of(lens, row):
    bounds = [lens[row, 0]]
    for n in range(1, SEGS-1):
        bounds.append(bounds[-1] + lens[row, n])
    return bounds

def key_span(bounds, i, span):
    low = 0
    for bound in bounds:
        low = jnp.where(bound <= i*TILE, bound, low)
    high = span
    for bound in reversed(bounds):
        high = jnp.where(bound > i*TILE + TILE-1, bound, high)
    begin = lax.div(low, STEP)
    count = lax.div(high - begin*STEP + TILE-1, TILE)
    return jnp.minimum(begin, lax.div(span - count*TILE, STEP)), count

def marks(bounds, span, wide, hd, side):
    place = lax.broadcasted_iota(jnp.int32, (span, wide), 0)
    lane = lax.broadcasted_iota(jnp.int32, (span, wide), 1) - (hd if side == 0 else 0)
    lane = jnp.where((lane >= 0) & (lane < hd), lane, hd)
    seg = jnp.zeros((span, wide), jnp.int32)
    for bound in bounds:
        seg = seg + jnp.where(place >= bound, 1, 0)
    asked = jnp.where((lane < SEGS) & (lane != seg), 1.0, 0.0).astype(bf16)
    held = jnp.where(lane == seg, -1e30, jnp.where((lane >= SEGS) & (lane < SEGS+PARTS), 1.0, 0.0)).astype(bf16)
    return asked, held

def by_half(mine, work):
    for n in range(2):
        @pl.when(mine == n)
        def _():
            work(n)

def query_tiles(bounds, span, work, broad):
    tiles = span//TILE
    fewest = tiles
    for i in range(tiles):
        fewest = jnp.minimum(fewest, key_span(bounds, i, span)[1])
    @pl.when(fewest == tiles)
    def _():
        def one(i, carry):
            work(pl.ds(pl.multiple_of(i*broad, broad), broad), slice(0, span))
            return carry
        lax.fori_loop(0, span//broad, one, 0)
    @pl.when(fewest < tiles)
    def _():
        def one(i, carry):
            rows = pl.ds(pl.multiple_of(i*TILE, TILE), TILE)
            begin, count = key_span(bounds, i, span)
            start = pl.multiple_of(begin*STEP, STEP)
            for n in range(1, tiles+1):
                @pl.when(count == n)
                def _():
                    work(rows, pl.ds(start, n*TILE) if n < tiles else slice(0, span))
            return carry
        lax.fori_loop(0, tiles, one, 0)

def attend_kernel(spot, lens, xo_ref, xp_ref, own_ref, par_ref, qa_ref, qf, kf, ka, va, og, outs, *, hd, row):
    half = xo_ref.shape[0]
    bounds = bounds_of(lens, row)
    span = 2*half
    wide = 2*hd
    sides = side_rows(wide, hd)
    swap = cross_ones(wide, hd)
    first = lax.broadcasted_iota(jnp.int32, (span, wide), 1) < hd
    start = [hd+SEGS, SEGS]
    parts = [part_rows(wide, start[s]) for s in range(2)]
    @pl.when(pl.program_id(0) == 0)
    def _():
        for s in range(2):
            qf[s], kf[s] = marks(bounds, span, wide, hd, s)
    longest = None
    for x_ref in (xo_ref, xp_ref):
        kp = x_ref[:, wide:2*wide]
        norms = jnp.max(dot_nn(kp*kp, swap), axis=0, keepdims=True)
        longest = norms if longest is None else jnp.maximum(longest, norms)
    def place(n):
        for x_ref, at in ((xo_ref, n), (xp_ref, 1-n)):
            rows = slice(at*half, (at+1)*half)
            qp = x_ref[:, 0:wide]
            kp = x_ref[:, wide:2*wide]
            vp = x_ref[:, 2*wide:3*wide]
            top = jnp.sqrt(dot_nn(qp*qp, swap) * longest) * 1.02
            for s in range(2):
                qa_ref[s, rows, :] = qp*sides[s] + (qf[s, rows, :] - (top*parts[s][0]).astype(bf16))
                ka[s, rows, :] = kp*sides[s] + kf[s, rows, :]
                va[s, rows, :] = vp*sides[s] + sides[1-s]
    by_half(spot[0], place)
    def weigh(rows, keys):
        for s in range(2):
            w = jnp.exp2(dot_nt(qa_ref[s, rows, :], ka[s, keys, :])).astype(bf16)
            og[s, rows, :] = dot_nn(w, va[s, keys, :])
    query_tiles(bounds, span, weigh, 512)
    @pl.when(jnp.logical_not(jnp.min(jnp.where(first, og[1], og[0])) > 2.0**-80))
    def _():
        def exact_tile(i, carry):
            rows = pl.ds(pl.multiple_of(i*TILE, TILE), TILE)
            for s in range(2):
                plain = qa_ref[s, rows, :] * (1.0 - parts[s][0]).astype(bf16)
                m = jnp.max(dot_nt(plain, ka[s]), axis=1, keepdims=True)
                qa_ref[s, rows, :] = plain - (jnp.broadcast_to(m, (TILE, wide))*parts[s][0]).astype(bf16)
            weigh(rows, slice(0, span))
            return carry
        lax.fori_loop(0, span//TILE, exact_tile, 0)
    total = jnp.where(first, og[1], og[0])
    outs[...] = (jnp.where(first, og[0], og[1]) / pltpu.roll(total, hd, 1)).astype(bf16)
    lse = -jnp.log2(total)
    for s in range(2):
        qa_ref[s] = qa_ref[s] + spread(lse, parts[s][1:])
    def leave(n):
        own_ref[...] = outs[n*half:(n+1)*half, :]
        par_ref[...] = outs[(1-n)*half:(2-n)*half, :]
    by_half(spot[0], leave)

def attend(row, spot, lens, qkv, heads, hd):
    count = lens.shape[0]
    half = qkv.shape[0]//(2*count); span = 2*half; mine = heads*hd; wide = 2*hd
    col = lambda p, s, l: (0, p)
    return pl.pallas_call(
        functools.partial(attend_kernel, hd=hd, row=row),
        grid_spec=pltpu.PrefetchScalarGridSpec(
            num_scalar_prefetch=2, grid=(heads//2,),
            in_specs=[pl.BlockSpec((half, 3*wide), lambda p, s, l: (row, p)), pl.BlockSpec((half, 3*wide), lambda p, s, l: (count+row, p))],
            out_specs=[
                pl.BlockSpec((half, wide), col),
                pl.BlockSpec((half, wide), col),
                pl.BlockSpec((2, span, wide), lambda p, s, l: (p, 0, 0)),
            ],
            scratch_shapes=[
                pltpu.VMEM((2, span, wide), bf16),
                pltpu.VMEM((2, span, wide), bf16),
                pltpu.VMEM((2, span, wide), bf16),
                pltpu.VMEM((2, span, wide), bf16),
                pltpu.VMEM((2, span, wide), f32),
                pltpu.VMEM((span, wide), bf16),
            ]),
        out_shape=[
            jax.ShapeDtypeStruct((half, mine), bf16),
            jax.ShapeDtypeStruct((half, mine), bf16),
            jax.ShapeDtypeStruct((heads, span, wide), bf16),
        ],
        compiler_params=pltpu.CompilerParams(vmem_limit_bytes=32<<20),
        cost_estimate=pl.CostEstimate(flops=16*span*span*mine, bytes_accessed=span*mine*12, transcendentals=span*span*heads),
    )(spot, lens, qkv, qkv)

def attend_back_kernel(spot, lens, xo_ref, xp_ref, co_ref, cp_ref, go_ref, gp_ref, qa_ref, *refs, hd, row):
    out_ref, kf, ka, va, ga, kt, kacc, vacc, qacc = refs[-9:]
    half = xo_ref.shape[0]
    bounds = bounds_of(lens, row)
    span = 2*half
    wide = 2*hd
    sides = side_rows(wide, hd)
    low = [lane_row(lambda l: (l >= hd) & (l < hd+PARTS), wide, bf16), lane_row(lambda l: l < PARTS, wide, bf16)]
    parts = [part_rows(wide, hd), part_rows(wide, 0)]
    swap = cross_ones(wide, hd)
    first = lax.broadcasted_iota(jnp.int32, (half, wide), 1) < hd
    @pl.when(pl.program_id(0) == 0)
    def _():
        for s in range(2):
            kf[s] = marks(bounds, span, wide, hd, s)[1]
    def place(n):
        for x_ref, c_ref, g_ref, at in ((xo_ref, co_ref, go_ref, n), (xp_ref, cp_ref, gp_ref, 1-n)):
            rows = slice(at*half, (at+1)*half)
            kp = x_ref[:, wide:2*wide]
            vp = x_ref[:, 2*wide:3*wide]
            gp = g_ref[...]
            kt[:, rows] = kp.T
            prod = gp.astype(f32) * c_ref[...].astype(f32)
            top = prod.astype(bf16)
            delta = dot_nn(top, swap) + dot_nn((prod - top.astype(f32)).astype(bf16), swap)
            for s in range(2):
                ka[s, rows, :] = kp*sides[s] + kf[s, rows, :]
                va[s, rows, :] = vp*sides[s] + low[s]
                ga[s, rows, :] = gp*sides[s] + spread(-delta, parts[s])
    by_half(spot[0], place)
    kacc[...] = jnp.zeros_like(kacc)
    vacc[...] = jnp.zeros_like(vacc)
    def work(rows, keys):
        for s in range(2):
            qq = qa_ref[s, rows, :]
            gg = ga[s, rows, :]
            probs = jnp.exp2(dot_nt(ka[s, keys, :], qq))
            slope = (probs * dot_nt(va[s, keys, :], gg)).astype(bf16)
            vacc[s, keys, :] += dot_nn(probs.astype(bf16), gg)
            kacc[s, keys, :] += dot_nn(slope, qq)
            qacc[s*hd:(s+1)*hd, rows] = dot_nn(kt[s*hd:(s+1)*hd, keys], slope)
    query_tiles(bounds, span, work, TILE)
    def leave(n):
        for part, at in ((0, n), (1, 1-n)):
            rows = slice(at*half, (at+1)*half)
            out_ref[part, :, 0:wide] = (qacc[:, rows].T * LN2).astype(bf16)
            out_ref[part, :, wide:2*wide] = (jnp.where(first, kacc[0, rows, :], kacc[1, rows, :]) * LN2).astype(bf16)
            out_ref[part, :, 2*wide:3*wide] = jnp.where(first, vacc[0, rows, :], vacc[1, rows, :]).astype(bf16)
    by_half(spot[0], leave)

def attend_back(row, spot, lens, qkv, ctx_own, ctx_par, g_own, g_par, qa, before, heads, hd):
    count = lens.shape[0]
    half = qkv.shape[0]//(2*count); span = 2*half; mine = heads*hd; wide = 2*hd
    col = lambda p, s, l: (0, p)
    at_row = lambda p, s, l: (row, p)
    return pl.pallas_call(
        functools.partial(attend_back_kernel, hd=hd, row=row),
        grid_spec=pltpu.PrefetchScalarGridSpec(
            num_scalar_prefetch=2, grid=(heads//2,),
            in_specs=[pl.BlockSpec((half, 3*wide), at_row), pl.BlockSpec((half, 3*wide), lambda p, s, l: (count+row, p))] + [pl.BlockSpec((half, wide), col)]*4
            + [pl.BlockSpec((2, span, wide), lambda p, s, l: (p, 0, 0))] + [pl.BlockSpec(memory_space=pl.ANY)]*len(before),
            out_specs=pl.BlockSpec((2, half, 3*wide), lambda p, s, l: (0, row, p)),
            scratch_shapes=[
                pltpu.VMEM((2, span, wide), bf16),
                pltpu.VMEM((2, span, wide), bf16),
                pltpu.VMEM((2, span, wide), bf16),
                pltpu.VMEM((2, span, wide), bf16),
                pltpu.VMEM((wide, span), bf16),
                pltpu.VMEM((2, span, wide), f32),
                pltpu.VMEM((2, span, wide), f32),
                pltpu.VMEM((wide, span), f32),
            ]),
        out_shape=jax.ShapeDtypeStruct((2, count*half, 3*mine), bf16),
        input_output_aliases={9+n: n for n in range(len(before))},
        compiler_params=pltpu.CompilerParams(vmem_limit_bytes=50<<20),
        cost_estimate=pl.CostEstimate(flops=40*span*span*mine, bytes_accessed=span*mine*20, transcendentals=span*span*heads),
    )(spot, lens, qkv, qkv, ctx_own, ctx_par, g_own, g_par, qa, *before)


def pack_kernel(place, a_ref, q_ref, k_ref, v_ref, b_ref, out_ref, in_ref, back_ref, *refs, wide):
    vectors, (first_ref, second_ref, vecs) = refs[:-3], refs[-3:]
    vecs[...] = jnp.zeros_like(vecs)
    for n, ref in enumerate(vectors):
        vecs[n : n + 1, : ref.shape[0]] = ref[...].reshape(1, ref.shape[0])
    lead = a_ref.shape[0]
    width = out_ref.shape[1]
    row = 0
    pieces = [a_ref[:, at : at + wide] for at in range(0, a_ref.shape[1], wide)]
    for at in range(0, q_ref.shape[1], wide):
        pieces += [ref[:, at : at + wide] for ref in (q_ref, k_ref, v_ref)]
    pieces += [b_ref[:, at : at + wide] for at in range(0, b_ref.shape[1], wide)]
    for piece in pieces:
        first_ref[row : row + piece.shape[0], :] = piece
        row += piece.shape[0]
    row = 0
    pieces = [out_ref[...]]
    pieces += [in_ref[:, at : at + width] for at in range(0, in_ref.shape[1], width)]
    pieces += [back_ref[...]]
    for piece in pieces:
        second_ref[row : row + piece.shape[0], :] = piece
        row += piece.shape[0]


def packed(place, shared_a, w_query, w_key, w_value, shared_b, w_out, w_in, w_back, vectors, part, wide):
    lead, rank = shared_a.shape
    width = w_out.shape[1]
    rows = lead * (rank + 3 * part) // wide + shared_b.shape[0] * part // wide
    whole = lambda array: pl.BlockSpec(array.shape, lambda i, s: (0, 0))
    half = lambda array: pl.BlockSpec((array.shape[0], part), lambda i, s: (0, s[0]))
    total = lead + lead * w_in.shape[1] // width + w_back.shape[0]
    return pl.pallas_call(
        functools.partial(pack_kernel, wide=wide),
        grid_spec=pltpu.PrefetchScalarGridSpec(
            num_scalar_prefetch=1,
            grid=(1,),
            in_specs=[whole(shared_a), half(w_query), half(w_key), half(w_value), half(shared_b), whole(w_out), whole(w_in), whole(w_back)]
            + [pl.BlockSpec(vector.shape, lambda i, s: (0,)) for vector in vectors],
            out_specs=[pl.BlockSpec((rows, wide), lambda i, s: (0, 0)), pl.BlockSpec((total, width), lambda i, s: (0, 0)), pl.BlockSpec((8, rank), lambda i, s: (0, 0))],
        ),
        out_shape=[jax.ShapeDtypeStruct((rows, wide), bf16), jax.ShapeDtypeStruct((total, width), bf16), jax.ShapeDtypeStruct((8, rank), f32)],
        compiler_params=pltpu.CompilerParams(vmem_limit_bytes=60 << 20),
    )(place, shared_a, w_query, w_key, w_value, shared_b, w_out, w_in, w_back, *vectors)


def bent(vecs, at, side, part):
    row = vecs[at : at + 1, : 2 * part]
    return jnp.where(side == 0, row[:, :part], row[:, part:])


def merge_kernel(spot, *refs, shards, rank, part, wide):
    quads = refs[:4]
    vecs, down, lift, weights, merged, mixed = refs[4:]
    each = quads[0].shape[0] // 4
    lead = down.shape[1]
    deep = lift.shape[1]
    pairs = part // wide
    for j in range(shards):
        at = spot[1] ^ j
        piece = quads[j % 4]
        row = each * (j // 4)
        for n in range(rank // wide):
            down[at, :, n * wide : (n + 1) * wide] = piece[row : row + lead, :]
            row += lead
        for n in range(3 * pairs):
            mixed[at, :, n * wide : (n + 1) * wide] = piece[row : row + lead, :]
            row += lead
        for n in range(pairs):
            lift[at, :, n * wide : (n + 1) * wide] = piece[row : row + deep, :]
            row += deep
    low = down[...].reshape(shards * lead, rank)
    high = lift[...].reshape(shards * deep, part)
    delta_q = dot_nn(low * vecs[0:1, :].astype(bf16), high)
    merged[:, :part] = delta_q.astype(bf16)
    delta_q = delta_q * bent(vecs, 2, spot[0], part)
    delta_v = dot_nn(low * vecs[1:2, :].astype(bf16), high)
    merged[:, part:] = delta_v.astype(bf16)
    delta_v = delta_v * bent(vecs, 3, spot[0], part)
    for n in range(pairs):
        cols = slice(n * wide, (n + 1) * wide)
        base = 3 * n * wide
        get = lambda s: mixed[:, :, base + s * wide : base + (s + 1) * wide].reshape(shards * lead, wide)
        weights[:, base : base + wide] = ((get(0).astype(f32) + delta_q[:, cols]) * (0.125 * LOG2E)).astype(bf16)
        weights[:, base + wide : base + 2 * wide] = get(1)
        weights[:, base + 2 * wide : base + 3 * wide] = (get(2).astype(f32) + delta_v[:, cols]).astype(bf16)


def merge(spot, quads, vecs, shards, lead, deep, rank, part, wide):
    width = shards * lead
    whole = lambda shape: pl.BlockSpec(shape, lambda i, s: (0,) * len(shape))
    return pl.pallas_call(
        functools.partial(merge_kernel, shards=shards, rank=rank, part=part, wide=wide),
        grid_spec=pltpu.PrefetchScalarGridSpec(
            num_scalar_prefetch=1,
            grid=(1,),
            in_specs=[whole(quads[0].shape)] * 4 + [whole(vecs.shape)],
            out_specs=[whole((shards, lead, rank)), whole((shards, deep, part)), whole((width, 3 * part)), whole((width, 2 * part))],
            scratch_shapes=[pltpu.VMEM((shards, lead, 3 * part), bf16)],
        ),
        out_shape=[
            jax.ShapeDtypeStruct((shards, lead, rank), bf16),
            jax.ShapeDtypeStruct((shards, deep, part), bf16),
            jax.ShapeDtypeStruct((width, 3 * part), bf16),
            jax.ShapeDtypeStruct((width, 2 * part), bf16),
        ],
        compiler_params=pltpu.CompilerParams(vmem_limit_bytes=40 << 20),
        cost_estimate=pl.CostEstimate(flops=40 * width * rank * part, bytes_accessed=1 << 20, transcendentals=0),
    )(spot, *quads, vecs)


def flipped(block, mask):
    count = lax.axis_size("seq")
    return lax.ppermute(block, "seq", [(i, i ^ mask) for i in range(count)])


def far_piece(piece):
    count = lax.axis_size("seq")
    pairs = [(2 * i + b, 2 * (i ^ (8 + 4 * b)) + b) for i in range(count) for b in range(2)]
    return lax.ppermute(piece, ("seq", "blk"), pairs)


def spread_square(block):
    across = flipped(block, 2)
    return [block, flipped(block, 1), across, flipped(across, 1)]


def trained_kernel(
    spot, turned_ref, grad_ref, vecs, merged_hbm, down_hbm, lift_hbm, out_ref, moment, merged_ref, down_ref, lift_ref, sems,
    *, wide
):
    held = ((merged_hbm, merged_ref), (down_hbm, down_ref), (lift_hbm, lift_ref))
    lead = down_ref.shape[1]
    width = down_ref.shape[0] * lead
    rank = down_ref.shape[2]
    part = lift_ref.shape[2]
    pairs = part // wide
    picked = [grad_ref[:, (3 * n + s) * wide : (3 * n + s + 1) * wide] for s in (0, 2) for n in range(pairs)]
    added = dot_nn(turned_ref[...], jnp.concatenate(picked, axis=1))
    @pl.when(pl.program_id(0) == 0)
    def _():
        for n, (source, target) in enumerate(held):
            pltpu.make_async_copy(source, target, sems.at[n]).start()
        moment[...] = added
    @pl.when(pl.program_id(0) > 0)
    def _():
        moment[...] += added
    @pl.when(pl.program_id(0) == pl.num_programs(0) - 1)
    def _():
        for n, (source, target) in enumerate(held):
            pltpu.make_async_copy(source, target, sems.at[n]).wait()
        down = down_ref[...].reshape(width, rank).astype(f32)
        lift = lift_ref[...].reshape(rank, part)
        out_ref[...] = jnp.zeros_like(out_ref)
        base = 0
        for s, coef in ((0, 0.125 * LOG2E), (1, 1.0)):
            cols = slice(s * part, (s + 1) * part)
            shift = jnp.sum(merged_ref[:, cols].astype(f32) * moment[:, cols], axis=0, keepdims=True) * coef
            bend = bent(vecs, 2 + s, spot[0], part) * coef
            bent_moment = (moment[:, cols] * bend).astype(bf16)
            scale = jnp.sum(down * dot_nt(bent_moment, lift), axis=0, keepdims=True)
            for n in range(rank // wide):
                out_ref[base + n : base + n + 1, :] = scale[:, n * wide : (n + 1) * wide]
            base += rank // wide
            for n in range(pairs):
                out_ref[pl.ds(base + pairs * spot[0] + n, 1), :] = shift[:, n * wide : (n + 1) * wide]
            base += 2 * pairs


def trained(spot, turned, grads, merged, down, lift, vecs, wide):
    rank, part = down.shape[2], lift.shape[2]
    width, total = turned.shape
    step = total // 4
    whole = lambda array: pl.BlockSpec(array.shape, lambda i, s: (0,) * array.ndim)
    rows = 2 * (rank + 2 * part) // wide
    return pl.pallas_call(
        functools.partial(trained_kernel, wide=wide),
        grid_spec=pltpu.PrefetchScalarGridSpec(
            num_scalar_prefetch=1,
            grid=(4,),
            in_specs=[
                pl.BlockSpec((width, step), lambda i, s: (0, i)),
                pl.BlockSpec((step, grads.shape[1]), lambda i, s: (i, 0)),
            ]
            + [whole(vecs)] + [pl.BlockSpec(memory_space=pl.ANY)] * 3,
            out_specs=pl.BlockSpec((rows, wide), lambda i, s: (0, 0)),
            scratch_shapes=[pltpu.VMEM((width, 2 * part), f32)]
            + [pltpu.VMEM(array.shape, bf16) for array in (merged, down, lift)] + [pltpu.SemaphoreType.DMA((3,))],
        ),
        out_shape=jax.ShapeDtypeStruct((rows, wide), f32),
        compiler_params=pltpu.CompilerParams(vmem_limit_bytes=60 << 20),
        cost_estimate=pl.CostEstimate(flops=8 * width * total * part, bytes_accessed=12 << 20, transcendentals=0),
    )(spot, turned, grads, vecs, merged, down, lift)


def finish_kernel(base_ref, *refs, parts):
    out_ref = refs[-1]
    each = refs[0].shape[0]
    for n in range(parts):
        rows = slice(n * each, (n + 1) * each)
        out_ref[rows, :] = (base_ref[rows, :].astype(f32) + refs[n][...].astype(f32)).astype(bf16)


def finish(row, count, base, sent, before):
    each, width = sent[0].shape
    span = each * len(sent)
    return pl.pallas_call(
        functools.partial(finish_kernel, parts=len(sent)),
        grid=(1,),
        in_specs=[pl.BlockSpec((span, width), lambda i: (row, 0))]
        + [pl.BlockSpec((each, width), lambda i: (0, 0))] * len(sent)
        + [pl.BlockSpec(memory_space=pl.ANY)] * len(before),
        out_specs=pl.BlockSpec((None, span, width), lambda i: (row, 0, 0)),
        out_shape=jax.ShapeDtypeStruct((count, span, width), bf16),
        input_output_aliases={1 + len(sent) + n: n for n in range(len(before))},
        compiler_params=pltpu.CompilerParams(vmem_limit_bytes=60 << 20),
    )(base, *sent, *before)


def centred(hidden):
    off = hidden - jnp.mean(hidden, axis=-1, keepdims=True)
    scale = lax.rsqrt(jnp.mean(off*off, axis=-1, keepdims=True) + 1e-05)
    return off*scale, scale

def norm_back(grad, unit, scale):
    inner = jnp.mean(grad*unit, axis=-1, keepdims=True)
    return scale*(grad - jnp.mean(grad, axis=-1, keepdims=True) - unit*inner)

def gelu_pair(x):
    size = jnp.abs(x)
    base = 1.0 + size*(0.3275911*0.7071067811865476)
    t = pl.reciprocal(base, approx=True)
    t = t*(2.0 - base*t)
    bell = jnp.exp2(x*x*(-0.7213475204444817))
    tail = t*(0.127414796 + t*(-0.142248368 + t*(0.7107068705 + t*(-0.7265760135 + t*0.5307027145))))*bell
    below = jnp.where(x < 0, tail, 1.0 - tail)
    return x*below, below + x*(bell*0.3989422804014327)

def ffn_kernel(spot, co_hbm, cr_hbm, x_hbm, cot_hbm, g1_ref, g2_ref, *refs, shards, cuts, row):
    pieces = refs[:shards]
    out_ref, grad_ref, own_ref, send_ref, co_ref, cr_ref, x_ref, cot_ref, wo, wi, wb, slopes, acts, sems = refs[-14:]
    width = x_ref.shape[1]
    lead = wo.shape[1]
    back = wb.shape[1]
    per = shards//cuts
    mine = spot[0]
    seat = spot[1]
    groups = [0, 4, 8 + 4*mine, 12 - 4*mine]
    ats = [seat ^ (groups[j//per] + j%per) for j in range(shards)]
    def bring(source, target, n):
        pltpu.make_async_copy(source, target, sems.at[n]).start()
    def arrived(held, n):
        pltpu.make_async_copy(held, held, sems.at[n]).wait()
    bring(co_hbm, co_ref, 1+2*cuts)
    bring(cr_hbm, cr_ref, 2+2*cuts)
    bring(x_hbm.at[row], x_ref, 3+2*cuts)
    for j in range(shards):
        bring(pieces[j].at[0:lead, :], wo.at[ats[j]], 0)
    for g in range(cuts):
        block = lax.shift_right_logical(seat ^ groups[g], 2)
        start = pl.multiple_of(lead*(1+block), 16)
        for j in range(shards):
            bring(pieces[j].at[pl.ds(start, lead), :], wi.at[g, ats[j]], 1+g)
        for j in range(g*per, (g+1)*per):
            bring(pieces[j].at[lead*(1+cuts):lead*(1+cuts)+back, :], wb.at[g*per + (ats[j] & (per-1))], 1+cuts+g)
    bring(cot_hbm.at[row], cot_ref, 4+2*cuts)
    part = shards//2
    half = width//2
    def out_rows(who):
        return wo[pl.ds(pl.multiple_of(who*part, part), part)].reshape(half, width)
    def w_in(j): return wi[j].reshape(width, width)
    def w_back(j): return wb[j*per:(j+1)*per].reshape(per*back, width)
    arrived(co_ref, 1+2*cuts)
    arrived(cr_ref, 2+2*cuts)
    arrived(x_ref, 3+2*cuts)
    arrived(wo, 0)
    resid = x_ref[...].astype(f32) + dot_nn(co_ref[...], out_rows(mine)) + dot_nn(cr_ref[...], out_rows(1-mine))
    unit_one, scale_one = centred(resid)
    gain_one = g1_ref[...].reshape(1, width)
    gain_two = g2_ref[...].reshape(1, width)
    normed = unit_one*gain_one
    low = normed.astype(bf16)
    total = normed
    for j in range(cuts):
        arrived(wi.at[j], 1+j)
        arrived(wb.at[j*per:(j+1)*per], 1+cuts+j)
    for j in range(cuts):
        for at in range(0, width, 256):
            for top in range(0, x_ref.shape[0], 256):
                act, slope = gelu_pair(dot_nn(low[top:top+256], wi[j, :, :, at:at+256].reshape(width, 256)))
                acts[top:top+256, at:at+256] = act.astype(bf16)
                slopes[j, top:top+256, at:at+256] = slope.astype(bf16)
        total = total + dot_nn(acts[...], w_back(j))
    unit_two, scale_two = centred(total)
    out_ref[...] = (unit_two*gain_two).astype(bf16)
    arrived(cot_ref, 4+2*cuts)
    grad_two = norm_back(cot_ref[...].astype(f32)*gain_two, unit_two, scale_two)
    low_two = grad_two.astype(bf16)
    grad = grad_two
    for j in range(cuts):
        pre_grad = (dot_nt(low_two, w_back(j))*slopes[j].astype(f32)).astype(bf16)
        grad = grad + dot_nt(pre_grad, w_in(j))
    grad_one = norm_back(grad*gain_one, unit_one, scale_one)
    low_one = grad_one.astype(bf16)
    grad_ref[...] = low_one
    send_ref[...] = dot_nt(low_one, out_rows(1-mine)).astype(bf16)
    own_ref[...] = dot_nt(low_one, out_rows(mine)).astype(bf16)

def ffn(row, spot, ctx_own, ctx_recv, x, cot, gain_one, gain_two, pieces, before, cuts):
    count, span, width = x.shape
    shards = len(pieces)
    lead = width//shards
    back = cuts*width//shards
    whole = lambda shape: pl.BlockSpec(shape, lambda i, s: (0,)*len(shape))
    at_row = pl.BlockSpec((None, span, width), lambda i, s: (row, 0, 0))
    anywhere = pl.BlockSpec(memory_space=pl.ANY)
    return pl.pallas_call(
        functools.partial(ffn_kernel, shards=shards, cuts=cuts, row=row),
        grid_spec=pltpu.PrefetchScalarGridSpec(
            num_scalar_prefetch=1, grid=(1,),
            in_specs=[anywhere]*4 + [whole((width,))]*2 + [anywhere]*(shards+len(before)),
            out_specs=[at_row, at_row, whole((span, width//2)), whole((span, width//2))],
            scratch_shapes=[
                pltpu.VMEM((span, width//2), bf16),
                pltpu.VMEM((span, width//2), bf16),
                pltpu.VMEM((span, width), bf16),
                pltpu.VMEM((span, width), bf16),
                pltpu.VMEM((shards, lead, width), bf16),
                pltpu.VMEM((cuts, shards, lead, width), bf16),
                pltpu.VMEM((shards, back, width), bf16),
                pltpu.VMEM((cuts, span, width), bf16),
                pltpu.VMEM((span, width), bf16),
                pltpu.SemaphoreType.DMA((5+2*cuts,)),
            ]),
        out_shape=[
            jax.ShapeDtypeStruct((count, span, width), bf16),
            jax.ShapeDtypeStruct((count, span, width), bf16),
            jax.ShapeDtypeStruct((span, width//2), bf16),
            jax.ShapeDtypeStruct((span, width//2), bf16),
        ],
        input_output_aliases={7+shards+n: n for n in range(len(before))},
        compiler_params=pltpu.CompilerParams(vmem_limit_bytes=56<<20),
        cost_estimate=pl.CostEstimate(flops=8*span*width*width*(2+4*cuts), bytes_accessed=2*(2+2*cuts)*width*width, transcendentals=2*span*width*cuts),
    )(spot, ctx_own, ctx_recv, x, cot, gain_one, gain_two, *pieces, *before)


def shifted(shard, axis, by):
    count = lax.axis_size(axis)
    return lax.ppermute(shard, axis, [(i, (i + by) % count) for i in range(count)])


def layer_norm(hidden, gain):
    centre = hidden - jnp.mean(hidden, axis=-1, keepdims=True)
    spread = jnp.mean(centre * centre, axis=-1, keepdims=True)
    return centre * lax.rsqrt(spread + 1e-05) * gain


def exact_gelu(values):
    return jax.nn.gelu(values, approximate=False)


def segment_ids(lengths, total):
    place = jnp.arange(total, dtype=jnp.int32)[None, :]
    bounds = jnp.cumsum(lengths, axis=1)
    counted = jnp.zeros((lengths.shape[0], total), jnp.int32)
    for column in range(lengths.shape[1]):
        counted = counted + (place >= bounds[:, column : column + 1]).astype(jnp.int32)
    return counted


def dot_plain(left, right):
    return jnp.dot(left, right, preferred_element_type=jnp.float32)


def dot_trans(left, right):
    return lax.dot_general(
        left, right, (((1,), (1,)), ((), ())), preferred_element_type=jnp.float32
    )


def block_grads(query_h, out_grad, lse_rows, delta_rows, key_h, value_h, allowed):
    scores = (
        jnp.einsum("rqhd,rkhd->rqhk", query_h, key_h, preferred_element_type=jnp.float32) * 0.125
    )
    probs = jnp.where(allowed, jnp.exp(scores - lse_rows[..., None]), 0.0)
    value_grad = jnp.einsum(
        "rqhk,rqhd->rkhd", probs.astype(jnp.bfloat16), out_grad, preferred_element_type=jnp.float32
    )
    prob_grad = jnp.einsum("rqhd,rkhd->rqhk", out_grad, value_h, preferred_element_type=jnp.float32)
    score_grad = (probs * (prob_grad - delta_rows[..., None])).astype(jnp.bfloat16)
    query_grad = (
        jnp.einsum("rqhk,rkhd->rqhd", score_grad, key_h, preferred_element_type=jnp.float32) * 0.125
    )
    key_grad = (
        jnp.einsum("rqhk,rqhd->rkhd", score_grad, query_h, preferred_element_type=jnp.float32)
        * 0.125
    )
    return (query_grad, key_grad, value_grad)


def body_any(
    tokens,
    sent_lengths,
    w_query,
    w_key,
    w_value,
    w_out,
    shared_a,
    shared_b,
    w_in,
    w_back,
    gain_one,
    gain_two,
    scale_dq,
    shift_bq,
    scale_dv,
    shift_bv,
    cotangent,
):
    row_count, span, width = tokens.shape
    head_count = HEADS
    head_size = HEAD_DIM
    blocks = lax.axis_size("blk")
    my_block = lax.axis_index("blk")
    token_count = row_count * span
    token_rows = tokens.reshape(token_count, width)
    seg_full = segment_ids(sent_lengths, span * blocks)
    seg_mine = lax.dynamic_slice_in_dim(seg_full, my_block * span, span, 1)
    w_queries, w_keys, w_values, proj_a, proj_b = (
        lax.all_gather(w_query, "seq", axis=0, tiled=True),
        lax.all_gather(w_key, "seq", axis=0, tiled=True),
        lax.all_gather(w_value, "seq", axis=0, tiled=True),
        lax.all_gather(shared_a, "seq", axis=0, tiled=True),
        lax.all_gather(shared_b, "seq", axis=0, tiled=True),
    )
    projected = dot_plain(token_rows, proj_a).astype(jnp.bfloat16)
    proj_float = projected.astype(jnp.float32)
    lift_q = (proj_float * scale_dq).astype(jnp.bfloat16)
    lift_v = (proj_float * scale_dv).astype(jnp.bfloat16)
    extra_q = dot_plain(lift_q, proj_b)
    extra_v = dot_plain(lift_v, proj_b)
    queries = (dot_plain(token_rows, w_queries) + shift_bq * extra_q).astype(jnp.bfloat16)
    key_rows = dot_plain(token_rows, w_keys).astype(jnp.bfloat16)
    value_rows = (dot_plain(token_rows, w_values) + shift_bv * extra_v).astype(jnp.bfloat16)
    shape4 = (row_count, span, head_count, head_size)
    query_h = queries.reshape(shape4)
    key_h = key_rows.reshape(shape4)
    value_h = value_rows.reshape(shape4)
    start_best = jnp.full((row_count, span, head_count), -1e30, jnp.float32)
    best = start_best
    key_piece = lax.all_gather(key_rows.reshape(row_count, span, width), "blk", axis=1, tiled=True)
    value_piece = lax.all_gather(
        value_rows.reshape(row_count, span, width), "blk", axis=1, tiled=True
    )
    length = key_piece.shape[1]
    key_part = key_piece.reshape(row_count, length, head_count, head_size)
    value_part = value_piece.reshape(row_count, length, head_count, head_size)
    seg_keys = seg_full
    allowed = (seg_mine[:, :, None] == seg_keys[:, None, :])[:, :, None, :]
    scores = (
        jnp.einsum("rqhd,rkhd->rqhk", query_h, key_part, preferred_element_type=jnp.float32) * 0.125
    )
    scores = jnp.where(allowed, scores, -1e30)
    new_best = jnp.maximum(best, jnp.max(scores, axis=-1))
    weight = jnp.where(allowed, jnp.exp(scores - new_best[..., None]), 0.0)
    total = jnp.sum(weight, axis=-1)
    accum = jnp.einsum(
        "rqhk,rkhd->rqhd",
        weight.astype(jnp.bfloat16),
        value_part,
        preferred_element_type=jnp.float32,
    )
    best, total, accum = (new_best, total, accum)
    log_total = best + jnp.log(total)
    context = accum / total[..., None]
    context_b = context.reshape(token_count, width).astype(jnp.bfloat16)
    w_outs, w_ins, w_backs = (
        lax.all_gather(w_out, "seq", axis=0, tiled=True),
        lax.all_gather(w_in, "seq", axis=0, tiled=True),
        lax.all_gather(w_back, "seq", axis=0, tiled=True),
    )

    def norm_first(hidden):
        return layer_norm(hidden, gain_one)

    def norm_second(hidden):
        return layer_norm(hidden, gain_two)

    resid_one = token_rows.astype(jnp.float32) + dot_plain(context_b, w_outs)
    normed_one, norm_one_pull = jax.vjp(norm_first, resid_one)
    pre_act = dot_plain(normed_one.astype(jnp.bfloat16), w_ins)
    act_float, gelu_pull = jax.vjp(exact_gelu, pre_act)
    ffn_part = dot_plain(act_float.astype(jnp.bfloat16), w_backs)
    normed_two, norm_two_pull = jax.vjp(norm_second, normed_one + ffn_part)
    layer_out = normed_two.astype(jnp.bfloat16).reshape(row_count, span, width)
    w_outs, w_ins, w_backs = (
        lax.all_gather(w_out, "seq", axis=0, tiled=True),
        lax.all_gather(w_in, "seq", axis=0, tiled=True),
        lax.all_gather(w_back, "seq", axis=0, tiled=True),
    )
    (grad_two,) = norm_two_pull(cotangent.reshape(token_count, width).astype(jnp.float32))
    act_grad = dot_trans(grad_two.astype(jnp.bfloat16), w_backs)
    (pre_grad,) = gelu_pull(act_grad)
    normed_grad = grad_two + dot_trans(pre_grad.astype(jnp.bfloat16), w_ins)
    (grad_one,) = norm_one_pull(normed_grad)
    context_grad = dot_trans(grad_one.astype(jnp.bfloat16), w_outs).astype(jnp.bfloat16)
    out_grad = context_grad.reshape(shape4)
    delta_rows = jnp.sum(out_grad.astype(jnp.float32) * context, axis=-1)
    zero_grads = jnp.zeros(shape4, jnp.float32)

    def key_step(step, carry):
        key_cur, value_cur, query_acc, key_acc, value_acc = carry
        source = (my_block - step) % blocks
        seg_keys = lax.dynamic_slice_in_dim(seg_full, source * span, span, 1)
        allowed = (seg_mine[:, :, None] == seg_keys[:, None, :])[:, :, None, :]
        q_part, k_part, v_part = block_grads(
            query_h, out_grad, log_total, delta_rows, key_cur, value_cur, allowed
        )
        key_acc, value_acc = (
            shifted((key_acc + k_part).astype(jnp.bfloat16), "blk", 1).astype(jnp.float32),
            shifted((value_acc + v_part).astype(jnp.bfloat16), "blk", 1).astype(jnp.float32),
        )
        key_cur, value_cur = shifted((key_cur, value_cur), "blk", 1)
        return (key_cur, value_cur, query_acc + q_part, key_acc, value_acc)

    looped = lax.fori_loop(
        0, blocks, key_step, (key_h, value_h, zero_grads, zero_grads, zero_grads)
    )
    query_acc, key_acc, value_acc = (looped[2], looped[3], looped[4])
    query_grad = query_acc.reshape(token_count, width).astype(jnp.bfloat16)
    key_grad = key_acc.reshape(token_count, width).astype(jnp.bfloat16)
    value_grad = value_acc.reshape(token_count, width).astype(jnp.bfloat16)
    w_queries, w_keys, w_values, proj_a, proj_b = (
        lax.all_gather(w_query, "seq", axis=0, tiled=True),
        lax.all_gather(w_key, "seq", axis=0, tiled=True),
        lax.all_gather(w_value, "seq", axis=0, tiled=True),
        lax.all_gather(shared_a, "seq", axis=0, tiled=True),
        lax.all_gather(shared_b, "seq", axis=0, tiled=True),
    )
    query_float = query_grad.astype(jnp.float32)
    value_float = value_grad.astype(jnp.float32)
    part_bq = jnp.sum(query_float * extra_q, axis=0)
    part_bv = jnp.sum(value_float * extra_v, axis=0)
    lift_q_grad = dot_trans((query_float * shift_bq).astype(jnp.bfloat16), proj_b)
    lift_v_grad = dot_trans((value_float * shift_bv).astype(jnp.bfloat16), proj_b)
    part_dq = jnp.sum(lift_q_grad * proj_float, axis=0)
    part_dv = jnp.sum(lift_v_grad * proj_float, axis=0)
    proj_grad = (lift_q_grad * scale_dq + lift_v_grad * scale_dv).astype(jnp.bfloat16)
    token_grad = (
        grad_one
        + dot_trans(query_grad, w_queries)
        + dot_trans(key_grad, w_keys)
        + dot_trans(value_grad, w_values)
        + dot_trans(proj_grad, proj_a)
    )
    grad_dq, grad_bq, grad_dv, grad_bv = lax.psum(
        (part_dq, part_bq, part_dv, part_bv), ("seq", "blk")
    )
    return (
        layer_out,
        token_grad.astype(jnp.bfloat16).reshape(row_count, span, width),
        grad_dq,
        grad_bq,
        grad_dv,
        grad_bv,
    )


def swapped(block):
    return lax.ppermute(block, "blk", [(0, 1), (1, 0)])


def summed_groups(vector):
    vector = vector + flipped(vector, 1)
    vector = vector + flipped(vector, 2)
    return (vector + flipped(vector, 4)) + (flipped(vector, 8) + flipped(vector, 12))


def body_two(
    tokens,
    sent_lengths,
    w_query,
    w_key,
    w_value,
    w_out,
    shared_a,
    shared_b,
    w_in,
    w_back,
    gain_one,
    gain_two,
    scale_dq,
    shift_bq,
    scale_dv,
    shift_bv,
    cotangent,
):
    row_count, span, width = tokens.shape
    shards = lax.axis_size("seq")
    heads = HEADS // 2
    part = heads * HEAD_DIM
    wide = 2 * HEAD_DIM
    lead, rank = shared_a.shape
    deep = shared_b.shape[0]
    cuts = w_in.shape[1] // width
    rows = range(row_count)
    spot = jnp.stack([lax.axis_index("blk"), lax.axis_index("seq")]).astype(jnp.int32)

    first, second, vecs = packed(
        spot, shared_a, w_query, w_key, w_value, shared_b, w_out, w_in, w_back,
        (scale_dq, scale_dv, shift_bq, shift_bv), part, wide,
    )
    tie = lax.optimization_barrier

    def core(block):
        return flipped(block, 1)

    other = swapped(tokens)
    lines = [flipped(first, 4), flipped(first, 8), flipped(first, 12)]
    second_over = flipped(second, 2)
    lines, second_over, second = tie((lines, second_over, second))
    quad = jnp.concatenate([first] + lines, axis=0)
    quad_over = flipped(quad, 2)
    quad_core = core(quad)
    far = far_piece(second)
    near = flipped(second, 4)
    both = jnp.concatenate([tokens, other], axis=0).reshape(2 * row_count * span, width)
    turned = both.T
    quad_over, quad_core, far, near, both, turned = tie((quad_over, quad_core, far, near, both, turned))
    down, lift, weights, merged = merge(
        spot, (quad, quad_core, quad_over, core(quad_over)), vecs, shards, lead, deep, rank, part, wide
    )
    qkv = dot_nn(both, weights).astype(bf16)
    qkv, second, second_over, far, near = tie((qkv, second, second_over, far, near))
    last = swapped(far)
    far_over = flipped(far, 2)
    near_over = flipped(second_over, 4)
    second_core, second_over_core = core(second), core(second_over)
    seen = [attend(0, spot, sent_lengths, qkv, heads, HEAD_DIM)]
    seen[0], last, far_over, near_over, second_core, second_over_core, qkv, near, far = tie(
        (seen[0], last, far_over, near_over, second_core, second_over_core, qkv, near, far)
    )
    ctx_recv = [swapped(seen[0][1])]
    last_over = flipped(last, 2)
    near_core, far_core, near_over_core = core(near), core(far), core(near_over)
    seen.append(attend(1, spot, sent_lengths, qkv, heads, HEAD_DIM))
    seen[1], ctx_recv[0], last_over, near_core, far_core, near_over_core, far_over, last = tie(
        (seen[1], ctx_recv[0], last_over, near_core, far_core, near_over_core, far_over, last)
    )
    ctx_recv.append(swapped(seen[1][1]))
    pack = [second, second_core, second_over, second_over_core, near, near_core, near_over, near_over_core]
    pack += [far, far_core, far_over, core(far_over), last, core(last), last_over, core(last_over)]
    fed = []
    for row in rows:
        before = fed[-1][:2] if fed else []
        fed.append(
            ffn(row, spot, seen[row][0], ctx_recv[row], tokens, cotangent, gain_one, gain_two, pack, before, cuts)
        )
    layer_out, grad_one = fed[-1][:2]
    grad_recv = [swapped(fed[row][3]) for row in rows]
    sent = []
    grads = []
    for row in rows:
        whole = attend_back(
            row, spot, sent_lengths, qkv, seen[row][0], seen[row][1],
            fed[row][2], grad_recv[row], seen[row][2], grads, heads, HEAD_DIM,
        )
        halves = 1 if row + 1 < row_count else 2
        each = span // halves
        partials = [
            dot_nt(whole[1, row * span + n * each : row * span + (n + 1) * each], weights).astype(bf16)
            for n in range(halves)
        ]
        if sent:
            whole, partials, sent[-1] = tie((whole, partials, sent[-1]))
        whole, partials = tie((whole, partials))
        grads = [whole]
        sent.append([swapped(partial) for partial in partials])
    whole = grads[0]
    flat = trained(spot, turned, whole.reshape(2 * row_count * span, 3 * part), merged, down, lift, vecs, wide)
    flat, sent[-1][0] = tie((flat, sent[-1][0]))
    flat = summed_groups(flat)
    base = grad_one.reshape(row_count * span, width).astype(f32) + dot_nt(whole[0], weights)
    base = base.astype(bf16)
    token_grad = []
    for row in rows[:-1]:
        token_grad = [finish(row, row_count, base, sent[row], token_grad)]
    flat, sent[-1], token_grad = tie((flat, sent[-1], token_grad))
    flat = (flat + swapped(flat)).reshape(-1)
    token_grad = finish(row_count - 1, row_count, base, sent[-1], token_grad)
    return (
        layer_out,
        token_grad,
        flat[:rank],
        flat[rank : rank + width],
        flat[rank + width : 2 * rank + width],
        flat[2 * rank + width :],
    )


def solution(mesh):
    return jax.shard_map(
        body_two if mesh.shape["blk"] == 2 and mesh.shape["seq"] == 16 else body_any,
        mesh=mesh,
        in_specs=(
            P("seq", "blk", None),
            P("seq", None),
            P("seq", None),
            P("seq", None),
            P("seq", None),
            P("seq", None),
            P("seq", None),
            P("seq", None),
            P("seq", None),
            P("seq", None),
            P(),
            P(),
            P(),
            P(),
            P(),
            P(),
            P("seq", "blk", None),
        ),
        out_specs=(P("seq", "blk", None), P("seq", "blk", None), P(), P(), P(), P()),
        check_vma=False,
    )
```

```python
import functools

import jax
import jax.numpy as jnp
from jax import lax
from jax.experimental import pallas as pl
from jax.experimental.pallas import tpu as pltpu
from jax.sharding import PartitionSpec as P

HEADS = 12
HEAD_DIM = 64
bf16 = jnp.bfloat16
f32 = jnp.float32


LN2 = 0.6931471805599453
LOG2E = 1.4426950408889634
SEGS = 5
PARTS = 3
TILE = 256
STEP = 128

def dot_nt(a,b): return lax.dot_general(a,b,(((1,),(1,)),((),())),preferred_element_type=f32)
def dot_nn(a,b): return jnp.dot(a,b,preferred_element_type=f32)

def lane_row(test, wide, kind=f32):
    lane = lax.broadcasted_iota(jnp.int32, (1, wide), 1)
    return jnp.where(test(lane), 1.0, 0.0).astype(kind)

def part_rows(wide, start):
    return [lane_row(lambda l: l == start + n, wide) for n in range(PARTS)]

def spread(column, rows):
    top = column.astype(bf16).astype(f32)
    return (top*rows[0] + (column-top)*rows[1]).astype(bf16)

def cross_ones(wide, hd):
    a = lax.broadcasted_iota(jnp.int32, (wide, wide), 0) < hd
    b = lax.broadcasted_iota(jnp.int32, (wide, wide), 1) < hd
    return jnp.where(a != b, 1.0, 0.0).astype(bf16)

def side_rows(wide, hd):
    return [lane_row(lambda l: l < hd, wide, bf16), lane_row(lambda l: l >= hd, wide, bf16)]

def bounds_of(lens, row):
    bounds = [lens[row, 0]]
    for n in range(1, SEGS-1):
        bounds.append(bounds[-1] + lens[row, n])
    return bounds

def key_span(bounds, i, span):
    low = 0
    for bound in bounds:
        low = jnp.where(bound <= i*TILE, bound, low)
    high = span
    for bound in reversed(bounds):
        high = jnp.where(bound > i*TILE + TILE-1, bound, high)
    begin = lax.div(low, STEP)
    count = lax.div(high - begin*STEP + TILE-1, TILE)
    return jnp.minimum(begin, lax.div(span - count*TILE, STEP)), count

def marks(bounds, span, wide, hd, side):
    place = lax.broadcasted_iota(jnp.int32, (span, wide), 0)
    lane = lax.broadcasted_iota(jnp.int32, (span, wide), 1) - (hd if side == 0 else 0)
    lane = jnp.where((lane >= 0) & (lane < hd), lane, hd)
    seg = jnp.zeros((span, wide), jnp.int32)
    for bound in bounds:
        seg = seg + jnp.where(place >= bound, 1, 0)
    asked = jnp.where((lane < SEGS) & (lane != seg), 1.0, 0.0).astype(bf16)
    held = jnp.where(lane == seg, -1e30, jnp.where((lane >= SEGS) & (lane < SEGS+PARTS), 1.0, 0.0)).astype(bf16)
    return asked, held

def by_half(mine, work):
    for n in range(2):
        @pl.when(mine == n)
        def _():
            work(n)

def query_tiles(bounds, span, work, broad):
    tiles = span//TILE
    fewest = tiles
    for i in range(tiles):
        fewest = jnp.minimum(fewest, key_span(bounds, i, span)[1])
    @pl.when(fewest == tiles)
    def _():
        def one(i, carry):
            work(pl.ds(pl.multiple_of(i*broad, broad), broad), slice(0, span))
            return carry
        lax.fori_loop(0, span//broad, one, 0)
    @pl.when(fewest < tiles)
    def _():
        def one(i, carry):
            rows = pl.ds(pl.multiple_of(i*TILE, TILE), TILE)
            begin, count = key_span(bounds, i, span)
            start = pl.multiple_of(begin*STEP, STEP)
            for n in range(1, tiles+1):
                @pl.when(count == n)
                def _():
                    work(rows, pl.ds(start, n*TILE) if n < tiles else slice(0, span))
            return carry
        lax.fori_loop(0, tiles, one, 0)

def attend_kernel(spot, lens, xo_ref, xp_ref, own_ref, par_ref, qa_ref, qf, kf, ka, va, og, outs, *, hd, row):
    half = xo_ref.shape[0]
    bounds = bounds_of(lens, row)
    span = 2*half
    wide = 2*hd
    sides = side_rows(wide, hd)
    swap = cross_ones(wide, hd)
    first = lax.broadcasted_iota(jnp.int32, (span, wide), 1) < hd
    start = [hd+SEGS, SEGS]
    parts = [part_rows(wide, start[s]) for s in range(2)]
    @pl.when(pl.program_id(0) == 0)
    def _():
        for s in range(2):
            qf[s], kf[s] = marks(bounds, span, wide, hd, s)
    longest = None
    for x_ref in (xo_ref, xp_ref):
        kp = x_ref[:, wide:2*wide]
        norms = jnp.max(dot_nn(kp*kp, swap), axis=0, keepdims=True)
        longest = norms if longest is None else jnp.maximum(longest, norms)
    def place(n):
        for x_ref, at in ((xo_ref, n), (xp_ref, 1-n)):
            rows = slice(at*half, (at+1)*half)
            qp = x_ref[:, 0:wide]
            kp = x_ref[:, wide:2*wide]
            vp = x_ref[:, 2*wide:3*wide]
            top = jnp.sqrt(dot_nn(qp*qp, swap) * longest) * 1.02
            for s in range(2):
                qa_ref[s, rows, :] = qp*sides[s] + (qf[s, rows, :] - (top*parts[s][0]).astype(bf16))
                ka[s, rows, :] = kp*sides[s] + kf[s, rows, :]
                va[s, rows, :] = vp*sides[s] + sides[1-s]
    by_half(spot[0], place)
    def weigh(rows, keys):
        for s in range(2):
            w = jnp.exp2(dot_nt(qa_ref[s, rows, :], ka[s, keys, :])).astype(bf16)
            og[s, rows, :] = dot_nn(w, va[s, keys, :])
    query_tiles(bounds, span, weigh, 512)
    @pl.when(jnp.logical_not(jnp.min(jnp.where(first, og[1], og[0])) > 2.0**-80))
    def _():
        def exact_tile(i, carry):
            rows = pl.ds(pl.multiple_of(i*TILE, TILE), TILE)
            for s in range(2):
                plain = qa_ref[s, rows, :] * (1.0 - parts[s][0]).astype(bf16)
                m = jnp.max(dot_nt(plain, ka[s]), axis=1, keepdims=True)
                qa_ref[s, rows, :] = plain - (jnp.broadcast_to(m, (TILE, wide))*parts[s][0]).astype(bf16)
            weigh(rows, slice(0, span))
            return carry
        lax.fori_loop(0, span//TILE, exact_tile, 0)
    total = jnp.where(first, og[1], og[0])
    outs[...] = (jnp.where(first, og[0], og[1]) / pltpu.roll(total, hd, 1)).astype(bf16)
    lse = -jnp.log2(total)
    for s in range(2):
        qa_ref[s] = qa_ref[s] + spread(lse, parts[s][1:])
    def leave(n):
        own_ref[...] = outs[n*half:(n+1)*half, :]
        par_ref[...] = outs[(1-n)*half:(2-n)*half, :]
    by_half(spot[0], leave)

def attend(row, spot, lens, qkv, heads, hd):
    count = lens.shape[0]
    half = qkv.shape[0]//(2*count); span = 2*half; mine = heads*hd; wide = 2*hd
    col = lambda p, s, l: (0, p)
    return pl.pallas_call(
        functools.partial(attend_kernel, hd=hd, row=row),
        grid_spec=pltpu.PrefetchScalarGridSpec(
            num_scalar_prefetch=2, grid=(heads//2,),
            in_specs=[pl.BlockSpec((half, 3*wide), lambda p, s, l: (row, p)), pl.BlockSpec((half, 3*wide), lambda p, s, l: (count+row, p))],
            out_specs=[
                pl.BlockSpec((half, wide), col),
                pl.BlockSpec((half, wide), col),
                pl.BlockSpec((2, span, wide), lambda p, s, l: (p, 0, 0)),
            ],
            scratch_shapes=[
                pltpu.VMEM((2, span, wide), bf16),
                pltpu.VMEM((2, span, wide), bf16),
                pltpu.VMEM((2, span, wide), bf16),
                pltpu.VMEM((2, span, wide), bf16),
                pltpu.VMEM((2, span, wide), f32),
                pltpu.VMEM((span, wide), bf16),
            ]),
        out_shape=[
            jax.ShapeDtypeStruct((half, mine), bf16),
            jax.ShapeDtypeStruct((half, mine), bf16),
            jax.ShapeDtypeStruct((heads, span, wide), bf16),
        ],
        compiler_params=pltpu.CompilerParams(vmem_limit_bytes=32<<20),
        cost_estimate=pl.CostEstimate(flops=16*span*span*mine, bytes_accessed=span*mine*12, transcendentals=span*span*heads),
    )(spot, lens, qkv, qkv)

def attend_back_kernel(spot, lens, xo_ref, xp_ref, co_ref, cp_ref, go_ref, gp_ref, qa_ref, *refs, hd, row):
    out_ref, kf, ka, va, ga, kt, kacc, vacc, qacc = refs[-9:]
    half = xo_ref.shape[0]
    bounds = bounds_of(lens, row)
    span = 2*half
    wide = 2*hd
    sides = side_rows(wide, hd)
    low = [lane_row(lambda l: (l >= hd) & (l < hd+PARTS), wide, bf16), lane_row(lambda l: l < PARTS, wide, bf16)]
    parts = [part_rows(wide, hd), part_rows(wide, 0)]
    swap = cross_ones(wide, hd)
    first = lax.broadcasted_iota(jnp.int32, (half, wide), 1) < hd
    @pl.when(pl.program_id(0) == 0)
    def _():
        for s in range(2):
            kf[s] = marks(bounds, span, wide, hd, s)[1]
    def place(n):
        for x_ref, c_ref, g_ref, at in ((xo_ref, co_ref, go_ref, n), (xp_ref, cp_ref, gp_ref, 1-n)):
            rows = slice(at*half, (at+1)*half)
            kp = x_ref[:, wide:2*wide]
            vp = x_ref[:, 2*wide:3*wide]
            gp = g_ref[...]
            kt[:, rows] = kp.T
            prod = gp.astype(f32) * c_ref[...].astype(f32)
            top = prod.astype(bf16)
            delta = dot_nn(top, swap) + dot_nn((prod - top.astype(f32)).astype(bf16), swap)
            for s in range(2):
                ka[s, rows, :] = kp*sides[s] + kf[s, rows, :]
                va[s, rows, :] = vp*sides[s] + low[s]
                ga[s, rows, :] = gp*sides[s] + spread(-delta, parts[s])
    by_half(spot[0], place)
    kacc[...] = jnp.zeros_like(kacc)
    vacc[...] = jnp.zeros_like(vacc)
    def work(rows, keys):
        for s in range(2):
            qq = qa_ref[s, rows, :]
            gg = ga[s, rows, :]
            probs = jnp.exp2(dot_nt(ka[s, keys, :], qq))
            slope = (probs * dot_nt(va[s, keys, :], gg)).astype(bf16)
            vacc[s, keys, :] += dot_nn(probs.astype(bf16), gg)
            kacc[s, keys, :] += dot_nn(slope, qq)
            qacc[s*hd:(s+1)*hd, rows] = dot_nn(kt[s*hd:(s+1)*hd, keys], slope)
    query_tiles(bounds, span, work, 2*TILE)
    def leave(n):
        for part, at in ((0, n), (1, 1-n)):
            rows = slice(at*half, (at+1)*half)
            out_ref[part, :, 0:wide] = (qacc[:, rows].T * LN2).astype(bf16)
            out_ref[part, :, wide:2*wide] = (jnp.where(first, kacc[0, rows, :], kacc[1, rows, :]) * LN2).astype(bf16)
            out_ref[part, :, 2*wide:3*wide] = jnp.where(first, vacc[0, rows, :], vacc[1, rows, :]).astype(bf16)
    by_half(spot[0], leave)

def attend_back(row, spot, lens, qkv, ctx_own, ctx_par, g_own, g_par, qa, before, heads, hd):
    count = lens.shape[0]
    half = qkv.shape[0]//(2*count); span = 2*half; mine = heads*hd; wide = 2*hd
    col = lambda p, s, l: (0, p)
    at_row = lambda p, s, l: (row, p)
    return pl.pallas_call(
        functools.partial(attend_back_kernel, hd=hd, row=row),
        grid_spec=pltpu.PrefetchScalarGridSpec(
            num_scalar_prefetch=2, grid=(heads//2,),
            in_specs=[pl.BlockSpec((half, 3*wide), at_row), pl.BlockSpec((half, 3*wide), lambda p, s, l: (count+row, p))] + [pl.BlockSpec((half, wide), col)]*4
            + [pl.BlockSpec((2, span, wide), lambda p, s, l: (p, 0, 0))] + [pl.BlockSpec(memory_space=pl.ANY)]*len(before),
            out_specs=pl.BlockSpec((2, half, 3*wide), lambda p, s, l: (0, row, p)),
            scratch_shapes=[
                pltpu.VMEM((2, span, wide), bf16),
                pltpu.VMEM((2, span, wide), bf16),
                pltpu.VMEM((2, span, wide), bf16),
                pltpu.VMEM((2, span, wide), bf16),
                pltpu.VMEM((wide, span), bf16),
                pltpu.VMEM((2, span, wide), f32),
                pltpu.VMEM((2, span, wide), f32),
                pltpu.VMEM((wide, span), f32),
            ]),
        out_shape=jax.ShapeDtypeStruct((2, count*half, 3*mine), bf16),
        input_output_aliases={9+n: n for n in range(len(before))},
        compiler_params=pltpu.CompilerParams(vmem_limit_bytes=(50 if row + 1 < count else 44)<<20),
        cost_estimate=pl.CostEstimate(flops=40*span*span*mine, bytes_accessed=span*mine*20, transcendentals=span*span*heads),
    )(spot, lens, qkv, qkv, ctx_own, ctx_par, g_own, g_par, qa, *before)


def pack_kernel(place, a_ref, q_ref, k_ref, v_ref, b_ref, out_ref, in_ref, back_ref, *refs, wide):
    vectors, (first_ref, second_ref, vecs) = refs[:-3], refs[-3:]
    vecs[...] = jnp.zeros_like(vecs)
    for n, ref in enumerate(vectors):
        vecs[n : n + 1, : ref.shape[0]] = ref[...].reshape(1, ref.shape[0])
    lead = a_ref.shape[0]
    width = out_ref.shape[1]
    row = 0
    pieces = [a_ref[:, at : at + wide] for at in range(0, a_ref.shape[1], wide)]
    for at in range(0, q_ref.shape[1], wide):
        pieces += [ref[:, at : at + wide] for ref in (q_ref, k_ref, v_ref)]
    pieces += [b_ref[:, at : at + wide] for at in range(0, b_ref.shape[1], wide)]
    for piece in pieces:
        first_ref[row : row + piece.shape[0], :] = piece
        row += piece.shape[0]
    row = 0
    pieces = [out_ref[...]]
    pieces += [in_ref[:, at : at + width] for at in range(0, in_ref.shape[1], width)]
    pieces += [back_ref[...]]
    for piece in pieces:
        second_ref[row : row + piece.shape[0], :] = piece
        row += piece.shape[0]


def packed(place, shared_a, w_query, w_key, w_value, shared_b, w_out, w_in, w_back, vectors, part, wide):
    lead, rank = shared_a.shape
    width = w_out.shape[1]
    rows = lead * (rank + 3 * part) // wide + shared_b.shape[0] * part // wide
    whole = lambda array: pl.BlockSpec(array.shape, lambda i, s: (0, 0))
    half = lambda array: pl.BlockSpec((array.shape[0], part), lambda i, s: (0, s[0]))
    total = lead + lead * w_in.shape[1] // width + w_back.shape[0]
    return pl.pallas_call(
        functools.partial(pack_kernel, wide=wide),
        grid_spec=pltpu.PrefetchScalarGridSpec(
            num_scalar_prefetch=1,
            grid=(1,),
            in_specs=[whole(shared_a), half(w_query), half(w_key), half(w_value), half(shared_b), whole(w_out), whole(w_in), whole(w_back)]
            + [pl.BlockSpec(vector.shape, lambda i, s: (0,)) for vector in vectors],
            out_specs=[pl.BlockSpec((rows, wide), lambda i, s: (0, 0)), pl.BlockSpec((total, width), lambda i, s: (0, 0)), pl.BlockSpec((8, rank), lambda i, s: (0, 0))],
        ),
        out_shape=[jax.ShapeDtypeStruct((rows, wide), bf16), jax.ShapeDtypeStruct((total, width), bf16), jax.ShapeDtypeStruct((8, rank), f32)],
        compiler_params=pltpu.CompilerParams(vmem_limit_bytes=60 << 20),
    )(place, shared_a, w_query, w_key, w_value, shared_b, w_out, w_in, w_back, *vectors)


def bent(vecs, at, side, part):
    row = vecs[at : at + 1, : 2 * part]
    return jnp.where(side == 0, row[:, :part], row[:, part:])


def merge_kernel(spot, *refs, shards, rank, part, wide):
    quads = refs[:4]
    vecs, down, lift, weights, merged, mixed = refs[4:]
    each = quads[0].shape[0] // 4
    lead = down.shape[1]
    deep = lift.shape[1]
    pairs = part // wide
    for j in range(shards):
        at = spot[1] ^ j
        piece = quads[j % 4]
        row = each * (j // 4)
        for n in range(rank // wide):
            down[at, :, n * wide : (n + 1) * wide] = piece[row : row + lead, :]
            row += lead
        for n in range(3 * pairs):
            mixed[at, :, n * wide : (n + 1) * wide] = piece[row : row + lead, :]
            row += lead
        for n in range(pairs):
            lift[at, :, n * wide : (n + 1) * wide] = piece[row : row + deep, :]
            row += deep
    low = down[...].reshape(shards * lead, rank)
    high = lift[...].reshape(shards * deep, part)
    delta_q = dot_nn(low * vecs[0:1, :].astype(bf16), high)
    merged[:, :part] = delta_q.astype(bf16)
    delta_q = delta_q * bent(vecs, 2, spot[0], part)
    delta_v = dot_nn(low * vecs[1:2, :].astype(bf16), high)
    merged[:, part:] = delta_v.astype(bf16)
    delta_v = delta_v * bent(vecs, 3, spot[0], part)
    for n in range(pairs):
        cols = slice(n * wide, (n + 1) * wide)
        base = 3 * n * wide
        get = lambda s: mixed[:, :, base + s * wide : base + (s + 1) * wide].reshape(shards * lead, wide)
        weights[:, base : base + wide] = ((get(0).astype(f32) + delta_q[:, cols]) * (0.125 * LOG2E)).astype(bf16)
        weights[:, base + wide : base + 2 * wide] = get(1)
        weights[:, base + 2 * wide : base + 3 * wide] = (get(2).astype(f32) + delta_v[:, cols]).astype(bf16)


def merge(spot, quads, vecs, shards, lead, deep, rank, part, wide):
    width = shards * lead
    whole = lambda shape: pl.BlockSpec(shape, lambda i, s: (0,) * len(shape))
    return pl.pallas_call(
        functools.partial(merge_kernel, shards=shards, rank=rank, part=part, wide=wide),
        grid_spec=pltpu.PrefetchScalarGridSpec(
            num_scalar_prefetch=1,
            grid=(1,),
            in_specs=[whole(quads[0].shape)] * 4 + [whole(vecs.shape)],
            out_specs=[whole((shards, lead, rank)), whole((shards, deep, part)), whole((width, 3 * part)), whole((width, 2 * part))],
            scratch_shapes=[pltpu.VMEM((shards, lead, 3 * part), bf16)],
        ),
        out_shape=[
            jax.ShapeDtypeStruct((shards, lead, rank), bf16),
            jax.ShapeDtypeStruct((shards, deep, part), bf16),
            jax.ShapeDtypeStruct((width, 3 * part), bf16),
            jax.ShapeDtypeStruct((width, 2 * part), bf16),
        ],
        compiler_params=pltpu.CompilerParams(vmem_limit_bytes=40 << 20),
        cost_estimate=pl.CostEstimate(flops=40 * width * rank * part, bytes_accessed=1 << 20, transcendentals=0),
    )(spot, *quads, vecs)


def flipped(block, mask):
    count = lax.axis_size("seq")
    return lax.ppermute(block, "seq", [(i, i ^ mask) for i in range(count)])


def far_piece(piece):
    count = lax.axis_size("seq")
    pairs = [(2 * i + b, 2 * (i ^ (8 + 4 * b)) + b) for i in range(count) for b in range(2)]
    return lax.ppermute(piece, ("seq", "blk"), pairs)


def spread_square(block):
    across = flipped(block, 2)
    return [block, flipped(block, 1), across, flipped(across, 1)]


def trained_kernel(
    spot, turned_ref, grad_ref, vecs, merged_hbm, down_hbm, lift_hbm, out_ref, moment, merged_ref, down_ref, lift_ref, sems,
    *, wide
):
    held = ((merged_hbm, merged_ref), (down_hbm, down_ref), (lift_hbm, lift_ref))
    lead = down_ref.shape[1]
    width = down_ref.shape[0] * lead
    rank = down_ref.shape[2]
    part = lift_ref.shape[2]
    pairs = part // wide
    picked = [grad_ref[:, (3 * n + s) * wide : (3 * n + s + 1) * wide] for s in (0, 2) for n in range(pairs)]
    added = dot_nn(turned_ref[...], jnp.concatenate(picked, axis=1))
    @pl.when(pl.program_id(0) == 0)
    def _():
        for n, (source, target) in enumerate(held):
            pltpu.make_async_copy(source, target, sems.at[n]).start()
        moment[...] = added
    @pl.when(pl.program_id(0) > 0)
    def _():
        moment[...] += added
    @pl.when(pl.program_id(0) == pl.num_programs(0) - 1)
    def _():
        for n, (source, target) in enumerate(held):
            pltpu.make_async_copy(source, target, sems.at[n]).wait()
        down = down_ref[...].reshape(width, rank).astype(f32)
        lift = lift_ref[...].reshape(rank, part)
        out_ref[...] = jnp.zeros_like(out_ref)
        base = 0
        for s, coef in ((0, 0.125 * LOG2E), (1, 1.0)):
            cols = slice(s * part, (s + 1) * part)
            shift = jnp.sum(merged_ref[:, cols].astype(f32) * moment[:, cols], axis=0, keepdims=True) * coef
            bend = bent(vecs, 2 + s, spot[0], part) * coef
            bent_moment = (moment[:, cols] * bend).astype(bf16)
            scale = jnp.sum(down * dot_nt(bent_moment, lift), axis=0, keepdims=True)
            for n in range(rank // wide):
                out_ref[base + n : base + n + 1, :] = scale[:, n * wide : (n + 1) * wide]
            base += rank // wide
            for n in range(pairs):
                out_ref[pl.ds(base + pairs * spot[0] + n, 1), :] = shift[:, n * wide : (n + 1) * wide]
            base += 2 * pairs


def trained(spot, turned, grads, merged, down, lift, vecs, wide):
    rank, part = down.shape[2], lift.shape[2]
    width, total = turned.shape
    step = total // 2
    whole = lambda array: pl.BlockSpec(array.shape, lambda i, s: (0,) * array.ndim)
    rows = 2 * (rank + 2 * part) // wide
    return pl.pallas_call(
        functools.partial(trained_kernel, wide=wide),
        grid_spec=pltpu.PrefetchScalarGridSpec(
            num_scalar_prefetch=1,
            grid=(2,),
            in_specs=[
                pl.BlockSpec((width, step), lambda i, s: (0, i)),
                pl.BlockSpec((step, grads.shape[1]), lambda i, s: (i, 0)),
            ]
            + [whole(vecs)] + [pl.BlockSpec(memory_space=pl.ANY)] * 3,
            out_specs=pl.BlockSpec((rows, wide), lambda i, s: (0, 0)),
            scratch_shapes=[pltpu.VMEM((width, 2 * part), f32)]
            + [pltpu.VMEM(array.shape, bf16) for array in (merged, down, lift)] + [pltpu.SemaphoreType.DMA((3,))],
        ),
        out_shape=jax.ShapeDtypeStruct((rows, wide), f32),
        compiler_params=pltpu.CompilerParams(vmem_limit_bytes=60 << 20),
        cost_estimate=pl.CostEstimate(flops=8 * width * total * part, bytes_accessed=12 << 20, transcendentals=0),
    )(spot, turned, grads, vecs, merged, down, lift)


def finish_kernel(turned_ref, w_ref, grad_ref, *refs):
    sent, out_ref = refs[:-1], refs[-1]
    held = grad_ref[...].astype(f32) + dot_nt(turned_ref[...], w_ref[...])
    for n, ref in enumerate(sent):
        @pl.when(pl.program_id(0) == n)
        def _():
            out_ref[...] = (held + ref[...].astype(f32)).astype(bf16)


def finish(grad_one, turned, weights, sent):
    count, span, width = grad_one.shape
    at_row = pl.BlockSpec((None, span, width), lambda i: (i, 0, 0))
    cols = turned.shape[2]
    return pl.pallas_call(
        finish_kernel,
        grid=(count,),
        in_specs=[
            pl.BlockSpec((None, span, cols), lambda i: (0, i, 0)),
            pl.BlockSpec((width, cols), lambda i: (0, 0)),
            at_row,
        ]
        + [pl.BlockSpec((span, width), lambda i: (0, 0))] * count,
        out_specs=at_row,
        out_shape=jax.ShapeDtypeStruct((count, span, width), bf16),
        compiler_params=pltpu.CompilerParams(vmem_limit_bytes=48 << 20),
    )(turned, weights, grad_one, *sent)


def centred(hidden):
    off = hidden - jnp.mean(hidden, axis=-1, keepdims=True)
    scale = lax.rsqrt(jnp.mean(off*off, axis=-1, keepdims=True) + 1e-05)
    return off*scale, scale

def norm_back(grad, unit, scale):
    inner = jnp.mean(grad*unit, axis=-1, keepdims=True)
    return scale*(grad - jnp.mean(grad, axis=-1, keepdims=True) - unit*inner)

def gelu_pair(x):
    size = jnp.abs(x)
    base = 1.0 + size*(0.3275911*0.7071067811865476)
    t = pl.reciprocal(base, approx=True)
    t = t*(2.0 - base*t)
    bell = jnp.exp2(x*x*(-0.7213475204444817))
    tail = t*(0.127414796 + t*(-0.142248368 + t*(0.7107068705 + t*(-0.7265760135 + t*0.5307027145))))*bell
    below = jnp.where(x < 0, tail, 1.0 - tail)
    return x*below, below + x*(bell*0.3989422804014327)

def ffn_kernel(spot, co_hbm, cr_hbm, x_hbm, cot_hbm, g1_ref, g2_ref, *refs, shards, cuts, row):
    pieces = refs[:shards]
    out_ref, grad_ref, own_ref, send_ref, co_ref, cr_ref, x_ref, cot_ref, wo, wi, wb, slopes, acts, sems = refs[-14:]
    width = x_ref.shape[1]
    lead = wo.shape[1]
    back = wb.shape[1]
    per = shards//cuts
    mine = spot[0]
    seat = spot[1]
    groups = [0, 4, 8 + 4*mine, 12 - 4*mine]
    ats = [seat ^ (groups[j//per] + j%per) for j in range(shards)]
    def bring(source, target, n):
        pltpu.make_async_copy(source, target, sems.at[n]).start()
    def arrived(held, n):
        pltpu.make_async_copy(held, held, sems.at[n]).wait()
    bring(co_hbm, co_ref, 1+2*cuts)
    bring(cr_hbm, cr_ref, 2+2*cuts)
    bring(x_hbm.at[row], x_ref, 3+2*cuts)
    for j in range(shards):
        bring(pieces[j].at[0:lead, :], wo.at[ats[j]], 0)
    for g in range(cuts):
        block = lax.shift_right_logical(seat ^ groups[g], 2)
        start = pl.multiple_of(lead*(1+block), 16)
        for j in range(shards):
            bring(pieces[j].at[pl.ds(start, lead), :], wi.at[g, ats[j]], 1+g)
        for j in range(g*per, (g+1)*per):
            bring(pieces[j].at[lead*(1+cuts):lead*(1+cuts)+back, :], wb.at[g*per + (ats[j] & (per-1))], 1+cuts+g)
    bring(cot_hbm.at[row], cot_ref, 4+2*cuts)
    part = shards//2
    half = width//2
    def out_rows(who):
        return wo[pl.ds(pl.multiple_of(who*part, part), part)].reshape(half, width)
    def w_in(j): return wi[j].reshape(width, width)
    def w_back(j): return wb[j*per:(j+1)*per].reshape(per*back, width)
    arrived(co_ref, 1+2*cuts)
    arrived(cr_ref, 2+2*cuts)
    arrived(x_ref, 3+2*cuts)
    arrived(wo, 0)
    resid = x_ref[...].astype(f32) + dot_nn(co_ref[...], out_rows(mine)) + dot_nn(cr_ref[...], out_rows(1-mine))
    unit_one, scale_one = centred(resid)
    gain_one = g1_ref[...].reshape(1, width)
    gain_two = g2_ref[...].reshape(1, width)
    normed = unit_one*gain_one
    low = normed.astype(bf16)
    total = normed
    for j in range(cuts):
        arrived(wi.at[j], 1+j)
        arrived(wb.at[j*per:(j+1)*per], 1+cuts+j)
    for j in range(cuts):
        for at in range(0, width, 256):
            for top in range(0, x_ref.shape[0], 256):
                act, slope = gelu_pair(dot_nn(low[top:top+256], wi[j, :, :, at:at+256].reshape(width, 256)))
                acts[top:top+256, at:at+256] = act.astype(bf16)
                slopes[j, top:top+256, at:at+256] = slope.astype(bf16)
        total = total + dot_nn(acts[...], w_back(j))
    unit_two, scale_two = centred(total)
    out_ref[...] = (unit_two*gain_two).astype(bf16)
    arrived(cot_ref, 4+2*cuts)
    grad_two = norm_back(cot_ref[...].astype(f32)*gain_two, unit_two, scale_two)
    low_two = grad_two.astype(bf16)
    grad = grad_two
    for j in range(cuts):
        pre_grad = (dot_nt(low_two, w_back(j))*slopes[j].astype(f32)).astype(bf16)
        grad = grad + dot_nt(pre_grad, w_in(j))
    grad_one = norm_back(grad*gain_one, unit_one, scale_one)
    low_one = grad_one.astype(bf16)
    grad_ref[...] = low_one
    send_ref[...] = dot_nt(low_one, out_rows(1-mine)).astype(bf16)
    own_ref[...] = dot_nt(low_one, out_rows(mine)).astype(bf16)

def ffn(row, spot, ctx_own, ctx_recv, x, cot, gain_one, gain_two, pieces, before, cuts):
    count, span, width = x.shape
    shards = len(pieces)
    lead = width//shards
    back = cuts*width//shards
    whole = lambda shape: pl.BlockSpec(shape, lambda i, s: (0,)*len(shape))
    at_row = pl.BlockSpec((None, span, width), lambda i, s: (row, 0, 0))
    anywhere = pl.BlockSpec(memory_space=pl.ANY)
    return pl.pallas_call(
        functools.partial(ffn_kernel, shards=shards, cuts=cuts, row=row),
        grid_spec=pltpu.PrefetchScalarGridSpec(
            num_scalar_prefetch=1, grid=(1,),
            in_specs=[anywhere]*4 + [whole((width,))]*2 + [anywhere]*(shards+len(before)),
            out_specs=[at_row, at_row, whole((span, width//2)), whole((span, width//2))],
            scratch_shapes=[
                pltpu.VMEM((span, width//2), bf16),
                pltpu.VMEM((span, width//2), bf16),
                pltpu.VMEM((span, width), bf16),
                pltpu.VMEM((span, width), bf16),
                pltpu.VMEM((shards, lead, width), bf16),
                pltpu.VMEM((cuts, shards, lead, width), bf16),
                pltpu.VMEM((shards, back, width), bf16),
                pltpu.VMEM((cuts, span, width), bf16),
                pltpu.VMEM((span, width), bf16),
                pltpu.SemaphoreType.DMA((5+2*cuts,)),
            ]),
        out_shape=[
            jax.ShapeDtypeStruct((count, span, width), bf16),
            jax.ShapeDtypeStruct((count, span, width), bf16),
            jax.ShapeDtypeStruct((span, width//2), bf16),
            jax.ShapeDtypeStruct((span, width//2), bf16),
        ],
        input_output_aliases={7+shards+n: n for n in range(len(before))},
        compiler_params=pltpu.CompilerParams(vmem_limit_bytes=56<<20),
        cost_estimate=pl.CostEstimate(flops=8*span*width*width*(2+4*cuts), bytes_accessed=2*(2+2*cuts)*width*width, transcendentals=2*span*width*cuts),
    )(spot, ctx_own, ctx_recv, x, cot, gain_one, gain_two, *pieces, *before)


def shifted(shard, axis, by):
    count = lax.axis_size(axis)
    return lax.ppermute(shard, axis, [(i, (i + by) % count) for i in range(count)])


def layer_norm(hidden, gain):
    centre = hidden - jnp.mean(hidden, axis=-1, keepdims=True)
    spread = jnp.mean(centre * centre, axis=-1, keepdims=True)
    return centre * lax.rsqrt(spread + 1e-05) * gain


def exact_gelu(values):
    return jax.nn.gelu(values, approximate=False)


def segment_ids(lengths, total):
    place = jnp.arange(total, dtype=jnp.int32)[None, :]
    bounds = jnp.cumsum(lengths, axis=1)
    counted = jnp.zeros((lengths.shape[0], total), jnp.int32)
    for column in range(lengths.shape[1]):
        counted = counted + (place >= bounds[:, column : column + 1]).astype(jnp.int32)
    return counted


def dot_plain(left, right):
    return jnp.dot(left, right, preferred_element_type=jnp.float32)


def dot_trans(left, right):
    return lax.dot_general(
        left, right, (((1,), (1,)), ((), ())), preferred_element_type=jnp.float32
    )


def block_grads(query_h, out_grad, lse_rows, delta_rows, key_h, value_h, allowed):
    scores = (
        jnp.einsum("rqhd,rkhd->rqhk", query_h, key_h, preferred_element_type=jnp.float32) * 0.125
    )
    probs = jnp.where(allowed, jnp.exp(scores - lse_rows[..., None]), 0.0)
    value_grad = jnp.einsum(
        "rqhk,rqhd->rkhd", probs.astype(jnp.bfloat16), out_grad, preferred_element_type=jnp.float32
    )
    prob_grad = jnp.einsum("rqhd,rkhd->rqhk", out_grad, value_h, preferred_element_type=jnp.float32)
    score_grad = (probs * (prob_grad - delta_rows[..., None])).astype(jnp.bfloat16)
    query_grad = (
        jnp.einsum("rqhk,rkhd->rqhd", score_grad, key_h, preferred_element_type=jnp.float32) * 0.125
    )
    key_grad = (
        jnp.einsum("rqhk,rqhd->rkhd", score_grad, query_h, preferred_element_type=jnp.float32)
        * 0.125
    )
    return (query_grad, key_grad, value_grad)


def body_any(
    tokens,
    sent_lengths,
    w_query,
    w_key,
    w_value,
    w_out,
    shared_a,
    shared_b,
    w_in,
    w_back,
    gain_one,
    gain_two,
    scale_dq,
    shift_bq,
    scale_dv,
    shift_bv,
    cotangent,
):
    row_count, span, width = tokens.shape
    head_count = HEADS
    head_size = HEAD_DIM
    blocks = lax.axis_size("blk")
    my_block = lax.axis_index("blk")
    token_count = row_count * span
    token_rows = tokens.reshape(token_count, width)
    seg_full = segment_ids(sent_lengths, span * blocks)
    seg_mine = lax.dynamic_slice_in_dim(seg_full, my_block * span, span, 1)
    w_queries, w_keys, w_values, proj_a, proj_b = (
        lax.all_gather(w_query, "seq", axis=0, tiled=True),
        lax.all_gather(w_key, "seq", axis=0, tiled=True),
        lax.all_gather(w_value, "seq", axis=0, tiled=True),
        lax.all_gather(shared_a, "seq", axis=0, tiled=True),
        lax.all_gather(shared_b, "seq", axis=0, tiled=True),
    )
    projected = dot_plain(token_rows, proj_a).astype(jnp.bfloat16)
    proj_float = projected.astype(jnp.float32)
    lift_q = (proj_float * scale_dq).astype(jnp.bfloat16)
    lift_v = (proj_float * scale_dv).astype(jnp.bfloat16)
    extra_q = dot_plain(lift_q, proj_b)
    extra_v = dot_plain(lift_v, proj_b)
    queries = (dot_plain(token_rows, w_queries) + shift_bq * extra_q).astype(jnp.bfloat16)
    key_rows = dot_plain(token_rows, w_keys).astype(jnp.bfloat16)
    value_rows = (dot_plain(token_rows, w_values) + shift_bv * extra_v).astype(jnp.bfloat16)
    shape4 = (row_count, span, head_count, head_size)
    query_h = queries.reshape(shape4)
    key_h = key_rows.reshape(shape4)
    value_h = value_rows.reshape(shape4)
    start_best = jnp.full((row_count, span, head_count), -1e30, jnp.float32)
    best = start_best
    key_piece = lax.all_gather(key_rows.reshape(row_count, span, width), "blk", axis=1, tiled=True)
    value_piece = lax.all_gather(
        value_rows.reshape(row_count, span, width), "blk", axis=1, tiled=True
    )
    length = key_piece.shape[1]
    key_part = key_piece.reshape(row_count, length, head_count, head_size)
    value_part = value_piece.reshape(row_count, length, head_count, head_size)
    seg_keys = seg_full
    allowed = (seg_mine[:, :, None] == seg_keys[:, None, :])[:, :, None, :]
    scores = (
        jnp.einsum("rqhd,rkhd->rqhk", query_h, key_part, preferred_element_type=jnp.float32) * 0.125
    )
    scores = jnp.where(allowed, scores, -1e30)
    new_best = jnp.maximum(best, jnp.max(scores, axis=-1))
    weight = jnp.where(allowed, jnp.exp(scores - new_best[..., None]), 0.0)
    total = jnp.sum(weight, axis=-1)
    accum = jnp.einsum(
        "rqhk,rkhd->rqhd",
        weight.astype(jnp.bfloat16),
        value_part,
        preferred_element_type=jnp.float32,
    )
    best, total, accum = (new_best, total, accum)
    log_total = best + jnp.log(total)
    context = accum / total[..., None]
    context_b = context.reshape(token_count, width).astype(jnp.bfloat16)
    w_outs, w_ins, w_backs = (
        lax.all_gather(w_out, "seq", axis=0, tiled=True),
        lax.all_gather(w_in, "seq", axis=0, tiled=True),
        lax.all_gather(w_back, "seq", axis=0, tiled=True),
    )

    def norm_first(hidden):
        return layer_norm(hidden, gain_one)

    def norm_second(hidden):
        return layer_norm(hidden, gain_two)

    resid_one = token_rows.astype(jnp.float32) + dot_plain(context_b, w_outs)
    normed_one, norm_one_pull = jax.vjp(norm_first, resid_one)
    pre_act = dot_plain(normed_one.astype(jnp.bfloat16), w_ins)
    act_float, gelu_pull = jax.vjp(exact_gelu, pre_act)
    ffn_part = dot_plain(act_float.astype(jnp.bfloat16), w_backs)
    normed_two, norm_two_pull = jax.vjp(norm_second, normed_one + ffn_part)
    layer_out = normed_two.astype(jnp.bfloat16).reshape(row_count, span, width)
    w_outs, w_ins, w_backs = (
        lax.all_gather(w_out, "seq", axis=0, tiled=True),
        lax.all_gather(w_in, "seq", axis=0, tiled=True),
        lax.all_gather(w_back, "seq", axis=0, tiled=True),
    )
    (grad_two,) = norm_two_pull(cotangent.reshape(token_count, width).astype(jnp.float32))
    act_grad = dot_trans(grad_two.astype(jnp.bfloat16), w_backs)
    (pre_grad,) = gelu_pull(act_grad)
    normed_grad = grad_two + dot_trans(pre_grad.astype(jnp.bfloat16), w_ins)
    (grad_one,) = norm_one_pull(normed_grad)
    context_grad = dot_trans(grad_one.astype(jnp.bfloat16), w_outs).astype(jnp.bfloat16)
    out_grad = context_grad.reshape(shape4)
    delta_rows = jnp.sum(out_grad.astype(jnp.float32) * context, axis=-1)
    zero_grads = jnp.zeros(shape4, jnp.float32)

    def key_step(step, carry):
        key_cur, value_cur, query_acc, key_acc, value_acc = carry
        source = (my_block - step) % blocks
        seg_keys = lax.dynamic_slice_in_dim(seg_full, source * span, span, 1)
        allowed = (seg_mine[:, :, None] == seg_keys[:, None, :])[:, :, None, :]
        q_part, k_part, v_part = block_grads(
            query_h, out_grad, log_total, delta_rows, key_cur, value_cur, allowed
        )
        key_acc, value_acc = (
            shifted((key_acc + k_part).astype(jnp.bfloat16), "blk", 1).astype(jnp.float32),
            shifted((value_acc + v_part).astype(jnp.bfloat16), "blk", 1).astype(jnp.float32),
        )
        key_cur, value_cur = shifted((key_cur, value_cur), "blk", 1)
        return (key_cur, value_cur, query_acc + q_part, key_acc, value_acc)

    looped = lax.fori_loop(
        0, blocks, key_step, (key_h, value_h, zero_grads, zero_grads, zero_grads)
    )
    query_acc, key_acc, value_acc = (looped[2], looped[3], looped[4])
    query_grad = query_acc.reshape(token_count, width).astype(jnp.bfloat16)
    key_grad = key_acc.reshape(token_count, width).astype(jnp.bfloat16)
    value_grad = value_acc.reshape(token_count, width).astype(jnp.bfloat16)
    w_queries, w_keys, w_values, proj_a, proj_b = (
        lax.all_gather(w_query, "seq", axis=0, tiled=True),
        lax.all_gather(w_key, "seq", axis=0, tiled=True),
        lax.all_gather(w_value, "seq", axis=0, tiled=True),
        lax.all_gather(shared_a, "seq", axis=0, tiled=True),
        lax.all_gather(shared_b, "seq", axis=0, tiled=True),
    )
    query_float = query_grad.astype(jnp.float32)
    value_float = value_grad.astype(jnp.float32)
    part_bq = jnp.sum(query_float * extra_q, axis=0)
    part_bv = jnp.sum(value_float * extra_v, axis=0)
    lift_q_grad = dot_trans((query_float * shift_bq).astype(jnp.bfloat16), proj_b)
    lift_v_grad = dot_trans((value_float * shift_bv).astype(jnp.bfloat16), proj_b)
    part_dq = jnp.sum(lift_q_grad * proj_float, axis=0)
    part_dv = jnp.sum(lift_v_grad * proj_float, axis=0)
    proj_grad = (lift_q_grad * scale_dq + lift_v_grad * scale_dv).astype(jnp.bfloat16)
    token_grad = (
        grad_one
        + dot_trans(query_grad, w_queries)
        + dot_trans(key_grad, w_keys)
        + dot_trans(value_grad, w_values)
        + dot_trans(proj_grad, proj_a)
    )
    grad_dq, grad_bq, grad_dv, grad_bv = lax.psum(
        (part_dq, part_bq, part_dv, part_bv), ("seq", "blk")
    )
    return (
        layer_out,
        token_grad.astype(jnp.bfloat16).reshape(row_count, span, width),
        grad_dq,
        grad_bq,
        grad_dv,
        grad_bv,
    )


def swapped(block):
    return lax.ppermute(block, "blk", [(0, 1), (1, 0)])


def body_two(
    tokens,
    sent_lengths,
    w_query,
    w_key,
    w_value,
    w_out,
    shared_a,
    shared_b,
    w_in,
    w_back,
    gain_one,
    gain_two,
    scale_dq,
    shift_bq,
    scale_dv,
    shift_bv,
    cotangent,
):
    row_count, span, width = tokens.shape
    shards = lax.axis_size("seq")
    heads = HEADS // 2
    part = heads * HEAD_DIM
    wide = 2 * HEAD_DIM
    lead, rank = shared_a.shape
    deep = shared_b.shape[0]
    cuts = w_in.shape[1] // width
    rows = range(row_count)
    spot = jnp.stack([lax.axis_index("blk"), lax.axis_index("seq")]).astype(jnp.int32)

    first, second, vecs = packed(
        spot, shared_a, w_query, w_key, w_value, shared_b, w_out, w_in, w_back,
        (scale_dq, scale_dv, shift_bq, shift_bv), part, wide,
    )
    tie = lax.optimization_barrier

    def core(block):
        return flipped(block, 1)

    other = swapped(tokens)
    lines = [flipped(first, 4), flipped(first, 8), flipped(first, 12)]
    second_over = flipped(second, 2)
    lines, second_over, second = tie((lines, second_over, second))
    quad = jnp.concatenate([first] + lines, axis=0)
    quad_over = flipped(quad, 2)
    quad_core = core(quad)
    far = far_piece(second)
    near = flipped(second, 4)
    both = jnp.concatenate([tokens, other], axis=0).reshape(2 * row_count * span, width)
    turned = both.T
    quad_over, quad_core, far, near, both, turned = tie((quad_over, quad_core, far, near, both, turned))
    down, lift, weights, merged = merge(
        spot, (quad, quad_core, quad_over, core(quad_over)), vecs, shards, lead, deep, rank, part, wide
    )
    qkv = dot_nn(both, weights).astype(bf16)
    near_core, far_core = core(near), core(far)
    qkv, second, second_over, far, near, near_core, far_core = tie(
        (qkv, second, second_over, far, near, near_core, far_core)
    )
    last = swapped(far)
    far_over = flipped(far, 2)
    near_over = flipped(second_over, 4)
    second_core, second_over_core = core(second), core(second_over)
    seen = [attend(0, spot, sent_lengths, qkv, heads, HEAD_DIM)]
    seen[0], last, far_over, near_over, second_core, second_over_core, qkv, near, far = tie(
        (seen[0], last, far_over, near_over, second_core, second_over_core, qkv, near, far)
    )
    ctx_recv = [swapped(seen[0][1])]
    last_over = flipped(last, 2)
    near_over_core, far_over_core, last_core = core(near_over), core(far_over), core(last)
    seen.append(attend(1, spot, sent_lengths, qkv, heads, HEAD_DIM))
    seen[1], ctx_recv[0], last_over, near_over_core, far_over_core, last_core = tie(
        (seen[1], ctx_recv[0], last_over, near_over_core, far_over_core, last_core)
    )
    ctx_recv.append(swapped(seen[1][1]))
    pack = [second, second_core, second_over, second_over_core, near, near_core, near_over, near_over_core]
    pack += [far, far_core, far_over, far_over_core, last, last_core, last_over, core(last_over)]
    fed = []
    for row in rows:
        before = fed[-1][:2] if fed else []
        fed.append(
            ffn(row, spot, seen[row][0], ctx_recv[row], tokens, cotangent, gain_one, gain_two, pack, before, cuts)
        )
    layer_out, grad_one = fed[-1][:2]
    grad_recv = [swapped(fed[row][3]) for row in rows]
    sent = []
    grads = []
    for row in rows:
        whole = attend_back(
            row, spot, sent_lengths, qkv, seen[row][0], seen[row][1],
            fed[row][2], grad_recv[row], seen[row][2], grads, heads, HEAD_DIM,
        )
        partial = dot_nt(whole[1, row * span : (row + 1) * span], weights).astype(bf16)
        if sent:
            whole, partial, sent[-1] = tie((whole, partial, sent[-1]))
        whole, partial = tie((whole, partial))
        grads = [whole]
        sent.append(swapped(partial))
    flat = trained(
        spot, turned, whole.reshape(2 * row_count * span, 3 * part), merged, down, lift, vecs, wide
    )
    flat = flat + core(flat)
    flat = flat + flipped(flat, 2)
    level, far_levels = flipped(flat, 4), flipped(flat, 8) + flipped(flat, 12)
    level, sent[-1] = tie((level, sent[-1]))
    flat = (flat + level) + far_levels
    flat = (flat + swapped(flat)).reshape(-1)
    token_grad = finish(grad_one, whole, weights, sent)
    return (
        layer_out,
        token_grad,
        flat[:rank],
        flat[rank : rank + width],
        flat[rank + width : 2 * rank + width],
        flat[2 * rank + width :],
    )


def solution(mesh):
    return jax.shard_map(
        body_two if mesh.shape["blk"] == 2 and mesh.shape["seq"] == 16 else body_any,
        mesh=mesh,
        in_specs=(
            P("seq", "blk", None),
            P("seq", None),
            P("seq", None),
            P("seq", None),
            P("seq", None),
            P("seq", None),
            P("seq", None),
            P("seq", None),
            P("seq", None),
            P("seq", None),
            P(),
            P(),
            P(),
            P(),
            P(),
            P(),
            P("seq", "blk", None),
        ),
        out_specs=(P("seq", "blk", None), P("seq", "blk", None), P(), P(), P(), P()),
        check_vma=False,
    )
```

```python
import functools

import jax
import jax.numpy as jnp
from jax import lax
from jax.experimental import pallas as pl
from jax.experimental.pallas import tpu as pltpu
from jax.sharding import PartitionSpec as P

HEADS = 12
HEAD_DIM = 64
bf16 = jnp.bfloat16
f32 = jnp.float32


LN2 = 0.6931471805599453
LOG2E = 1.4426950408889634
SEGS = 5
PARTS = 5
TILE = 256
STEP = 128

def dot_nt(a,b): return lax.dot_general(a,b,(((1,),(1,)),((),())),preferred_element_type=f32)
def dot_nn(a,b): return jnp.dot(a,b,preferred_element_type=f32)

def lane_row(test, wide, kind=f32):
    lane = lax.broadcasted_iota(jnp.int32, (1, wide), 1)
    return jnp.where(test(lane), 1.0, 0.0).astype(kind)

def part_rows(wide, start):
    return [lane_row(lambda l: l == start + n, wide) for n in range(PARTS)]

def spread(column, rows):
    total = 0.0
    for n, row in enumerate(rows):
        piece = column if n + 1 == len(rows) else column.astype(bf16).astype(f32)
        total = total + piece*row
        column = column - piece
    return total.astype(bf16)

def cross_ones(wide, hd):
    a = lax.broadcasted_iota(jnp.int32, (wide, wide), 0) < hd
    b = lax.broadcasted_iota(jnp.int32, (wide, wide), 1) < hd
    return jnp.where(a != b, 1.0, 0.0).astype(bf16)

def side_rows(wide, hd):
    return [lane_row(lambda l: l < hd, wide, bf16), lane_row(lambda l: l >= hd, wide, bf16)]

def bounds_of(lens, row):
    bounds = [lens[row, 0]]
    for n in range(1, SEGS-1):
        bounds.append(bounds[-1] + lens[row, n])
    return bounds

def key_span(bounds, i, span):
    low = 0
    for bound in bounds:
        low = jnp.where(bound <= i*TILE, bound, low)
    high = span
    for bound in reversed(bounds):
        high = jnp.where(bound > i*TILE + TILE-1, bound, high)
    begin = lax.div(low, STEP)
    count = lax.div(high - begin*STEP + TILE-1, TILE)
    return jnp.minimum(begin, lax.div(span - count*TILE, STEP)), count

def marks(bounds, span, wide, hd, side):
    place = lax.broadcasted_iota(jnp.int32, (span, wide), 0)
    lane = lax.broadcasted_iota(jnp.int32, (span, wide), 1) - (hd if side == 0 else 0)
    lane = jnp.where((lane >= 0) & (lane < hd), lane, hd)
    seg = jnp.zeros((span, wide), jnp.int32)
    for bound in bounds:
        seg = seg + jnp.where(place >= bound, 1, 0)
    asked = jnp.where((lane < SEGS) & (lane != seg), 1.0, 0.0).astype(bf16)
    held = jnp.where(lane == seg, -1e30, jnp.where((lane >= SEGS) & (lane < SEGS+PARTS), 1.0, 0.0)).astype(bf16)
    return asked, held

def by_half(mine, work):
    for n in range(2):
        @pl.when(mine == n)
        def _():
            work(n)

def query_tiles(bounds, span, work, broad):
    tiles = span//TILE
    fewest = tiles
    for i in range(tiles):
        fewest = jnp.minimum(fewest, key_span(bounds, i, span)[1])
    @pl.when(fewest == tiles)
    def _():
        def one(i, carry):
            work(pl.ds(pl.multiple_of(i*broad, broad), broad), slice(0, span))
            return carry
        lax.fori_loop(0, span//broad, one, 0)
    @pl.when(fewest < tiles)
    def _():
        def one(i, carry):
            rows = pl.ds(pl.multiple_of(i*TILE, TILE), TILE)
            begin, count = key_span(bounds, i, span)
            start = pl.multiple_of(begin*STEP, STEP)
            for n in range(1, tiles+1):
                @pl.when(count == n)
                def _():
                    work(rows, pl.ds(start, n*TILE) if n < tiles else slice(0, span))
            return carry
        lax.fori_loop(0, tiles, one, 0)

def attend_kernel(spot, lens, xo_ref, xp_ref, own_ref, par_ref, qa_ref, qf, kf, ka, va, og, outs, *, hd, row):
    half = xo_ref.shape[0]
    bounds = bounds_of(lens, row)
    span = 2*half
    wide = 2*hd
    sides = side_rows(wide, hd)
    swap = cross_ones(wide, hd)
    first = lax.broadcasted_iota(jnp.int32, (span, wide), 1) < hd
    start = [hd+SEGS, SEGS]
    parts = [part_rows(wide, start[s]) for s in range(2)]
    @pl.when(pl.program_id(0) == 0)
    def _():
        for s in range(2):
            qf[s], kf[s] = marks(bounds, span, wide, hd, s)
    longest = None
    for x_ref in (xo_ref, xp_ref):
        kp = x_ref[:, wide:2*wide]
        norms = jnp.max(dot_nn(kp*kp, swap), axis=0, keepdims=True)
        longest = norms if longest is None else jnp.maximum(longest, norms)
    def place(n):
        for x_ref, at in ((xo_ref, n), (xp_ref, 1-n)):
            rows = slice(at*half, (at+1)*half)
            qp = x_ref[:, 0:wide]
            kp = x_ref[:, wide:2*wide]
            vp = x_ref[:, 2*wide:3*wide]
            top = jnp.sqrt(dot_nn(qp*qp, swap) * longest) * 1.02
            for s in range(2):
                qa_ref[s, rows, :] = qp*sides[s] + (qf[s, rows, :] - (top*parts[s][0]).astype(bf16))
                ka[s, rows, :] = kp*sides[s] + kf[s, rows, :]
                va[s, rows, :] = vp*sides[s] + sides[1-s]
    by_half(spot[0], place)
    def weigh(rows, keys):
        for s in range(2):
            w = jnp.exp2(dot_nt(qa_ref[s, rows, :], ka[s, keys, :])).astype(bf16)
            og[s, rows, :] = dot_nn(w, va[s, keys, :])
    query_tiles(bounds, span, weigh, 512)
    @pl.when(jnp.logical_not(jnp.min(jnp.where(first, og[1], og[0])) > 2.0**-80))
    def _():
        def exact_tile(i, carry):
            rows = pl.ds(pl.multiple_of(i*TILE, TILE), TILE)
            for s in range(2):
                plain = qa_ref[s, rows, :] * (1.0 - parts[s][0]).astype(bf16)
                m = jnp.max(dot_nt(plain, ka[s]), axis=1, keepdims=True)
                qa_ref[s, rows, :] = plain + spread(-jnp.broadcast_to(m, (TILE, wide)), parts[s][:3])
            weigh(rows, slice(0, span))
            return carry
        lax.fori_loop(0, span//TILE, exact_tile, 0)
    total = jnp.where(first, og[1], og[0])
    outs[...] = (jnp.where(first, og[0], og[1]) / pltpu.roll(total, hd, 1)).astype(bf16)
    lse = -jnp.log2(total)
    for s in range(2):
        qa_ref[s] = qa_ref[s] + spread(lse, parts[s][3:])
    def leave(n):
        own_ref[...] = outs[n*half:(n+1)*half, :]
        par_ref[...] = outs[(1-n)*half:(2-n)*half, :]
    by_half(spot[0], leave)

def attend(row, spot, lens, qkv, heads, hd):
    count = lens.shape[0]
    half = qkv.shape[0]//(2*count); span = 2*half; mine = heads*hd; wide = 2*hd
    col = lambda p, s, l: (0, p)
    return pl.pallas_call(
        functools.partial(attend_kernel, hd=hd, row=row),
        grid_spec=pltpu.PrefetchScalarGridSpec(
            num_scalar_prefetch=2, grid=(heads//2,),
            in_specs=[pl.BlockSpec((half, 3*wide), lambda p, s, l: (row, p)), pl.BlockSpec((half, 3*wide), lambda p, s, l: (count+row, p))],
            out_specs=[
                pl.BlockSpec((half, wide), col),
                pl.BlockSpec((half, wide), col),
                pl.BlockSpec((2, span, wide), lambda p, s, l: (p, 0, 0)),
            ],
            scratch_shapes=[
                pltpu.VMEM((2, span, wide), bf16),
                pltpu.VMEM((2, span, wide), bf16),
                pltpu.VMEM((2, span, wide), bf16),
                pltpu.VMEM((2, span, wide), bf16),
                pltpu.VMEM((2, span, wide), f32),
                pltpu.VMEM((span, wide), bf16),
            ]),
        out_shape=[
            jax.ShapeDtypeStruct((half, mine), bf16),
            jax.ShapeDtypeStruct((half, mine), bf16),
            jax.ShapeDtypeStruct((heads, span, wide), bf16),
        ],
        compiler_params=pltpu.CompilerParams(vmem_limit_bytes=32<<20),
        cost_estimate=pl.CostEstimate(flops=16*span*span*mine, bytes_accessed=span*mine*12, transcendentals=span*span*heads),
    )(spot, lens, qkv, qkv)

def attend_back_kernel(spot, lens, xo_ref, xp_ref, co_ref, cp_ref, go_ref, gp_ref, qa_ref, *refs, hd, row):
    out_ref, kf, ka, va, ga, kt, kacc, vacc, qacc = refs[-9:]
    half = xo_ref.shape[0]
    bounds = bounds_of(lens, row)
    span = 2*half
    wide = 2*hd
    sides = side_rows(wide, hd)
    low = [lane_row(lambda l: (l >= hd) & (l < hd+PARTS), wide, bf16), lane_row(lambda l: l < PARTS, wide, bf16)]
    parts = [part_rows(wide, hd), part_rows(wide, 0)]
    swap = cross_ones(wide, hd)
    first = lax.broadcasted_iota(jnp.int32, (half, wide), 1) < hd
    @pl.when(pl.program_id(0) == 0)
    def _():
        for s in range(2):
            kf[s] = marks(bounds, span, wide, hd, s)[1]
    def place(n):
        for x_ref, c_ref, g_ref, at in ((xo_ref, co_ref, go_ref, n), (xp_ref, cp_ref, gp_ref, 1-n)):
            rows = slice(at*half, (at+1)*half)
            kp = x_ref[:, wide:2*wide]
            vp = x_ref[:, 2*wide:3*wide]
            gp = g_ref[...]
            kt[:, rows] = kp.T
            prod = gp.astype(f32) * c_ref[...].astype(f32)
            top = prod.astype(bf16)
            delta = dot_nn(top, swap) + dot_nn((prod - top.astype(f32)).astype(bf16), swap)
            for s in range(2):
                ka[s, rows, :] = kp*sides[s] + kf[s, rows, :]
                va[s, rows, :] = vp*sides[s] + low[s]
                ga[s, rows, :] = gp*sides[s] + spread(-delta, parts[s][:2])
    by_half(spot[0], place)
    kacc[...] = jnp.zeros_like(kacc)
    vacc[...] = jnp.zeros_like(vacc)
    def work(rows, keys):
        for s in range(2):
            qq = qa_ref[s, rows, :]
            gg = ga[s, rows, :]
            probs = jnp.exp2(dot_nt(ka[s, keys, :], qq))
            slope = (probs * dot_nt(va[s, keys, :], gg)).astype(bf16)
            vacc[s, keys, :] += dot_nn(probs.astype(bf16), gg)
            kacc[s, keys, :] += dot_nn(slope, qq)
            qacc[s*hd:(s+1)*hd, rows] = dot_nn(kt[s*hd:(s+1)*hd, keys], slope)
    query_tiles(bounds, span, work, 2*TILE)
    def leave(n):
        for part, at in ((0, n), (1, 1-n)):
            rows = slice(at*half, (at+1)*half)
            out_ref[part, :, 0:wide] = (qacc[:, rows].T * LN2).astype(bf16)
            out_ref[part, :, wide:2*wide] = (jnp.where(first, kacc[0, rows, :], kacc[1, rows, :]) * LN2).astype(bf16)
            out_ref[part, :, 2*wide:3*wide] = jnp.where(first, vacc[0, rows, :], vacc[1, rows, :]).astype(bf16)
    by_half(spot[0], leave)

def attend_back(row, spot, lens, qkv, ctx_own, ctx_par, g_own, g_par, qa, before, heads, hd):
    count = lens.shape[0]
    half = qkv.shape[0]//(2*count); span = 2*half; mine = heads*hd; wide = 2*hd
    col = lambda p, s, l: (0, p)
    at_row = lambda p, s, l: (row, p)
    return pl.pallas_call(
        functools.partial(attend_back_kernel, hd=hd, row=row),
        grid_spec=pltpu.PrefetchScalarGridSpec(
            num_scalar_prefetch=2, grid=(heads//2,),
            in_specs=[pl.BlockSpec((half, 3*wide), at_row), pl.BlockSpec((half, 3*wide), lambda p, s, l: (count+row, p))] + [pl.BlockSpec((half, wide), col)]*4
            + [pl.BlockSpec((2, span, wide), lambda p, s, l: (p, 0, 0))] + [pl.BlockSpec(memory_space=pl.ANY)]*len(before),
            out_specs=pl.BlockSpec((2, half, 3*wide), lambda p, s, l: (0, row, p)),
            scratch_shapes=[
                pltpu.VMEM((2, span, wide), bf16),
                pltpu.VMEM((2, span, wide), bf16),
                pltpu.VMEM((2, span, wide), bf16),
                pltpu.VMEM((2, span, wide), bf16),
                pltpu.VMEM((wide, span), bf16),
                pltpu.VMEM((2, span, wide), f32),
                pltpu.VMEM((2, span, wide), f32),
                pltpu.VMEM((wide, span), f32),
            ]),
        out_shape=jax.ShapeDtypeStruct((2, count*half, 3*mine), bf16),
        input_output_aliases={9+n: n for n in range(len(before))},
        compiler_params=pltpu.CompilerParams(vmem_limit_bytes=(50 if row + 1 < count else 44)<<20),
        cost_estimate=pl.CostEstimate(flops=40*span*span*mine, bytes_accessed=span*mine*20, transcendentals=span*span*heads),
    )(spot, lens, qkv, qkv, ctx_own, ctx_par, g_own, g_par, qa, *before)


def pack_kernel(place, a_ref, q_ref, k_ref, v_ref, b_ref, out_ref, in_ref, back_ref, *refs, wide):
    vectors, (first_ref, second_ref, vecs) = refs[:-3], refs[-3:]
    vecs[...] = jnp.zeros_like(vecs)
    for n, ref in enumerate(vectors):
        vecs[n : n + 1, : ref.shape[0]] = ref[...].reshape(1, ref.shape[0])
    lead = a_ref.shape[0]
    width = out_ref.shape[1]
    row = 0
    pieces = [a_ref[:, at : at + wide] for at in range(0, a_ref.shape[1], wide)]
    for at in range(0, q_ref.shape[1], wide):
        pieces += [ref[:, at : at + wide] for ref in (q_ref, k_ref, v_ref)]
    pieces += [b_ref[:, at : at + wide] for at in range(0, b_ref.shape[1], wide)]
    for piece in pieces:
        first_ref[row : row + piece.shape[0], :] = piece
        row += piece.shape[0]
    row = 0
    pieces = [out_ref[...]]
    pieces += [in_ref[:, at : at + width] for at in range(0, in_ref.shape[1], width)]
    pieces += [back_ref[...]]
    for piece in pieces:
        second_ref[row : row + piece.shape[0], :] = piece
        row += piece.shape[0]


def packed(place, shared_a, w_query, w_key, w_value, shared_b, w_out, w_in, w_back, vectors, part, wide):
    lead, rank = shared_a.shape
    width = w_out.shape[1]
    rows = lead * (rank + 3 * part) // wide + shared_b.shape[0] * part // wide
    whole = lambda array: pl.BlockSpec(array.shape, lambda i, s: (0, 0))
    half = lambda array: pl.BlockSpec((array.shape[0], part), lambda i, s: (0, s[0]))
    total = lead + lead * w_in.shape[1] // width + w_back.shape[0]
    return pl.pallas_call(
        functools.partial(pack_kernel, wide=wide),
        grid_spec=pltpu.PrefetchScalarGridSpec(
            num_scalar_prefetch=1,
            grid=(1,),
            in_specs=[whole(shared_a), half(w_query), half(w_key), half(w_value), half(shared_b), whole(w_out), whole(w_in), whole(w_back)]
            + [pl.BlockSpec(vector.shape, lambda i, s: (0,)) for vector in vectors],
            out_specs=[pl.BlockSpec((rows, wide), lambda i, s: (0, 0)), pl.BlockSpec((total, width), lambda i, s: (0, 0)), pl.BlockSpec((8, rank), lambda i, s: (0, 0))],
        ),
        out_shape=[jax.ShapeDtypeStruct((rows, wide), bf16), jax.ShapeDtypeStruct((total, width), bf16), jax.ShapeDtypeStruct((8, rank), f32)],
        compiler_params=pltpu.CompilerParams(vmem_limit_bytes=60 << 20),
    )(place, shared_a, w_query, w_key, w_value, shared_b, w_out, w_in, w_back, *vectors)


def bent(vecs, at, side, part):
    row = vecs[at : at + 1, : 2 * part]
    return jnp.where(side == 0, row[:, :part], row[:, part:])


def merge_kernel(spot, *refs, shards, rank, part, wide):
    quads = refs[:4]
    vecs, down, lift, weights, merged, mixed = refs[4:]
    each = quads[0].shape[0] // 4
    lead = down.shape[1]
    deep = lift.shape[1]
    pairs = part // wide
    for j in range(shards):
        at = spot[1] ^ j
        piece = quads[j % 4]
        row = each * (j // 4)
        for n in range(rank // wide):
            down[at, :, n * wide : (n + 1) * wide] = piece[row : row + lead, :]
            row += lead
        for n in range(3 * pairs):
            mixed[at, :, n * wide : (n + 1) * wide] = piece[row : row + lead, :]
            row += lead
        for n in range(pairs):
            lift[at, :, n * wide : (n + 1) * wide] = piece[row : row + deep, :]
            row += deep
    low = down[...].reshape(shards * lead, rank)
    high = lift[...].reshape(shards * deep, part)
    delta_q = dot_nn(low * vecs[0:1, :].astype(bf16), high)
    merged[:, :part] = delta_q.astype(bf16)
    delta_q = delta_q * bent(vecs, 2, spot[0], part)
    delta_v = dot_nn(low * vecs[1:2, :].astype(bf16), high)
    merged[:, part:] = delta_v.astype(bf16)
    delta_v = delta_v * bent(vecs, 3, spot[0], part)
    for n in range(pairs):
        cols = slice(n * wide, (n + 1) * wide)
        base = 3 * n * wide
        get = lambda s: mixed[:, :, base + s * wide : base + (s + 1) * wide].reshape(shards * lead, wide)
        weights[:, base : base + wide] = ((get(0).astype(f32) + delta_q[:, cols]) * (0.125 * LOG2E)).astype(bf16)
        weights[:, base + wide : base + 2 * wide] = get(1)
        weights[:, base + 2 * wide : base + 3 * wide] = (get(2).astype(f32) + delta_v[:, cols]).astype(bf16)


def merge(spot, quads, vecs, shards, lead, deep, rank, part, wide):
    width = shards * lead
    whole = lambda shape: pl.BlockSpec(shape, lambda i, s: (0,) * len(shape))
    return pl.pallas_call(
        functools.partial(merge_kernel, shards=shards, rank=rank, part=part, wide=wide),
        grid_spec=pltpu.PrefetchScalarGridSpec(
            num_scalar_prefetch=1,
            grid=(1,),
            in_specs=[whole(quads[0].shape)] * 4 + [whole(vecs.shape)],
            out_specs=[whole((shards, lead, rank)), whole((shards, deep, part)), whole((width, 3 * part)), whole((width, 2 * part))],
            scratch_shapes=[pltpu.VMEM((shards, lead, 3 * part), bf16)],
        ),
        out_shape=[
            jax.ShapeDtypeStruct((shards, lead, rank), bf16),
            jax.ShapeDtypeStruct((shards, deep, part), bf16),
            jax.ShapeDtypeStruct((width, 3 * part), bf16),
            jax.ShapeDtypeStruct((width, 2 * part), bf16),
        ],
        compiler_params=pltpu.CompilerParams(vmem_limit_bytes=40 << 20),
        cost_estimate=pl.CostEstimate(flops=40 * width * rank * part, bytes_accessed=1 << 20, transcendentals=0),
    )(spot, *quads, vecs)


def flipped(block, mask):
    count = lax.axis_size("seq")
    return lax.ppermute(block, "seq", [(i, i ^ mask) for i in range(count)])


def far_piece(piece):
    count = lax.axis_size("seq")
    pairs = [(2 * i + b, 2 * (i ^ (8 + 4 * b)) + b) for i in range(count) for b in range(2)]
    return lax.ppermute(piece, ("seq", "blk"), pairs)


def spread_square(block):
    across = flipped(block, 2)
    return [block, flipped(block, 1), across, flipped(across, 1)]


def trained_kernel(
    spot, turned_ref, grad_ref, vecs, merged_hbm, down_hbm, lift_hbm, out_ref, moment, merged_ref, down_ref, lift_ref, sems,
    *, wide
):
    held = ((merged_hbm, merged_ref), (down_hbm, down_ref), (lift_hbm, lift_ref))
    lead = down_ref.shape[1]
    width = down_ref.shape[0] * lead
    rank = down_ref.shape[2]
    part = lift_ref.shape[2]
    pairs = part // wide
    picked = [grad_ref[:, (3 * n + s) * wide : (3 * n + s + 1) * wide] for s in (0, 2) for n in range(pairs)]
    added = dot_nn(turned_ref[...], jnp.concatenate(picked, axis=1))
    @pl.when(pl.program_id(0) == 0)
    def _():
        for n, (source, target) in enumerate(held):
            pltpu.make_async_copy(source, target, sems.at[n]).start()
        moment[...] = added
    @pl.when(pl.program_id(0) > 0)
    def _():
        moment[...] += added
    @pl.when(pl.program_id(0) == pl.num_programs(0) - 1)
    def _():
        for n, (source, target) in enumerate(held):
            pltpu.make_async_copy(source, target, sems.at[n]).wait()
        down = down_ref[...].reshape(width, rank).astype(f32)
        lift = lift_ref[...].reshape(rank, part)
        out_ref[...] = jnp.zeros_like(out_ref)
        base = 0
        for s, coef in ((0, 0.125 * LOG2E), (1, 1.0)):
            cols = slice(s * part, (s + 1) * part)
            shift = jnp.sum(merged_ref[:, cols].astype(f32) * moment[:, cols], axis=0, keepdims=True) * coef
            bend = bent(vecs, 2 + s, spot[0], part) * coef
            bent_moment = (moment[:, cols] * bend).astype(bf16)
            scale = jnp.sum(down * dot_nt(bent_moment, lift), axis=0, keepdims=True)
            for n in range(rank // wide):
                out_ref[base + n : base + n + 1, :] = scale[:, n * wide : (n + 1) * wide]
            base += rank // wide
            for n in range(pairs):
                out_ref[pl.ds(base + pairs * spot[0] + n, 1), :] = shift[:, n * wide : (n + 1) * wide]
            base += 2 * pairs


def trained(spot, turned, grads, merged, down, lift, vecs, wide):
    rank, part = down.shape[2], lift.shape[2]
    width, total = turned.shape
    step = total // 2
    whole = lambda array: pl.BlockSpec(array.shape, lambda i, s: (0,) * array.ndim)
    rows = 2 * (rank + 2 * part) // wide
    return pl.pallas_call(
        functools.partial(trained_kernel, wide=wide),
        grid_spec=pltpu.PrefetchScalarGridSpec(
            num_scalar_prefetch=1,
            grid=(2,),
            in_specs=[
                pl.BlockSpec((width, step), lambda i, s: (0, i)),
                pl.BlockSpec((step, grads.shape[1]), lambda i, s: (i, 0)),
            ]
            + [whole(vecs)] + [pl.BlockSpec(memory_space=pl.ANY)] * 3,
            out_specs=pl.BlockSpec((rows, wide), lambda i, s: (0, 0)),
            scratch_shapes=[pltpu.VMEM((width, 2 * part), f32)]
            + [pltpu.VMEM(array.shape, bf16) for array in (merged, down, lift)] + [pltpu.SemaphoreType.DMA((3,))],
        ),
        out_shape=jax.ShapeDtypeStruct((rows, wide), f32),
        compiler_params=pltpu.CompilerParams(vmem_limit_bytes=60 << 20),
        cost_estimate=pl.CostEstimate(flops=8 * width * total * part, bytes_accessed=12 << 20, transcendentals=0),
    )(spot, turned, grads, vecs, merged, down, lift)


def finish_kernel(turned_ref, w_ref, grad_ref, *refs):
    sent, out_ref = refs[:-1], refs[-1]
    held = grad_ref[...].astype(f32) + dot_nt(turned_ref[...], w_ref[...])
    for n, ref in enumerate(sent):
        @pl.when(pl.program_id(0) == n)
        def _():
            out_ref[...] = (held + ref[...].astype(f32)).astype(bf16)


def finish(grad_one, turned, weights, sent):
    count, span, width = grad_one.shape
    at_row = pl.BlockSpec((None, span, width), lambda i: (i, 0, 0))
    cols = turned.shape[2]
    return pl.pallas_call(
        finish_kernel,
        grid=(count,),
        in_specs=[
            pl.BlockSpec((None, span, cols), lambda i: (0, i, 0)),
            pl.BlockSpec((width, cols), lambda i: (0, 0)),
            at_row,
        ]
        + [pl.BlockSpec((span, width), lambda i: (0, 0))] * count,
        out_specs=at_row,
        out_shape=jax.ShapeDtypeStruct((count, span, width), bf16),
        compiler_params=pltpu.CompilerParams(vmem_limit_bytes=48 << 20),
    )(turned, weights, grad_one, *sent)


def centred(hidden):
    off = hidden - jnp.mean(hidden, axis=-1, keepdims=True)
    scale = lax.rsqrt(jnp.mean(off*off, axis=-1, keepdims=True) + 1e-05)
    return off*scale, scale

def norm_back(grad, unit, scale):
    inner = jnp.mean(grad*unit, axis=-1, keepdims=True)
    return scale*(grad - jnp.mean(grad, axis=-1, keepdims=True) - unit*inner)

def gelu_pair(x):
    size = jnp.abs(x)
    base = 1.0 + size*(0.3275911*0.7071067811865476)
    t = pl.reciprocal(base, approx=True)
    t = t*(2.0 - base*t)
    bell = jnp.exp2(x*x*(-0.7213475204444817))
    tail = t*(0.127414796 + t*(-0.142248368 + t*(0.7107068705 + t*(-0.7265760135 + t*0.5307027145))))*bell
    below = jnp.where(x < 0, tail, 1.0 - tail)
    return x*below, below + x*(bell*0.3989422804014327)

def ffn_kernel(spot, co_hbm, cr_hbm, x_hbm, cot_hbm, g1_ref, g2_ref, *refs, shards, cuts, row):
    pieces = refs[:shards]
    out_ref, grad_ref, own_ref, send_ref, co_ref, cr_ref, x_ref, cot_ref, wo, wi, wb, slopes, acts, sems = refs[-14:]
    width = x_ref.shape[1]
    lead = wo.shape[1]
    back = wb.shape[1]
    per = shards//cuts
    mine = spot[0]
    seat = spot[1]
    groups = [0, 4, 8 + 4*mine, 12 - 4*mine]
    ats = [seat ^ (groups[j//per] + j%per) for j in range(shards)]
    def bring(source, target, n):
        pltpu.make_async_copy(source, target, sems.at[n]).start()
    def arrived(held, n):
        pltpu.make_async_copy(held, held, sems.at[n]).wait()
    bring(co_hbm, co_ref, 1+2*cuts)
    bring(cr_hbm, cr_ref, 2+2*cuts)
    bring(x_hbm.at[row], x_ref, 3+2*cuts)
    for j in range(shards):
        bring(pieces[j].at[0:lead, :], wo.at[ats[j]], 0)
    for g in range(cuts):
        block = lax.shift_right_logical(seat ^ groups[g], 2)
        start = pl.multiple_of(lead*(1+block), 16)
        for j in range(shards):
            bring(pieces[j].at[pl.ds(start, lead), :], wi.at[g, ats[j]], 1+g)
        for j in range(g*per, (g+1)*per):
            bring(pieces[j].at[lead*(1+cuts):lead*(1+cuts)+back, :], wb.at[g*per + (ats[j] & (per-1))], 1+cuts+g)
    bring(cot_hbm.at[row], cot_ref, 4+2*cuts)
    part = shards//2
    half = width//2
    def out_rows(who):
        return wo[pl.ds(pl.multiple_of(who*part, part), part)].reshape(half, width)
    def w_in(j): return wi[j].reshape(width, width)
    def w_back(j): return wb[j*per:(j+1)*per].reshape(per*back, width)
    arrived(co_ref, 1+2*cuts)
    arrived(cr_ref, 2+2*cuts)
    arrived(x_ref, 3+2*cuts)
    arrived(wo, 0)
    resid = x_ref[...].astype(f32) + dot_nn(co_ref[...], out_rows(mine)) + dot_nn(cr_ref[...], out_rows(1-mine))
    unit_one, scale_one = centred(resid)
    gain_one = g1_ref[...].reshape(1, width)
    gain_two = g2_ref[...].reshape(1, width)
    normed = unit_one*gain_one
    low = normed.astype(bf16)
    total = normed
    for j in range(cuts):
        arrived(wi.at[j], 1+j)
        arrived(wb.at[j*per:(j+1)*per], 1+cuts+j)
    for j in range(cuts):
        for at in range(0, width, 256):
            for top in range(0, x_ref.shape[0], 256):
                act, slope = gelu_pair(dot_nn(low[top:top+256], wi[j, :, :, at:at+256].reshape(width, 256)))
                acts[top:top+256, at:at+256] = act.astype(bf16)
                slopes[j, top:top+256, at:at+256] = slope.astype(bf16)
        total = total + dot_nn(acts[...], w_back(j))
    unit_two, scale_two = centred(total)
    out_ref[...] = (unit_two*gain_two).astype(bf16)
    arrived(cot_ref, 4+2*cuts)
    grad_two = norm_back(cot_ref[...].astype(f32)*gain_two, unit_two, scale_two)
    low_two = grad_two.astype(bf16)
    grad = grad_two
    for j in range(cuts):
        pre_grad = (dot_nt(low_two, w_back(j))*slopes[j].astype(f32)).astype(bf16)
        grad = grad + dot_nt(pre_grad, w_in(j))
    grad_one = norm_back(grad*gain_one, unit_one, scale_one)
    low_one = grad_one.astype(bf16)
    grad_ref[...] = low_one
    send_ref[...] = dot_nt(low_one, out_rows(1-mine)).astype(bf16)
    own_ref[...] = dot_nt(low_one, out_rows(mine)).astype(bf16)

def ffn(row, spot, ctx_own, ctx_recv, x, cot, gain_one, gain_two, pieces, before, cuts):
    count, span, width = x.shape
    shards = len(pieces)
    lead = width//shards
    back = cuts*width//shards
    whole = lambda shape: pl.BlockSpec(shape, lambda i, s: (0,)*len(shape))
    at_row = pl.BlockSpec((None, span, width), lambda i, s: (row, 0, 0))
    anywhere = pl.BlockSpec(memory_space=pl.ANY)
    return pl.pallas_call(
        functools.partial(ffn_kernel, shards=shards, cuts=cuts, row=row),
        grid_spec=pltpu.PrefetchScalarGridSpec(
            num_scalar_prefetch=1, grid=(1,),
            in_specs=[anywhere]*4 + [whole((width,))]*2 + [anywhere]*(shards+len(before)),
            out_specs=[at_row, at_row, whole((span, width//2)), whole((span, width//2))],
            scratch_shapes=[
                pltpu.VMEM((span, width//2), bf16),
                pltpu.VMEM((span, width//2), bf16),
                pltpu.VMEM((span, width), bf16),
                pltpu.VMEM((span, width), bf16),
                pltpu.VMEM((shards, lead, width), bf16),
                pltpu.VMEM((cuts, shards, lead, width), bf16),
                pltpu.VMEM((shards, back, width), bf16),
                pltpu.VMEM((cuts, span, width), bf16),
                pltpu.VMEM((span, width), bf16),
                pltpu.SemaphoreType.DMA((5+2*cuts,)),
            ]),
        out_shape=[
            jax.ShapeDtypeStruct((count, span, width), bf16),
            jax.ShapeDtypeStruct((count, span, width), bf16),
            jax.ShapeDtypeStruct((span, width//2), bf16),
            jax.ShapeDtypeStruct((span, width//2), bf16),
        ],
        input_output_aliases={7+shards+n: n for n in range(len(before))},
        compiler_params=pltpu.CompilerParams(vmem_limit_bytes=56<<20),
        cost_estimate=pl.CostEstimate(flops=8*span*width*width*(2+4*cuts), bytes_accessed=2*(2+2*cuts)*width*width, transcendentals=2*span*width*cuts),
    )(spot, ctx_own, ctx_recv, x, cot, gain_one, gain_two, *pieces, *before)


def shifted(shard, axis, by):
    count = lax.axis_size(axis)
    return lax.ppermute(shard, axis, [(i, (i + by) % count) for i in range(count)])


def layer_norm(hidden, gain):
    centre = hidden - jnp.mean(hidden, axis=-1, keepdims=True)
    spread = jnp.mean(centre * centre, axis=-1, keepdims=True)
    return centre * lax.rsqrt(spread + 1e-05) * gain


def exact_gelu(values):
    return jax.nn.gelu(values, approximate=False)


def segment_ids(lengths, total):
    place = jnp.arange(total, dtype=jnp.int32)[None, :]
    bounds = jnp.cumsum(lengths, axis=1)
    counted = jnp.zeros((lengths.shape[0], total), jnp.int32)
    for column in range(lengths.shape[1]):
        counted = counted + (place >= bounds[:, column : column + 1]).astype(jnp.int32)
    return counted


def dot_plain(left, right):
    return jnp.dot(left, right, preferred_element_type=jnp.float32)


def dot_trans(left, right):
    return lax.dot_general(
        left, right, (((1,), (1,)), ((), ())), preferred_element_type=jnp.float32
    )


def block_grads(query_h, out_grad, lse_rows, delta_rows, key_h, value_h, allowed):
    scores = (
        jnp.einsum("rqhd,rkhd->rqhk", query_h, key_h, preferred_element_type=jnp.float32) * 0.125
    )
    probs = jnp.where(allowed, jnp.exp(scores - lse_rows[..., None]), 0.0)
    value_grad = jnp.einsum(
        "rqhk,rqhd->rkhd", probs.astype(jnp.bfloat16), out_grad, preferred_element_type=jnp.float32
    )
    prob_grad = jnp.einsum("rqhd,rkhd->rqhk", out_grad, value_h, preferred_element_type=jnp.float32)
    score_grad = (probs * (prob_grad - delta_rows[..., None])).astype(jnp.bfloat16)
    query_grad = (
        jnp.einsum("rqhk,rkhd->rqhd", score_grad, key_h, preferred_element_type=jnp.float32) * 0.125
    )
    key_grad = (
        jnp.einsum("rqhk,rqhd->rkhd", score_grad, query_h, preferred_element_type=jnp.float32)
        * 0.125
    )
    return (query_grad, key_grad, value_grad)


def body_any(
    tokens,
    sent_lengths,
    w_query,
    w_key,
    w_value,
    w_out,
    shared_a,
    shared_b,
    w_in,
    w_back,
    gain_one,
    gain_two,
    scale_dq,
    shift_bq,
    scale_dv,
    shift_bv,
    cotangent,
):
    row_count, span, width = tokens.shape
    head_count = HEADS
    head_size = HEAD_DIM
    blocks = lax.axis_size("blk")
    my_block = lax.axis_index("blk")
    token_count = row_count * span
    token_rows = tokens.reshape(token_count, width)
    seg_full = segment_ids(sent_lengths, span * blocks)
    seg_mine = lax.dynamic_slice_in_dim(seg_full, my_block * span, span, 1)
    w_queries, w_keys, w_values, proj_a, proj_b = (
        lax.all_gather(w_query, "seq", axis=0, tiled=True),
        lax.all_gather(w_key, "seq", axis=0, tiled=True),
        lax.all_gather(w_value, "seq", axis=0, tiled=True),
        lax.all_gather(shared_a, "seq", axis=0, tiled=True),
        lax.all_gather(shared_b, "seq", axis=0, tiled=True),
    )
    projected = dot_plain(token_rows, proj_a).astype(jnp.bfloat16)
    proj_float = projected.astype(jnp.float32)
    lift_q = (proj_float * scale_dq).astype(jnp.bfloat16)
    lift_v = (proj_float * scale_dv).astype(jnp.bfloat16)
    extra_q = dot_plain(lift_q, proj_b)
    extra_v = dot_plain(lift_v, proj_b)
    queries = (dot_plain(token_rows, w_queries) + shift_bq * extra_q).astype(jnp.bfloat16)
    key_rows = dot_plain(token_rows, w_keys).astype(jnp.bfloat16)
    value_rows = (dot_plain(token_rows, w_values) + shift_bv * extra_v).astype(jnp.bfloat16)
    shape4 = (row_count, span, head_count, head_size)
    query_h = queries.reshape(shape4)
    key_h = key_rows.reshape(shape4)
    value_h = value_rows.reshape(shape4)
    start_best = jnp.full((row_count, span, head_count), -1e30, jnp.float32)
    best = start_best
    key_piece = lax.all_gather(key_rows.reshape(row_count, span, width), "blk", axis=1, tiled=True)
    value_piece = lax.all_gather(
        value_rows.reshape(row_count, span, width), "blk", axis=1, tiled=True
    )
    length = key_piece.shape[1]
    key_part = key_piece.reshape(row_count, length, head_count, head_size)
    value_part = value_piece.reshape(row_count, length, head_count, head_size)
    seg_keys = seg_full
    allowed = (seg_mine[:, :, None] == seg_keys[:, None, :])[:, :, None, :]
    scores = (
        jnp.einsum("rqhd,rkhd->rqhk", query_h, key_part, preferred_element_type=jnp.float32) * 0.125
    )
    scores = jnp.where(allowed, scores, -1e30)
    new_best = jnp.maximum(best, jnp.max(scores, axis=-1))
    weight = jnp.where(allowed, jnp.exp(scores - new_best[..., None]), 0.0)
    total = jnp.sum(weight, axis=-1)
    accum = jnp.einsum(
        "rqhk,rkhd->rqhd",
        weight.astype(jnp.bfloat16),
        value_part,
        preferred_element_type=jnp.float32,
    )
    best, total, accum = (new_best, total, accum)
    log_total = best + jnp.log(total)
    context = accum / total[..., None]
    context_b = context.reshape(token_count, width).astype(jnp.bfloat16)
    w_outs, w_ins, w_backs = (
        lax.all_gather(w_out, "seq", axis=0, tiled=True),
        lax.all_gather(w_in, "seq", axis=0, tiled=True),
        lax.all_gather(w_back, "seq", axis=0, tiled=True),
    )

    def norm_first(hidden):
        return layer_norm(hidden, gain_one)

    def norm_second(hidden):
        return layer_norm(hidden, gain_two)

    resid_one = token_rows.astype(jnp.float32) + dot_plain(context_b, w_outs)
    normed_one, norm_one_pull = jax.vjp(norm_first, resid_one)
    pre_act = dot_plain(normed_one.astype(jnp.bfloat16), w_ins)
    act_float, gelu_pull = jax.vjp(exact_gelu, pre_act)
    ffn_part = dot_plain(act_float.astype(jnp.bfloat16), w_backs)
    normed_two, norm_two_pull = jax.vjp(norm_second, normed_one + ffn_part)
    layer_out = normed_two.astype(jnp.bfloat16).reshape(row_count, span, width)
    w_outs, w_ins, w_backs = (
        lax.all_gather(w_out, "seq", axis=0, tiled=True),
        lax.all_gather(w_in, "seq", axis=0, tiled=True),
        lax.all_gather(w_back, "seq", axis=0, tiled=True),
    )
    (grad_two,) = norm_two_pull(cotangent.reshape(token_count, width).astype(jnp.float32))
    act_grad = dot_trans(grad_two.astype(jnp.bfloat16), w_backs)
    (pre_grad,) = gelu_pull(act_grad)
    normed_grad = grad_two + dot_trans(pre_grad.astype(jnp.bfloat16), w_ins)
    (grad_one,) = norm_one_pull(normed_grad)
    context_grad = dot_trans(grad_one.astype(jnp.bfloat16), w_outs).astype(jnp.bfloat16)
    out_grad = context_grad.reshape(shape4)
    delta_rows = jnp.sum(out_grad.astype(jnp.float32) * context, axis=-1)
    zero_grads = jnp.zeros(shape4, jnp.float32)

    def key_step(step, carry):
        key_cur, value_cur, query_acc, key_acc, value_acc = carry
        source = (my_block - step) % blocks
        seg_keys = lax.dynamic_slice_in_dim(seg_full, source * span, span, 1)
        allowed = (seg_mine[:, :, None] == seg_keys[:, None, :])[:, :, None, :]
        q_part, k_part, v_part = block_grads(
            query_h, out_grad, log_total, delta_rows, key_cur, value_cur, allowed
        )
        key_acc, value_acc = (
            shifted((key_acc + k_part).astype(jnp.bfloat16), "blk", 1).astype(jnp.float32),
            shifted((value_acc + v_part).astype(jnp.bfloat16), "blk", 1).astype(jnp.float32),
        )
        key_cur, value_cur = shifted((key_cur, value_cur), "blk", 1)
        return (key_cur, value_cur, query_acc + q_part, key_acc, value_acc)

    looped = lax.fori_loop(
        0, blocks, key_step, (key_h, value_h, zero_grads, zero_grads, zero_grads)
    )
    query_acc, key_acc, value_acc = (looped[2], looped[3], looped[4])
    query_grad = query_acc.reshape(token_count, width).astype(jnp.bfloat16)
    key_grad = key_acc.reshape(token_count, width).astype(jnp.bfloat16)
    value_grad = value_acc.reshape(token_count, width).astype(jnp.bfloat16)
    w_queries, w_keys, w_values, proj_a, proj_b = (
        lax.all_gather(w_query, "seq", axis=0, tiled=True),
        lax.all_gather(w_key, "seq", axis=0, tiled=True),
        lax.all_gather(w_value, "seq", axis=0, tiled=True),
        lax.all_gather(shared_a, "seq", axis=0, tiled=True),
        lax.all_gather(shared_b, "seq", axis=0, tiled=True),
    )
    query_float = query_grad.astype(jnp.float32)
    value_float = value_grad.astype(jnp.float32)
    part_bq = jnp.sum(query_float * extra_q, axis=0)
    part_bv = jnp.sum(value_float * extra_v, axis=0)
    lift_q_grad = dot_trans((query_float * shift_bq).astype(jnp.bfloat16), proj_b)
    lift_v_grad = dot_trans((value_float * shift_bv).astype(jnp.bfloat16), proj_b)
    part_dq = jnp.sum(lift_q_grad * proj_float, axis=0)
    part_dv = jnp.sum(lift_v_grad * proj_float, axis=0)
    proj_grad = (lift_q_grad * scale_dq + lift_v_grad * scale_dv).astype(jnp.bfloat16)
    token_grad = (
        grad_one
        + dot_trans(query_grad, w_queries)
        + dot_trans(key_grad, w_keys)
        + dot_trans(value_grad, w_values)
        + dot_trans(proj_grad, proj_a)
    )
    grad_dq, grad_bq, grad_dv, grad_bv = lax.psum(
        (part_dq, part_bq, part_dv, part_bv), ("seq", "blk")
    )
    return (
        layer_out,
        token_grad.astype(jnp.bfloat16).reshape(row_count, span, width),
        grad_dq,
        grad_bq,
        grad_dv,
        grad_bv,
    )


def swapped(block):
    return lax.ppermute(block, "blk", [(0, 1), (1, 0)])


def body_two(
    tokens,
    sent_lengths,
    w_query,
    w_key,
    w_value,
    w_out,
    shared_a,
    shared_b,
    w_in,
    w_back,
    gain_one,
    gain_two,
    scale_dq,
    shift_bq,
    scale_dv,
    shift_bv,
    cotangent,
):
    row_count, span, width = tokens.shape
    shards = lax.axis_size("seq")
    heads = HEADS // 2
    part = heads * HEAD_DIM
    wide = 2 * HEAD_DIM
    lead, rank = shared_a.shape
    deep = shared_b.shape[0]
    cuts = w_in.shape[1] // width
    rows = range(row_count)
    spot = jnp.stack([lax.axis_index("blk"), lax.axis_index("seq")]).astype(jnp.int32)

    first, second, vecs = packed(
        spot, shared_a, w_query, w_key, w_value, shared_b, w_out, w_in, w_back,
        (scale_dq, scale_dv, shift_bq, shift_bv), part, wide,
    )
    tie = lax.optimization_barrier

    def core(block):
        return flipped(block, 1)

    other = swapped(tokens)
    lines = [flipped(first, 4), flipped(first, 8), flipped(first, 12)]
    second_over = flipped(second, 2)
    lines, second_over, second = tie((lines, second_over, second))
    quad = jnp.concatenate([first] + lines, axis=0)
    quad_over = flipped(quad, 2)
    quad_core = core(quad)
    far = far_piece(second)
    near = flipped(second, 4)
    both = jnp.concatenate([tokens, other], axis=0).reshape(2 * row_count * span, width)
    turned = both.T
    quad_over, quad_core, far, near, both, turned = tie((quad_over, quad_core, far, near, both, turned))
    down, lift, weights, merged = merge(
        spot, (quad, quad_core, quad_over, core(quad_over)), vecs, shards, lead, deep, rank, part, wide
    )
    qkv = dot_nn(both, weights).astype(bf16)
    near_core, far_core = core(near), core(far)
    qkv, second, second_over, far, near, near_core, far_core = tie(
        (qkv, second, second_over, far, near, near_core, far_core)
    )
    last = swapped(far)
    far_over = flipped(far, 2)
    near_over = flipped(second_over, 4)
    second_core, second_over_core = core(second), core(second_over)
    seen = [attend(0, spot, sent_lengths, qkv, heads, HEAD_DIM)]
    seen[0], last, far_over, near_over, second_core, second_over_core, qkv, near, far = tie(
        (seen[0], last, far_over, near_over, second_core, second_over_core, qkv, near, far)
    )
    ctx_recv = [swapped(seen[0][1])]
    last_over = flipped(last, 2)
    near_over_core, far_over_core, last_core = core(near_over), core(far_over), core(last)
    seen.append(attend(1, spot, sent_lengths, qkv, heads, HEAD_DIM))
    seen[1], ctx_recv[0], last_over, near_over_core, far_over_core, last_core = tie(
        (seen[1], ctx_recv[0], last_over, near_over_core, far_over_core, last_core)
    )
    ctx_recv.append(swapped(seen[1][1]))
    pack = [second, second_core, second_over, second_over_core, near, near_core, near_over, near_over_core]
    pack += [far, far_core, far_over, far_over_core, last, last_core, last_over, core(last_over)]
    fed = []
    for row in rows:
        before = fed[-1][:2] if fed else []
        fed.append(
            ffn(row, spot, seen[row][0], ctx_recv[row], tokens, cotangent, gain_one, gain_two, pack, before, cuts)
        )
    layer_out, grad_one = fed[-1][:2]
    grad_recv = [swapped(fed[row][3]) for row in rows]
    sent = []
    grads = []
    for row in rows:
        whole = attend_back(
            row, spot, sent_lengths, qkv, seen[row][0], seen[row][1],
            fed[row][2], grad_recv[row], seen[row][2], grads, heads, HEAD_DIM,
        )
        partial = dot_nt(whole[1, row * span : (row + 1) * span], weights).astype(bf16)
        if sent:
            whole, partial, sent[-1] = tie((whole, partial, sent[-1]))
        whole, partial = tie((whole, partial))
        grads = [whole]
        sent.append(swapped(partial))
    flat = trained(
        spot, turned, whole.reshape(2 * row_count * span, 3 * part), merged, down, lift, vecs, wide
    )
    flat = flat + core(flat)
    flat = flat + flipped(flat, 2)
    level, far_levels = flipped(flat, 4), flipped(flat, 8) + flipped(flat, 12)
    level, sent[-1] = tie((level, sent[-1]))
    flat = (flat + level) + far_levels
    flat = (flat + swapped(flat)).reshape(-1)
    token_grad = finish(grad_one, whole, weights, sent)
    return (
        layer_out,
        token_grad,
        flat[:rank],
        flat[rank : rank + width],
        flat[rank + width : 2 * rank + width],
        flat[2 * rank + width :],
    )


def solution(mesh):
    return jax.shard_map(
        body_two if mesh.shape["blk"] == 2 and mesh.shape["seq"] == 16 else body_any,
        mesh=mesh,
        in_specs=(
            P("seq", "blk", None),
            P("seq", None),
            P("seq", None),
            P("seq", None),
            P("seq", None),
            P("seq", None),
            P("seq", None),
            P("seq", None),
            P("seq", None),
            P("seq", None),
            P(),
            P(),
            P(),
            P(),
            P(),
            P(),
            P("seq", "blk", None),
        ),
        out_specs=(P("seq", "blk", None), P("seq", "blk", None), P(), P(), P(), P()),
        check_vma=False,
    )
```
